256 devices in a mesh: row: 16 (over z, core), col: 16 (over x, y).
Axes of the slice: x: 4, y: 4, z: 8, core: 2. Of those that a mesh axis runs over, the one named last changes fastest.
Arguments:
- right_aquifer: float32 [4, 12, 256, 4096], P(None, None, 'row', 'col'), may hold values from -24 to 24
- right_district: float32 [4, 3072], replicated, may hold values from -24 to 24
- head_scale: float32 [12, 256, 4096], P(None, 'row', 'col'), may hold values from 0.02 to 2
- crop_scale: float32 [6, 256, 4096], P(None, 'row', 'col'), may hold values from 0.02 to 2
- conductance: float32 [2, 256, 4096], P(None, 'row', 'col'), may hold values from 0.1 to 1
- water_use: float32 [12, 6], replicated, may hold values from 0.2 to 1
- climate: float32 [256, 4096], P('row', 'col'), may hold values from 0.5 to 2
- district_use: float32 [6], replicated, may hold values from 0.5 to 1.5
- district_id: int32 [256, 4096], P('row', 'col'), may hold values from 0 to 3071, as said below
- active: int32 [256, 4096], P('row', 'col'), may hold values 0 or 1
Outputs:
- dual_aquifer: float32 [4, 12, 256, 4096], P(None, None, 'row', 'col')
- dual_district: float32 [4, 3072], replicated
- residual_aquifer: float32 [4, 12, 256, 4096], P(None, None, 'row', 'col')
- residual_district: float32 [4, 3072], replicated
The draws below stay inside these ranges and needn't reach their ends.
Inputs may be any that keep to these rules, and one draw needn't show every extreme that they name: `district_id`: each district's cells form one axis-aligned rectangle of the grid, the districts together cover the grid, and every district has at least one cell.
All inputs are finite; a program needn't handle non-finite values. No bound on the sum of `active` on one device may be relied on, other than what follows from the above.
Results may differ from the reference program's by a relative error of at most 0.0003.
Values sent between devices are 32-bit elements; how exact they have to be, the bound alone decides.
A program may use at most 64 MiB of HBM per device.

```python
import math
import jax
import jax.numpy as jnp
from jax import lax

MONTHS = 12
CROPS = 6
RHS = 4
ITERS = 4
DHI = 128
DLO = 24
DISTRICTS = 3072
NR = 256
NC = 4096


def band_of(key, total, count):
    broad_span = total // 4
    key_opening, key_ranking = jax.random.split(key)
    opening = jax.random.randint(key_opening, (), 0, total - broad_span)
    position = jnp.arange(total, dtype=jnp.int32)
    blocked = (position == 0) | (position > opening) & (position <= opening + broad_span)
    ranking = jax.random.permutation(key_ranking, total).astype(jnp.int32)
    scores = jnp.where(blocked, total + position, ranking)
    chosen = jnp.argsort(scores, stable=True)[:count - 1]
    cut_marks = jnp.zeros((total,), jnp.int32).at[chosen].set(1)
    return jnp.cumsum(cut_marks).astype(jnp.int32)


def column_bands(sub_key):
    return band_of(sub_key, NC, DHI)


def draw_district_id(key, part):
    key = jax.random.fold_in(key, 11)
    key_rows, key_cols, key_names = jax.random.split(key, 3)
    row_band = band_of(key_rows, NR, DLO)
    col_table = jax.vmap(column_bands)(jax.random.split(key_cols, DLO))
    col_band = col_table[row_band]
    shuffled = jax.random.permutation(key_names, DISTRICTS).astype(jnp.int32)
    return shuffled[row_band[:, None] * DHI + col_band].astype(jnp.int32)


def plant(entries, own_key, least, top_value):
    extent = entries.shape
    index_at = [jax.random.randint(jax.random.fold_in(own_key, axis), (), 0, extent[axis]) for axis in range(len(extent))]
    entries = entries.at[tuple(index_at)].set(least)
    longest = extent.index(max(extent))
    index_at[longest] = (index_at[longest] + 1) % extent[longest]
    return entries.at[tuple(index_at)].set(top_value)


def block_scale(rng, extent, shards, smallest, high):
    loudness, own = 1.0, jax.random.fold_in(rng, 6)
    for dim, parts in shards:
        heights = jnp.exp(jax.random.uniform(jax.random.fold_in(own, dim), (parts,), jnp.float32, smallest / len(shards), high / len(shards)))
        loudness = loudness * jnp.repeat(heights, extent[dim] // parts).reshape([-1 if axis == dim else 1 for axis in range(len(extent))])
    return loudness


def gaussian(stream_key, dims, width, limit, cuts=(), kind=jnp.bfloat16):
    array = width * jax.random.normal(stream_key, dims, jnp.float32)
    if cuts:
        array = array * block_scale(stream_key, dims, cuts, -0.22, 0.18)
    return jnp.clip(array, -limit, limit).astype(kind)


def setup_inputs(seed: int = 0) -> dict:
    streams_of = jax.random.split(jax.random.key(seed), 11)
    right_aquifer = gaussian(streams_of[0], (RHS, MONTHS, NR, NC), 4.0, 24.0, ((2, 16), (3, 16)), jnp.float32)
    right_district = gaussian(streams_of[1], (RHS, DISTRICTS), 4.0, 24.0, (), jnp.float32)
    head_scale = jnp.clip(jnp.exp(math.log(2.0) - 4.6051702 * jax.random.uniform(streams_of[2], (MONTHS, NR, NC), jnp.float32) ** block_scale(streams_of[2], (MONTHS, NR, NC), ((1, 16), (2, 16)), -0.2, 0.2)), 0.02, 2.0)
    crop_scale = jnp.clip(jnp.exp(math.log(2.0) - 4.6051702 * jax.random.uniform(streams_of[3], (CROPS, NR, NC), jnp.float32) ** block_scale(streams_of[3], (CROPS, NR, NC), ((1, 16), (2, 16)), -0.2, 0.2)), 0.02, 2.0)
    conductance = jnp.clip(jnp.exp(math.log(1.0) - 2.3025851 * jax.random.uniform(streams_of[4], (2, NR, NC), jnp.float32) ** block_scale(streams_of[4], (2, NR, NC), ((1, 16), (2, 16)), -0.2, 0.2)), 0.1, 1.0)
    water_use = jnp.clip(jax.random.uniform(streams_of[5], (MONTHS, CROPS), jnp.float32, 0.2, 1.0), 0.2, 1.0)
    climate = jnp.clip(jnp.exp(math.log(2.0) - 1.3862944 * jax.random.uniform(streams_of[6], (NR, NC), jnp.float32) ** block_scale(streams_of[6], (NR, NC), ((0, 16), (1, 16)), -0.2, 0.2)), 0.5, 2.0)
    district_use = jnp.clip(jax.random.uniform(streams_of[7], (CROPS,), jnp.float32, 0.5, 1.5), 0.5, 1.5)
    district_id = draw_district_id(jax.random.fold_in(streams_of[10], 71), 0)
    active = plant((jax.random.randint(streams_of[9], (NR, NC), 0, 4) < 3).astype(jnp.int32), jax.random.fold_in(streams_of[9], 1), 0, 1)
    return {"right_aquifer": right_aquifer, "right_district": right_district, "head_scale": head_scale, "crop_scale": crop_scale, "conductance": conductance, "water_use": water_use, "climate": climate, "district_use": district_use, "district_id": district_id, "active": active}


PROXIMAL = 0.05
EXACT = lax.Precision.HIGHEST


def laplace(grid_values, east_faces, south_faces):
    middle = grid_values[..., 1:-1, 1:-1]
    return (east_faces[1:-1, 1:-1] * (middle - grid_values[..., 1:-1, 2:])
            + east_faces[1:-1, :-2] * (middle - grid_values[..., 1:-1, :-2])
            + south_faces[1:-1, 1:-1] * (middle - grid_values[..., 2:, 1:-1])
            + south_faces[:-2, 1:-1] * (middle - grid_values[..., :-2, 1:-1]))


def pad_grid(grid_values):
    widths = [(0, 0)] * (grid_values.ndim - 2) + [(1, 1), (1, 1)]
    return jnp.pad(grid_values, widths)


def reference(right_aquifer, right_district, head_scale, crop_scale, conductance, water_use, climate, district_use, district_id, active):
    rows_total, cols_total = climate.shape
    scale = (DISTRICTS / (rows_total * cols_total)) ** 0.5
    live = active.astype(jnp.float32)
    weight = live * climate
    coeff = scale * district_use[:, None, None] * live[None]
    east_faces = pad_grid(conductance[0])
    south_faces = pad_grid(conductance[1])
    head_pad = pad_grid(head_scale)
    flat_ids = district_id.reshape(-1)
    east_here = east_faces[1:-1, 1:-1]
    east_west = east_faces[1:-1, :-2]
    south_here = south_faces[1:-1, 1:-1]
    south_north = south_faces[:-2, 1:-1]
    lap_sum = east_here + east_west + south_here + south_north
    diag_aquifer = (head_scale * lap_sum * lap_sum
                    + east_here * east_here * head_pad[:, 1:-1, 2:]
                    + east_west * east_west * head_pad[:, 1:-1, :-2]
                    + south_here * south_here * head_pad[:, 2:, 1:-1]
                    + south_north * south_north * head_pad[:, :-2, 1:-1]
                    + weight * weight * jnp.einsum("mc,cij->mij", water_use * water_use, crop_scale, precision=EXACT)
                    + PROXIMAL)
    diag_district = jax.ops.segment_sum(jnp.sum(coeff * coeff * crop_scale, axis=0).reshape(-1), flat_ids, num_segments=DISTRICTS) + PROXIMAL

    def apply(direc_aq, direc_di):
        grad_head = laplace(pad_grid(direc_aq), east_faces, south_faces)
        grad_crop = weight * jnp.einsum("mc,mij->cij", water_use, direc_aq, precision=EXACT) + coeff * direc_di[district_id][None]
        scaled_crop = crop_scale * grad_crop
        image_aq = (laplace(pad_grid(head_scale * grad_head), east_faces, south_faces)
                    + weight * jnp.einsum("mc,cij->mij", water_use, scaled_crop, precision=EXACT)
                    + PROXIMAL * direc_aq)
        cell_sum = jnp.sum(coeff * scaled_crop, axis=0).reshape(-1)
        image_di = jax.ops.segment_sum(cell_sum, flat_ids, num_segments=DISTRICTS) + PROXIMAL * direc_di
        return image_aq, image_di

    def solve(pair):
        right_aq, right_di = pair
        dual_aq = jnp.zeros_like(right_aq)
        dual_di = jnp.zeros_like(right_di)
        res_aq, res_di = right_aq, right_di
        pre_aq = res_aq / diag_aquifer
        pre_di = res_di / diag_district
        dir_aq, dir_di = pre_aq, pre_di
        rho = jnp.sum(res_aq * pre_aq) + jnp.sum(res_di * pre_di)
        for repeat in range(ITERS):
            image_aq, image_di = apply(dir_aq, dir_di)
            curvature = jnp.sum(dir_aq * image_aq) + jnp.sum(dir_di * image_di)
            alpha = rho / curvature
            dual_aq = dual_aq + alpha * dir_aq
            dual_di = dual_di + alpha * dir_di
            res_aq = res_aq - alpha * image_aq
            res_di = res_di - alpha * image_di
            if repeat + 1 < ITERS:
                pre_aq = res_aq / diag_aquifer
                pre_di = res_di / diag_district
                rho_new = jnp.sum(res_aq * pre_aq) + jnp.sum(res_di * pre_di)
                dir_aq = pre_aq + (rho_new / rho) * dir_aq
                dir_di = pre_di + (rho_new / rho) * dir_di
                rho = rho_new
        image_aq, image_di = apply(dual_aq, dual_di)
        return (dual_aq, dual_di, right_aq - image_aq, right_di - image_di)

    dual_aquifer, dual_district, residual_aquifer, residual_district = lax.map(solve, (right_aquifer, right_district))
    return (dual_aquifer, dual_district, residual_aquifer, residual_district)
```

```python
import functools

import jax
import jax.numpy as jnp
from jax import lax
from jax.experimental import pallas as pl
from jax.experimental.pallas import tpu as pltpu
from jax.sharding import PartitionSpec as P

ITERS = 4
DHI = 24
DLO = 128
PROXIMAL = 0.05
SHIFTS = (0.5, 8.0, 3.0, 1.0)
EXACT = lax.Precision.HIGHEST
MESH = pl.DeviceIdType.MESH


def reduce_kernel(x_ref, out_ref, near, zsum, send_sem, recv_sem):
    rows, cols = lax.axis_size("row"), lax.axis_size("col")
    chips, group = rows // 2, 2 * cols
    row, col = lax.axis_index("row"), lax.axis_index("col")
    chip, core = row // 2, lax.rem(row, 2)
    mine = core * cols + col

    def peer(k):
        other = lax.rem(mine + k, group)
        return other, (chip * 2 + other // cols, lax.rem(other, cols))

    def stack(k):
        return (lax.rem(row + 2 * k, rows), col)

    barrier = pltpu.get_barrier_semaphore()

    def greet(k, carry):
        pl.semaphore_signal(barrier, inc=1, device_id=peer(k)[1], device_id_type=MESH)
        return carry

    def greet_stack(k, carry):
        pl.semaphore_signal(barrier, inc=1, device_id=stack(k), device_id_type=MESH)
        return carry

    lax.fori_loop(1, group, greet, 0)
    lax.fori_loop(1, chips, greet_stack, 0)
    pl.semaphore_wait(barrier, group + chips - 2)

    def scatter(k, carry):
        other, device = peer(k)
        pltpu.make_async_remote_copy(
            src_ref=x_ref.at[pl.ds(pl.multiple_of(other * 8, 8), 8)],
            dst_ref=near.at[k],
            send_sem=send_sem.at[0],
            recv_sem=recv_sem.at[0],
            device_id=device,
            device_id_type=MESH,
        ).start()
        return carry

    lax.fori_loop(1, group, scatter, 0)
    near[0] = x_ref[pl.ds(pl.multiple_of(mine * 8, 8), 8)]
    pltpu.make_async_copy(near.at[pl.ds(1, group - 1)], near.at[pl.ds(1, group - 1)], recv_sem.at[0]).wait()
    zsum[chip] = jnp.sum(near[...], axis=0)

    def spread(k, carry):
        pltpu.make_async_remote_copy(
            src_ref=zsum.at[chip],
            dst_ref=zsum.at[chip],
            send_sem=send_sem.at[1],
            recv_sem=recv_sem.at[1],
            device_id=stack(k),
            device_id_type=MESH,
        ).start()
        return carry

    lax.fori_loop(1, chips, spread, 0)
    pltpu.make_async_copy(zsum.at[pl.ds(1, chips - 1)], zsum.at[pl.ds(1, chips - 1)], recv_sem.at[1]).wait()
    here = pl.ds(pl.multiple_of(mine * 8, 8), 8)
    out_ref[here] = jnp.sum(zsum[...], axis=0)

    def gather(k, carry):
        other, device = peer(k)
        pltpu.make_async_remote_copy(
            src_ref=out_ref.at[here],
            dst_ref=out_ref.at[here],
            send_sem=send_sem.at[2],
            recv_sem=recv_sem.at[2],
            device_id=device,
            device_id_type=MESH,
        ).start()
        return carry

    lax.fori_loop(1, group, gather, 0)
    pltpu.make_async_copy(near.at[pl.ds(1, group - 1)], near.at[pl.ds(1, group - 1)], recv_sem.at[2]).wait()
    pltpu.make_async_copy(near.at[pl.ds(1, group - 1)], near.at[pl.ds(1, group - 1)], send_sem.at[0]).wait()
    pltpu.make_async_copy(zsum.at[pl.ds(1, chips - 1)], zsum.at[pl.ds(1, chips - 1)], send_sem.at[1]).wait()
    pltpu.make_async_copy(near.at[pl.ds(1, group - 1)], near.at[pl.ds(1, group - 1)], send_sem.at[2]).wait()


def all_sum(values):
    group = 2 * lax.axis_size("col")
    chips = lax.axis_size("row") // 2
    return pl.pallas_call(
        reduce_kernel,
        out_shape=jax.ShapeDtypeStruct(values.shape, jnp.float32),
        in_specs=[pl.BlockSpec(memory_space=pltpu.VMEM)],
        out_specs=pl.BlockSpec(memory_space=pltpu.VMEM),
        scratch_shapes=[
            pltpu.VMEM((group, 8, 128), jnp.float32),
            pltpu.VMEM((chips, 8, 128), jnp.float32),
            pltpu.SemaphoreType.DMA((3,)),
            pltpu.SemaphoreType.DMA((3,)),
        ],
        compiler_params=pltpu.CompilerParams(collective_id=0, has_side_effects=True),
    )(values)


def extended(value, sides, width):
    for axis, dim in sides:
        peers, length = (lax.axis_size(axis), value.shape[dim])
        up = [(i, (i + 1) % peers) for i in range(peers - 1)]
        down = [(j, i) for i, j in up]
        last = lax.slice_in_dim(value, length - width, length, axis=dim)
        first = lax.slice_in_dim(value, 0, width, axis=dim)
        before = lax.ppermute(last, axis, up)
        after = lax.ppermute(first, axis, down)
        value = jnp.concatenate([before, value, after], axis=dim)
    return value


def laplace(grid_values, east_faces, south_faces):
    middle = grid_values[..., 1:-1, 1:-1]
    return (
        east_faces[1:-1, 1:-1] * (middle - grid_values[..., 1:-1, 2:])
        + east_faces[1:-1, :-2] * (middle - grid_values[..., 1:-1, :-2])
        + south_faces[1:-1, 1:-1] * (middle - grid_values[..., 2:, 1:-1])
        + south_faces[:-2, 1:-1] * (middle - grid_values[..., :-2, 1:-1])
    )


def small_cg(gram):
    one, zero = jnp.ones_like(gram[0][0]), jnp.zeros_like(gram[0][0])
    x, r, d = [zero] * ITERS, [one] + [zero] * ITERS, [one] + [zero] * (ITERS - 1)
    rho = gram[0][0]
    for it in range(ITERS):
        image = [zero] * (ITERS + 1)
        for k in range(it + 1):
            image[k + 1] = image[k + 1] + d[k]
            image[k] = image[k] + SHIFTS[k] * d[k]
        curve = sum(d[i] * image[j] * gram[i][j] for i in range(it + 1) for j in range(it + 2))
        alpha = rho / curve
        x = [x[i] + alpha * d[i] for i in range(ITERS)]
        r = [r[i] - alpha * image[i] for i in range(ITERS + 1)]
        if it + 1 < ITERS:
            rho_new = sum(r[i] * r[j] * gram[i][j] for i in range(it + 2) for j in range(it + 2))
            ratio = rho_new / rho
            rho = rho_new
            d = [r[i] + ratio * d[i] for i in range(ITERS)]
    return x, r


def body(
    right_aquifer,
    right_district,
    head_scale,
    crop_scale,
    conductance,
    water_use,
    climate,
    district_use,
    district_id,
    active,
):
    rhs, months, tile_rows, tile_cols = right_aquifer.shape
    districts = right_district.shape[1]
    cell_count = tile_rows * tile_cols
    grid_cells = tile_rows * lax.axis_size("row") * tile_cols * lax.axis_size("col")
    scale = (districts / grid_cells) ** 0.5
    live = active.astype(jnp.float32)
    weight = live * climate
    coeff = scale * district_use[:, None, None] * live[None]
    flat_ids = district_id.reshape(cell_count)
    hot_high = (lax.iota(jnp.int32, DHI)[:, None] == (flat_ids // DLO)[None, :]).astype(jnp.float32)
    hot_low = (lax.iota(jnp.int32, DLO)[:, None] == (flat_ids % DLO)[None, :]).astype(jnp.float32)

    def to_district(values):
        values = values.reshape(-1, 1, cell_count)
        summed = jnp.einsum("ln,bhn->bhl", hot_low, values * hot_high[None], precision=EXACT)
        return summed.reshape(-1, DLO)

    def from_district(table_values):
        blocks = table_values.reshape(-1, DHI, DLO)
        picked = jnp.einsum("bhl,ln->bhn", blocks, hot_low, precision=EXACT)
        return jnp.sum(picked * hot_high[None], axis=1).reshape(-1, 1, tile_rows, tile_cols)

    def all_rows(parts):
        used = sum(p.shape[0] for p in parts)
        pad = jnp.zeros((16 * lax.axis_size("col") - used, DLO), jnp.float32)
        return all_sum(jnp.concatenate(list(parts) + [pad]))

    stacked = jnp.concatenate([conductance, head_scale], axis=0)
    near_stack = extended(stacked, (("row", 1), ("col", 2)), 1)
    east_near = near_stack[0]
    south_near = near_stack[1]
    head_near = near_stack[2:]
    east_here = east_near[1:-1, 1:-1]
    east_west = east_near[1:-1, :-2]
    south_here = south_near[1:-1, 1:-1]
    south_north = south_near[:-2, 1:-1]
    lap_sum = east_here + east_west + south_here + south_north
    diag_aq = (
        head_scale * lap_sum * lap_sum
        + east_here * east_here * head_near[:, 1:-1, 2:]
        + east_west * east_west * head_near[:, 1:-1, :-2]
        + south_here * south_here * head_near[:, 2:, 1:-1]
        + south_north * south_north * head_near[:, :-2, 1:-1]
        + weight
        * weight
        * jnp.einsum("mc,cij->mij", water_use * water_use, crop_scale, precision=EXACT)
        + PROXIMAL
    )
    cross = weight * jnp.einsum("mc,cij->mij", water_use, crop_scale * coeff, precision=EXACT)
    cross_d = cross / diag_aq

    def smooth(p):
        padded = extended(p, (("row", 2), ("col", 3)), 1)
        scaled_head = head_scale * laplace(padded, east_near, south_near)
        padded_scaled = extended(scaled_head, (("row", 2), ("col", 3)), 1)
        head_term = laplace(padded_scaled, east_near, south_near)
        scaled_crop = crop_scale * weight * jnp.einsum("mc,rmij->rcij", water_use, p, precision=EXACT)
        image = (
            head_term
            + weight * jnp.einsum("mc,rcij->rmij", water_use, scaled_crop, precision=EXACT)
            + PROXIMAL * p
        )
        return image / diag_aq

    def gather_cells(p):
        return jnp.sum(cross * p, axis=1)

    p0 = right_aquifer / diag_aq
    b0 = smooth(p0)
    diag_local = jnp.sum(coeff * coeff * crop_scale, axis=0)[None]
    wide_local = jnp.sum(cross * cross_d, axis=0)[None]
    sums = all_rows(
        [to_district(jnp.concatenate([diag_local, wide_local, gather_cells(p0), gather_cells(b0)]))]
    )[: DHI * (2 + 2 * rhs)].reshape(2 + 2 * rhs, districts)
    diag_di = sums[0] + PROXIMAL
    wide = sums[1]
    z0, y0 = sums[2 : 2 + rhs], sums[2 + rhs :]
    t0 = right_district / diag_di
    t1 = z0 / diag_di + (1 - SHIFTS[0]) * t0
    z1 = y0 + wide * t0 - SHIFTS[0] * z0
    t2 = z1 / diag_di + (1 - SHIFTS[1]) * t1
    looks = from_district(jnp.concatenate([t0, t1, t2]))
    p1 = b0 + cross_d * looks[:rhs] - SHIFTS[0] * p0
    p2 = smooth(p1) + cross_d * looks[rhs : 2 * rhs] - SHIFTS[1] * p1
    p3 = smooth(p2) + cross_d * looks[2 * rhs :] - SHIFTS[2] * p2
    b3 = smooth(p3)
    basis = [p0, p1, p2, p3]
    pairs = [(i, j) for i in range(ITERS) for j in range(i, ITERS)]
    products = [jnp.sum(diag_aq * basis[i] * basis[j], axis=(1, 2, 3)) for i, j in pairs]
    products.append(jnp.sum(diag_aq * p3 * b3, axis=(1, 2, 3)))
    scalars = jnp.pad(jnp.stack(products), ((0, 0), (0, DLO - rhs)))
    sums = all_rows([to_district(jnp.concatenate([gather_cells(p2), gather_cells(p3)])), scalars])
    z2 = sums[: rhs * DHI].reshape(rhs, districts)
    z3 = sums[rhs * DHI : 2 * rhs * DHI].reshape(rhs, districts)
    scalars = sums[2 * rhs * DHI : 2 * rhs * DHI + len(products), :rhs]
    t3 = z2 / diag_di + (1 - SHIFTS[2]) * t2
    t4 = z3 / diag_di + (1 - SHIFTS[3]) * t3
    tables = [t0, t1, t2, t3]
    gram = [[None] * (ITERS + 1) for _ in range(ITERS + 1)]
    for n, (i, j) in enumerate(pairs):
        gram[i][j] = gram[j][i] = scalars[n] + jnp.sum(diag_di * tables[i] * tables[j], axis=1)
    top = scalars[len(pairs)] + jnp.sum(t3 * (2 * z3 + diag_di * t3), axis=1)
    for i in range(ITERS):
        ahead = top if i == ITERS - 1 else gram[i + 1][ITERS - 1] + SHIFTS[i] * gram[i][ITERS - 1]
        gram[i][ITERS] = ahead - SHIFTS[ITERS - 1] * gram[i][ITERS - 1]
    x, r = small_cg(gram)
    p4 = b3 + cross_d * from_district(t3) - SHIFTS[3] * p3
    basis.append(p4)
    tables.append(t4)
    dual_aq = sum(x[i][:, None, None, None] * basis[i] for i in range(ITERS))
    dual_di = sum(x[i][:, None] * tables[i] for i in range(ITERS))
    res_aq = diag_aq * sum(r[i][:, None, None, None] * basis[i] for i in range(ITERS + 1))
    res_di = diag_di * sum(r[i][:, None] * tables[i] for i in range(ITERS + 1))
    return dual_aq, dual_di, res_aq, res_di


def solution(mesh):
    placed = (
        P(None, None, "row", "col"),
        P(),
        P(None, "row", "col"),
        P(None, "row", "col"),
        P(None, "row", "col"),
        P(),
        P("row", "col"),
        P(),
        P("row", "col"),
        P("row", "col"),
    )
    return jax.shard_map(
        body,
        mesh=mesh,
        in_specs=placed,
        out_specs=(P(None, None, "row", "col"), P(), P(None, None, "row", "col"), P()),
        check_vma=False,
    )
```

```python
import functools

import jax
import jax.numpy as jnp
from jax import lax
from jax.experimental import pallas as pl
from jax.experimental.pallas import tpu as pltpu
from jax.sharding import PartitionSpec as P

ITERS = 4
RHS = 4
MONTHS = 12
CROPS = 6
FIELDS = RHS * MONTHS
DHI = 8
DLO = 384
LANES = 128
TILE_ROWS = 16
CHUNKS = 32
PROXIMAL = 0.05
SHIFTS = (0.5, 8.0, 3.0, 1.0)
PAIRS = tuple((i, j) for i in range(ITERS) for j in range(i, ITERS))
MESH = pl.DeviceIdType.MESH
F32 = jnp.float32
CORE = pl.ds(8, 16)


def lanes_of(shape):
    return lax.broadcasted_iota(jnp.int32, shape, len(shape) - 1)


def rows_of(shape):
    return lax.broadcasted_iota(jnp.int32, shape, len(shape) - 2)


def beside(tiles):
    axis = tiles[0].ndim - 1
    lane = lanes_of(tiles[0].shape)
    ahead = [pltpu.roll(t, LANES - 1, axis) for t in tiles]
    behind = [pltpu.roll(t, 1, axis) for t in tiles]
    east = [jnp.where(lane == LANES - 1, ahead[(n + 1) % 3], ahead[n]) for n in range(3)]
    west = [jnp.where(lane == 0, behind[(n + 2) % 3], behind[n]) for n in range(3)]
    return east, west


def kernel(
    grid_cells,
    rhs_ref,
    rdi_ref,
    head_ref,
    crop_ref,
    cond_ref,
    climate_ref,
    id_ref,
    active_ref,
    wu_ref,
    use_ref,
    dual_ref,
    dual_di_ref,
    res_ref,
    res_di_ref,
    basis,
    image,
    stat,
    coef,
    headw,
    coefc,
    diag,
    dinv,
    cross,
    crossd,
    wcs,
    inner,
    grads,
    hot,
    lo_id,
    hi_id,
    cells,
    looks,
    segacc,
    table,
    diag_di,
    wide,
    bdi,
    sum_in,
    sum_near,
    sum_z,
    sum_out,
    late_near,
    late_z,
    late_in,
    factors,
    row_out,
    row_in,
    col_out,
    col_in,
    xch_send,
    xch_recv,
    sum_send,
    sum_recv,
):
    rows, cols = lax.axis_size("row"), lax.axis_size("col")
    chips, group = rows // 2, 2 * cols
    per = CHUNKS // group
    row, col = lax.axis_index("row"), lax.axis_index("col")
    chip, core = row // 2, lax.rem(row, 2)
    mine = core * cols + col
    districts = DHI * DLO

    def peer(k):
        other = lax.rem(mine + k, group)
        return other, (chip * 2 + other // cols, lax.rem(other, cols))

    def stack(k):
        return (lax.rem(row + 2 * k, rows), col)

    def around(dr, dc):
        return (lax.rem(row + dr + rows, rows), lax.rem(col + dc + cols, cols))

    barrier = pltpu.get_barrier_semaphore()

    def greet(k, carry):
        pl.semaphore_signal(barrier, inc=1, device_id=peer(k)[1], device_id_type=MESH)
        return carry

    def greet_stack(k, carry):
        pl.semaphore_signal(barrier, inc=1, device_id=stack(k), device_id_type=MESH)
        return carry

    lax.fori_loop(1, group, greet, 0)
    lax.fori_loop(1, chips, greet_stack, 0)
    offsets = [(dr, dc) for dr in (-1, 0, 1) for dc in (-1, 0, 1) if dr or dc]
    for dr, dc in offsets:
        pl.semaphore_signal(barrier, inc=1, device_id=around(dr, dc), device_id_type=MESH)

    north = jnp.where(row > 0, 1.0, 0.0).astype(F32)
    south = jnp.where(row < rows - 1, 1.0, 0.0).astype(F32)
    west = jnp.where(col > 0, 1.0, 0.0).astype(F32)
    east = jnp.where(col < cols - 1, 1.0, 0.0).astype(F32)

    def halo_copies(n, quads, groups):
        ahead, back = pl.ds(8, 8), pl.ds(0, 8)
        plan = [
            (row_out.at[n, 0, pl.ds(0, quads)], row_in.at[n, 0, pl.ds(0, quads)], (1, 0)),
            (row_out.at[n, 1, pl.ds(0, quads)], row_in.at[n, 1, pl.ds(0, quads)], (-1, 0)),
            (col_out.at[n, pl.ds(0, groups)], col_in.at[n, 0, pl.ds(0, groups), CORE], (0, 1)),
            (col_out.at[n, pl.ds(0, groups)], col_in.at[n, 1, pl.ds(0, groups), CORE], (0, -1)),
            (col_out.at[n, pl.ds(0, groups), ahead], col_in.at[n, 0, pl.ds(0, groups), pl.ds(0, 8)], (1, 1)),
            (col_out.at[n, pl.ds(0, groups), ahead], col_in.at[n, 1, pl.ds(0, groups), pl.ds(0, 8)], (1, -1)),
            (col_out.at[n, pl.ds(0, groups), back], col_in.at[n, 0, pl.ds(0, groups), pl.ds(24, 8)], (-1, 1)),
            (col_out.at[n, pl.ds(0, groups), back], col_in.at[n, 1, pl.ds(0, groups), pl.ds(24, 8)], (-1, -1)),
        ]
        return [
            pltpu.make_async_remote_copy(
                src_ref=src,
                dst_ref=dst,
                send_sem=xch_send.at[n, k],
                recv_sem=xch_recv.at[n, k],
                device_id=around(*to),
                device_id_type=MESH,
            )
            for k, (src, dst, to) in enumerate(plan)
        ]

    def halo_pack(n, ref, base, quads):
        lane = lanes_of((TILE_ROWS, LANES))

        def cols_of(f, packed, slot):
            both = jnp.where(lane < 64, ref[base + f, 0, CORE], ref[base + f, 1, CORE])
            moved = pltpu.roll(both, lax.rem(4 * slot + 2, LANES), 1)
            return jnp.where(lane // 4 == slot, moved, packed)

        for g in range((quads + 7) // 8):
            count = min(32, 4 * quads - 32 * g)

            def quad(k, packed):
                for u in range(4):
                    packed = cols_of(32 * g + 4 * k + u, packed, 4 * k + u)
                return packed

            col_out[n, g] = lax.fori_loop(0, count // 4, quad, jnp.zeros((TILE_ROWS, LANES), F32))

        def rows_quad(k, carry):
            for u in range(4):
                field = ref.at[base + 4 * k + u]
                for t in range(2):
                    row_out[n, 0, k, t, pl.ds(2 * u, 2)] = field[t, pl.ds(22, 2)]
                    row_out[n, 1, k, t, pl.ds(2 * u, 2)] = field[t, pl.ds(8, 2)]
            return carry

        lax.fori_loop(0, quads, rows_quad, 0)

    def halo_unpack(n, ref, base, quads):
        shape = (32, LANES)
        lane, place = lanes_of(shape), rows_of(shape)
        side = jnp.where(lax.rem(lane, 4) < 2, west, east)
        side = side * jnp.where(place < 8, north, jnp.where(place >= 24, south, 1.0))
        for g in range((quads + 7) // 8):
            count = min(32, 4 * quads - 32 * g)
            packed = jnp.where(lax.rem(lane, 4) < 2, col_in[n, 0, g], col_in[n, 1, g]) * side

            def quad(k, carry):
                for u in range(4):
                    slot = 4 * k + u
                    moved = pltpu.roll(packed, lax.rem(2 * LANES - 4 * slot - 2, LANES), 1)
                    ref[base + 32 * g + slot, 2] = moved
                return carry

            lax.fori_loop(0, count // 4, quad, 0)

        def rows_quad(k, carry):
            for u in range(4):
                for t in range(2):
                    ref[base + 4 * k + u, t, pl.ds(6, 2)] = row_in[n, 0, k, t, pl.ds(2 * u, 2)] * north
                    ref[base + 4 * k + u, t, pl.ds(24, 2)] = row_in[n, 1, k, t, pl.ds(2 * u, 2)] * south
            return carry

        lax.fori_loop(0, quads, rows_quad, 0)

    def bytes_of(ref, sem):
        pltpu.make_async_copy(ref, ref, sem).wait()

    def sum_scatter(n):
        def scatter(k, carry):
            other, device = peer(k)
            pltpu.make_async_remote_copy(
                src_ref=sum_in.at[n, other],
                dst_ref=sum_near.at[n, k],
                send_sem=sum_send.at[n, 0],
                recv_sem=sum_recv.at[n, 0],
                device_id=device,
                device_id_type=MESH,
            ).start()
            return carry

        lax.fori_loop(1, group, scatter, 0)
        sum_near[n, 0] = sum_in[n, mine]

    def sum_spread(n):
        bytes_of(sum_near.at[n, pl.ds(1, group - 1)], sum_recv.at[n, 0])
        sum_z[n, chip] = jnp.sum(sum_near[n], axis=0)

        def spread(k, carry):
            pltpu.make_async_remote_copy(
                src_ref=sum_z.at[n, chip],
                dst_ref=sum_z.at[n, chip],
                send_sem=sum_send.at[n, 1],
                recv_sem=sum_recv.at[n, 1],
                device_id=stack(k),
                device_id_type=MESH,
            ).start()
            return carry

        lax.fori_loop(1, chips, spread, 0)

    def sum_gather(n):
        bytes_of(sum_z.at[n, pl.ds(1, chips - 1)], sum_recv.at[n, 1])
        sum_out[n, mine] = jnp.sum(sum_z[n], axis=0)

        def gather(k, carry):
            pltpu.make_async_remote_copy(
                src_ref=sum_out.at[n, mine],
                dst_ref=sum_out.at[n, mine],
                send_sem=sum_send.at[n, 2],
                recv_sem=sum_recv.at[n, 2],
                device_id=peer(k)[1],
                device_id_type=MESH,
            ).start()
            return carry

        lax.fori_loop(1, group, gather, 0)

    def sum_done(n):
        bytes_of(sum_near.at[n, pl.ds(1, group - 1)], sum_recv.at[n, 2])

    def sum_drain(n):
        bytes_of(sum_near.at[n, pl.ds(1, group - 1)], sum_send.at[n, 0])
        bytes_of(sum_z.at[n, pl.ds(1, chips - 1)], sum_send.at[n, 1])
        bytes_of(sum_near.at[n, pl.ds(1, group - 1)], sum_send.at[n, 2])

    def chunk(k):
        return k // per, pl.ds(8 * (k % per), 8)

    def to_district(n, count, first):
        segacc[...] = jnp.zeros_like(segacc)
        size = count * DHI

        def line(i, carry):
            value = cells[pl.ds(0, count), pl.ds(i, 1), :]
            high = value.astype(jnp.bfloat16).astype(F32)
            here = (hi_id[pl.ds(i, 1), :] == rows_of((DHI, 2 * LANES)))[None]
            total = jnp.zeros((size, DLO), F32)
            for part in (high, value - high):
                spread = jnp.where(here, jnp.broadcast_to(part, (count, DHI, 2 * LANES)), 0.0)
                total += lax.dot_general(
                    spread.reshape(size, 2 * LANES).astype(jnp.bfloat16),
                    hot[i],
                    (((1,), (1,)), ((), ())),
                    preferred_element_type=F32,
                )
            segacc[pl.ds(0, size), :] += total
            return carry

        lax.fori_loop(0, TILE_ROWS, line, 0)
        for b in range(count):
            for t in range(3):
                at, part = chunk(3 * (first + b) + t)
                sum_in[n, at, part] = segacc[pl.ds(DHI * b, DHI), pl.ds(LANES * t, LANES)]

    def from_district(slot, count, first):
        values = jnp.concatenate(
            [
                jnp.concatenate([table[slot + s, r, t] for t in range(3)], axis=1)
                for s in range(count)
                for r in range(RHS)
            ],
            axis=0,
        )
        high = values.astype(jnp.bfloat16)
        low = (values - high.astype(F32)).astype(jnp.bfloat16)

        def line(i, carry):
            hot_here = hot[i]
            picked = jnp.dot(high, hot_here, preferred_element_type=F32) + jnp.dot(
                low, hot_here, preferred_element_type=F32
            )
            here = (hi_id[pl.ds(i, 1), :] == rows_of((DHI, 2 * LANES)))[None]
            picked = jnp.where(here, picked.reshape(count * RHS, DHI, 2 * LANES), 0.0)
            looks[pl.ds(first, count * RHS), pl.ds(i, 1), :] = jnp.sum(picked, axis=1, keepdims=True)
            return carry

        lax.fori_loop(0, TILE_ROWS, line, 0)

    def cells_of(load, first):
        def one(r, carry):
            for t in range(2):
                total = jnp.zeros((TILE_ROWS, LANES), F32)
                for m in range(MONTHS):
                    total += cross[m, t] * load(r * MONTHS + m, t)
                cells[first + r, :, pl.ds(LANES * t, LANES)] = total
            return carry

        lax.fori_loop(0, RHS, one, 0)

    def core_of(slot):
        return lambda f, t: basis[slot * FIELDS + f, t, CORE]

    def smooth(slot):
        def one(r, carry):
            base = slot * FIELDS + r * MONTHS
            for mb in range(0, MONTHS, 4):
                months = pl.ds(base + mb, 4)
                here = [basis[months, t, pl.ds(4, 24)] for t in range(3)]
                e, w = beside(here)
                for t in range(3):
                    n_val = basis[months, t, pl.ds(3, 24)]
                    s_val = basis[months, t, pl.ds(5, 24)]
                    lap = coef[4, t] * here[t] - coef[0, t] * e[t] - coef[1, t] * w[t]
                    lap = lap - coef[2, t] * s_val - coef[3, t] * n_val
                    inner[pl.ds(mb, 4), t] = headw[pl.ds(mb, 4), t] * lap
            for t in range(2):
                totals = [jnp.zeros((TILE_ROWS, LANES), F32)] * CROPS
                for m in range(MONTHS):
                    value = basis[base + m, t, CORE]
                    totals = [totals[c] + wu_ref[m, c] * value for c in range(CROPS)]
                for c in range(CROPS):
                    grads[c, t] = totals[c] * wcs[c, t]
            for mb in range(0, MONTHS, 4):
                here = [inner[pl.ds(mb, 4), t, pl.ds(4, 16)] for t in range(3)]
                e, w = beside(here)
                for t in range(2):
                    n_val = inner[pl.ds(mb, 4), t, pl.ds(3, 16)]
                    s_val = inner[pl.ds(mb, 4), t, pl.ds(5, 16)]
                    lap = coefc[4, t] * here[t] - coefc[0, t] * e[t] - coefc[1, t] * w[t]
                    lap = lap - coefc[2, t] * s_val - coefc[3, t] * n_val
                    lap = lap + PROXIMAL * basis[pl.ds(base + mb, 4), t, CORE]
                    for u in range(4):
                        m = mb + u
                        total = lap[u]
                        for c in range(CROPS):
                            total = total + wu_ref[m, c] * grads[c, t]
                        image[r * MONTHS + m, t] = dinv[m, t] * total
            return carry

        lax.fori_loop(0, RHS, one, 0)

    def advance(slot, look, shift):
        def one(r, carry):
            for t in range(2):
                seen = looks[look + r, :, pl.ds(LANES * t, LANES)]
                for m in range(MONTHS):
                    f = r * MONTHS + m
                    basis[(slot + 1) * FIELDS + f, t, CORE] = (
                        image[f, t] + crossd[m, t] * seen - shift * basis[slot * FIELDS + f, t, CORE]
                    )
            return carry

        lax.fori_loop(0, RHS, one, 0)

    for t in range(2):
        span = pl.ds(LANES * t, LANES)
        for k in range(2):
            stat[k, t, CORE] = cond_ref[k, :, span]
        for m in range(MONTHS):
            stat[2 + m, t, CORE] = head_ref[m, :, span]
        for k in range(2 + MONTHS, 16):
            stat[k, t, CORE] = jnp.zeros((TILE_ROWS, LANES), F32)
    halo_pack(0, stat, 0, 4)
    pl.semaphore_wait(barrier, group + chips - 2 + len(offsets))
    halo_stat = halo_copies(0, 4, 1)
    for copy in halo_stat:
        copy.start()

    scale = (districts / grid_cells) ** 0.5
    ids = id_ref[...]
    high_id = jnp.zeros_like(ids)
    for k in range(1, DHI):
        high_id = high_id + jnp.where(ids >= k * DLO, 1, 0)
    hi_id[...] = high_id
    lo_id[...] = ids - DLO * high_id

    def hot_line(i, carry):
        same = lo_id[pl.ds(i, 1), :] == rows_of((DLO, 2 * LANES))
        hot[i] = jnp.where(same, 1.0, 0.0).astype(jnp.bfloat16)
        return carry

    lax.fori_loop(0, TILE_ROWS, hot_line, 0)
    for t in range(2):
        span = pl.ds(LANES * t, LANES)
        live = active_ref[:, span].astype(F32)
        weight = live * climate_ref[:, span]
        crops = [crop_ref[c, :, span] for c in range(CROPS)]
        own = jnp.zeros((TILE_ROWS, LANES), F32)
        for c in range(CROPS):
            use = scale * use_ref[c] * live
            own = own + use * use * crops[c]
            wcs[c, t] = weight * weight * crops[c]
        cells[0, :, span] = own
        for m in range(MONTHS):
            square = jnp.zeros((TILE_ROWS, LANES), F32)
            mixed = jnp.zeros((TILE_ROWS, LANES), F32)
            for c in range(CROPS):
                drawn = wu_ref[m, c] * crops[c]
                square = square + wu_ref[m, c] * drawn
                mixed = mixed + use_ref[c] * drawn
            diag[m, t] = weight * weight * square + PROXIMAL
            cross[m, t] = weight * live * (scale * mixed)
    for r in range(RHS):
        for hi in range(DHI):
            for t in range(3):
                at = LANES * (3 * hi + t)
                bdi[r, t, pl.ds(hi, 1)] = rdi_ref[pl.ds(r, 1), pl.ds(at, LANES)]

    for copy in halo_stat:
        copy.wait_recv()
    halo_unpack(0, stat, 0, 4)
    window = pl.ds(4, 24)
    faces = [[stat[k, t, window] for t in range(3)] for k in range(2)]
    east_side, west_side = beside(faces[0])
    for t in range(3):
        south_north = stat[1, t, pl.ds(3, 24)]
        coef[0, t] = faces[0][t]
        coef[1, t] = west_side[t]
        coef[2, t] = faces[1][t]
        coef[3, t] = south_north
        coef[4, t] = faces[0][t] + west_side[t] + faces[1][t] + south_north
    for k in range(5):
        for t in range(2):
            coefc[k, t] = coef[k, t, pl.ds(4, 16)]

    def month_diag(m, carry):
        for t in range(3):
            headw[m, t] = stat[2 + m, t, window]
        here = [stat[2 + m, t, CORE] for t in range(3)]
        e, w = beside(here)
        for t in range(2):
            fe, fw, fs, fn, total = [coefc[k, t] for k in range(5)]
            value = diag[m, t] + here[t] * total * total + fe * fe * e[t] + fw * fw * w[t]
            value = value + fs * fs * stat[2 + m, t, pl.ds(9, 16)] + fn * fn * stat[2 + m, t, pl.ds(7, 16)]
            diag[m, t] = value
            inverse = 1.0 / value
            dinv[m, t] = inverse
            crossd[m, t] = cross[m, t] * inverse
        return carry

    lax.fori_loop(0, MONTHS, month_diag, 0)

    def start_basis(r, carry):
        for t in range(2):
            for m in range(MONTHS):
                f = r * MONTHS + m
                basis[f, t, CORE] = rhs_ref[f, :, pl.ds(LANES * t, LANES)] * dinv[m, t]
        return carry

    lax.fori_loop(0, RHS, start_basis, 0)

    halo_pack(1, basis, 0, FIELDS // 4)
    halo_first = halo_copies(1, FIELDS // 4, 2)
    for copy in halo_first:
        copy.start()
    for t in range(2):
        total = jnp.zeros((TILE_ROWS, LANES), F32)
        for m in range(MONTHS):
            total += cross[m, t] * crossd[m, t]
        cells[1, :, pl.ds(LANES * t, LANES)] = total
    cells_of(core_of(0), 2)
    sum_in[...] = jnp.zeros_like(sum_in)
    to_district(0, 2 + RHS, 0)
    sum_scatter(0)

    for copy in halo_first:
        copy.wait_recv()
    halo_unpack(1, basis, 0, FIELDS // 4)
    sum_spread(0)
    smooth(0)
    cells_of(lambda f, t: image[f, t], 0)
    to_district(1, RHS, 0)
    sum_scatter(1)
    sum_gather(0)
    sum_done(0)

    def total_of(n, b):
        return jnp.stack([sum_out[(n,) + chunk(3 * b + t)] for t in range(3)])

    diag_di[...] = total_of(0, 0) + PROXIMAL
    wide[...] = total_of(0, 1)
    for r in range(RHS):
        t0 = bdi[r] / diag_di[...]
        table[0, r] = t0
        table[1, r] = total_of(0, 2 + r) / diag_di[...] + (1 - SHIFTS[0]) * t0
    from_district(0, 2, 0)
    advance(0, 0, SHIFTS[0])
    halo_pack(2, basis, FIELDS, FIELDS // 4)
    halo_second = halo_copies(2, FIELDS // 4, 2)
    for copy in halo_second:
        copy.start()
    sum_spread(1)
    for copy in halo_second:
        copy.wait_recv()
    halo_unpack(2, basis, FIELDS, FIELDS // 4)
    smooth(1)
    advance(1, RHS, SHIFTS[1])
    halo_pack(3, basis, 2 * FIELDS, FIELDS // 4)
    halo_third = halo_copies(3, FIELDS // 4, 2)
    for copy in halo_third:
        copy.start()
    sum_gather(1)
    cells_of(core_of(2), 0)
    to_district(2, RHS, 0)
    for copy in halo_third:
        copy.wait_recv()
    halo_unpack(3, basis, 2 * FIELDS, FIELDS // 4)
    smooth(2)
    sum_done(1)
    for r in range(RHS):
        z1 = total_of(1, r) + wide[...] * table[0, r] - SHIFTS[0] * total_of(0, 2 + r)
        table[2, r] = z1 / diag_di[...] + (1 - SHIFTS[1]) * table[1, r]
    from_district(2, 1, 0)
    advance(2, 0, SHIFTS[2])
    cells_of(core_of(3), 0)
    to_district(2, RHS, RHS)
    sum_scatter(2)
    halo_pack(4, basis, 3 * FIELDS, FIELDS // 4)
    halo_fourth = halo_copies(4, FIELDS // 4, 2)
    for copy in halo_fourth:
        copy.start()

    shape = (8, LANES)

    def inner_products(r, packed):
        totals = [jnp.zeros(shape, F32) for _ in PAIRS]
        for m in range(MONTHS):
            for t in range(2):
                values = [basis[s * FIELDS + r * MONTHS + m, t, CORE] for s in range(ITERS)]
                scaled = [diag[m, t] * v for v in values]
                for n, (i, j) in enumerate(PAIRS):
                    term = scaled[i] * values[j]
                    totals[n] = totals[n] + (term[:8] + term[8:])
        for n, total in enumerate(totals):
            here = (rows_of(shape) == r) & (lanes_of(shape) == n)
            packed = jnp.where(here, jnp.sum(total, keepdims=True), packed)
        return packed

    packed = lax.fori_loop(0, RHS, inner_products, jnp.zeros(shape, F32))
    for copy in halo_fourth:
        copy.wait_recv()
    halo_unpack(4, basis, 3 * FIELDS, FIELDS // 4)
    sum_spread(2)
    smooth(3)

    def top_product(r, packed):
        total = jnp.zeros(shape, F32)
        for m in range(MONTHS):
            for t in range(2):
                f = r * MONTHS + m
                term = diag[m, t] * basis[3 * FIELDS + f, t, CORE] * image[f, t]
                total = total + (term[:8] + term[8:])
        here = (rows_of(shape) == r) & (lanes_of(shape) == len(PAIRS))
        return jnp.where(here, jnp.sum(total, keepdims=True), packed)

    late_in[...] = lax.fori_loop(0, RHS, top_product, packed)

    def late_first(k, carry):
        pltpu.make_async_remote_copy(
            src_ref=late_in,
            dst_ref=late_near.at[mine],
            send_sem=sum_send.at[3, 0],
            recv_sem=sum_recv.at[3, 0],
            device_id=peer(k)[1],
            device_id_type=MESH,
        ).start()
        return carry

    lax.fori_loop(1, group, late_first, 0)
    late_near[mine] = late_in[...]
    sum_gather(2)
    bytes_of(late_near.at[pl.ds(1, group - 1)], sum_recv.at[3, 0])
    late_z[chip] = jnp.sum(late_near[...], axis=0)

    def late_second(k, carry):
        pltpu.make_async_remote_copy(
            src_ref=late_z.at[chip],
            dst_ref=late_z.at[chip],
            send_sem=sum_send.at[3, 1],
            recv_sem=sum_recv.at[3, 1],
            device_id=stack(k),
            device_id_type=MESH,
        ).start()
        return carry

    lax.fori_loop(1, chips, late_second, 0)
    sum_done(2)
    for r in range(RHS):
        table[3, r] = total_of(2, r) / diag_di[...] + (1 - SHIFTS[2]) * table[2, r]
        table[4, r] = total_of(2, RHS + r) / diag_di[...] + (1 - SHIFTS[3]) * table[3, r]
    from_district(3, 1, 0)

    def district_part(i, j):
        out = jnp.zeros(shape, F32)
        for r in range(RHS):
            if j < ITERS:
                term = diag_di[...] * table[i, r] * table[j, r]
            else:
                term = table[3, r] * (2 * total_of(2, RHS + r) + diag_di[...] * table[3, r])
            line = jnp.sum(jnp.sum(term, axis=0), axis=0, keepdims=True)
            out = jnp.where(rows_of(shape) == r, line, out)
        return out

    parts = [district_part(i, j) for i, j in PAIRS + ((3, ITERS),)]
    bytes_of(late_z.at[pl.ds(1, chips - 1)], sum_recv.at[3, 1])
    totals = jnp.sum(late_z[...], axis=0)
    gram = [[None] * (ITERS + 1) for _ in range(ITERS + 1)]
    values = []
    for n, part in enumerate(parts):
        both = part + jnp.where(lanes_of(shape) == n, totals, 0.0)
        values.append(jnp.broadcast_to(jnp.sum(both, axis=1, keepdims=True), shape))
    for n, (i, j) in enumerate(PAIRS):
        gram[i][j] = gram[j][i] = values[n]
    for i in range(ITERS):
        ahead = values[-1] if i == ITERS - 1 else gram[i + 1][ITERS - 1] + SHIFTS[i] * gram[i][ITERS - 1]
        gram[i][ITERS] = ahead - SHIFTS[ITERS - 1] * gram[i][ITERS - 1]

    one, zero = jnp.ones(shape, F32), jnp.zeros(shape, F32)
    x, res, dirn = [zero] * ITERS, [one] + [zero] * ITERS, [one] + [zero] * (ITERS - 1)
    rho = gram[0][0]
    for it in range(ITERS):
        moved = [zero] * (ITERS + 1)
        for k in range(it + 1):
            moved[k + 1] = moved[k + 1] + dirn[k]
            moved[k] = moved[k] + SHIFTS[k] * dirn[k]
        curve = zero
        for i in range(it + 1):
            line = zero
            for j in range(it + 2):
                line = line + moved[j] * gram[i][j]
            curve = curve + dirn[i] * line
        alpha = rho / curve
        x = [x[i] + alpha * dirn[i] for i in range(ITERS)]
        res = [res[i] - alpha * moved[i] for i in range(ITERS + 1)]
        if it + 1 < ITERS:
            rho_new = zero
            for i in range(it + 2):
                line = zero
                for j in range(it + 2):
                    line = line + res[j] * gram[i][j]
                rho_new = rho_new + res[i] * line
            ratio = rho_new / rho
            rho = rho_new
            dirn = [res[i] + ratio * dirn[i] for i in range(ITERS)]
    for k, value in enumerate(x + res):
        factors[k] = value

    def finish(r, carry):
        xs = [factors[k, pl.ds(r, 1)] for k in range(ITERS)]
        rs = [factors[ITERS + k, pl.ds(r, 1)] for k in range(ITERS + 1)]
        for t in range(2):
            span = pl.ds(LANES * t, LANES)
            seen = looks[r, :, span]
            for m in range(MONTHS):
                f = r * MONTHS + m
                vs = [basis[s * FIELDS + f, t, CORE] for s in range(ITERS)]
                vs.append(image[f, t] + crossd[m, t] * seen - SHIFTS[3] * vs[3])
                dual_ref[f, :, span] = xs[0] * vs[0] + xs[1] * vs[1] + xs[2] * vs[2] + xs[3] * vs[3]
                total = rs[0] * vs[0]
                for k in range(1, ITERS + 1):
                    total = total + rs[k] * vs[k]
                res_ref[f, :, span] = diag[m, t] * total
        return carry

    lax.fori_loop(0, RHS, finish, 0)
    for r in range(RHS):
        xs = [factors[k, pl.ds(r, 1)] for k in range(ITERS)]
        rs = [factors[ITERS + k, pl.ds(r, 1)] for k in range(ITERS + 1)]
        for t in range(3):
            dual = xs[0] * table[0, r, t]
            total = rs[0] * table[0, r, t]
            for k in range(1, ITERS):
                dual = dual + xs[k] * table[k, r, t]
            for k in range(1, ITERS + 1):
                total = total + rs[k] * table[k, r, t]
            total = total * diag_di[t]
            for hi in range(DHI):
                span = pl.ds(LANES * (3 * hi + t), LANES)
                dual_di_ref[pl.ds(r, 1), span] = dual[hi : hi + 1]
                res_di_ref[pl.ds(r, 1), span] = total[hi : hi + 1]

    for copies in (halo_stat, halo_first, halo_second, halo_third, halo_fourth):
        for copy in copies:
            copy.wait_send()
    for n in range(3):
        sum_drain(n)
    bytes_of(late_near.at[pl.ds(1, group - 1)], sum_send.at[3, 0])
    bytes_of(late_z.at[pl.ds(1, chips - 1)], sum_send.at[3, 1])


def body(
    right_aquifer,
    right_district,
    head_scale,
    crop_scale,
    conductance,
    water_use,
    climate,
    district_use,
    district_id,
    active,
):
    rows, cols = lax.axis_size("row"), lax.axis_size("col")
    group, chips = 2 * cols, rows // 2
    per = CHUNKS // group
    tile_rows, tile_cols = climate.shape
    grid_cells = tile_rows * rows * tile_cols * cols
    whole = pl.BlockSpec(memory_space=pltpu.VMEM)
    scalars = pl.BlockSpec(memory_space=pltpu.SMEM)
    block = (FIELDS, tile_rows, tile_cols)
    vmem = lambda *shape: pltpu.VMEM(shape, F32)
    core = (2, TILE_ROWS, LANES)
    outs = pl.pallas_call(
        functools.partial(kernel, grid_cells),
        out_shape=(
            jax.ShapeDtypeStruct(block, F32),
            jax.ShapeDtypeStruct(right_district.shape, F32),
            jax.ShapeDtypeStruct(block, F32),
            jax.ShapeDtypeStruct(right_district.shape, F32),
        ),
        in_specs=[whole] * 8 + [scalars] * 2,
        out_specs=(whole,) * 4,
        scratch_shapes=[
            vmem(ITERS * FIELDS, 3, 32, LANES),
            vmem(FIELDS, *core),
            vmem(16, 3, 32, LANES),
            vmem(5, 3, 24, LANES),
            vmem(MONTHS, 3, 24, LANES),
            vmem(5, *core),
            vmem(MONTHS, *core),
            vmem(MONTHS, *core),
            vmem(MONTHS, *core),
            vmem(MONTHS, *core),
            vmem(CROPS, *core),
            vmem(MONTHS, 3, 24, LANES),
            vmem(CROPS, *core),
            pltpu.VMEM((TILE_ROWS, DLO, 2 * LANES), jnp.bfloat16),
            pltpu.VMEM((TILE_ROWS, 2 * LANES), jnp.int32),
            pltpu.VMEM((TILE_ROWS, 2 * LANES), jnp.int32),
            vmem(2 + RHS, TILE_ROWS, 2 * LANES),
            vmem(2 * RHS, TILE_ROWS, 2 * LANES),
            vmem((2 + RHS) * DHI, DLO),
            vmem(ITERS + 1, RHS, 3, DHI, LANES),
            vmem(3, DHI, LANES),
            vmem(3, DHI, LANES),
            vmem(RHS, 3, DHI, LANES),
            vmem(3, group, 8 * per, LANES),
            vmem(3, group, 8 * per, LANES),
            vmem(3, chips, 8 * per, LANES),
            vmem(3, group, 8 * per, LANES),
            vmem(group, 8, LANES),
            vmem(chips, 8, LANES),
            vmem(8, LANES),
            vmem(2 * ITERS + 1, 8, LANES),
            vmem(5, 2, FIELDS // 4, 2, 8, LANES),
            vmem(5, 2, FIELDS // 4, 2, 8, LANES),
            vmem(5, 2, TILE_ROWS, LANES),
            vmem(5, 2, 2, 32, LANES),
            pltpu.SemaphoreType.DMA((5, 8)),
            pltpu.SemaphoreType.DMA((5, 8)),
            pltpu.SemaphoreType.DMA((4, 3)),
            pltpu.SemaphoreType.DMA((4, 3)),
        ],
        compiler_params=pltpu.CompilerParams(
            collective_id=0, has_side_effects=True, vmem_limit_bytes=48 * 1024 * 1024
        ),
    )(
        right_aquifer.reshape(block),
        right_district,
        head_scale,
        crop_scale,
        conductance,
        climate,
        district_id,
        active,
        water_use,
        district_use,
    )
    dual, dual_di, res, res_di = outs
    return dual.reshape(right_aquifer.shape), dual_di, res.reshape(right_aquifer.shape), res_di


def solution(mesh):
    placed = (
        P(None, None, "row", "col"),
        P(),
        P(None, "row", "col"),
        P(None, "row", "col"),
        P(None, "row", "col"),
        P(),
        P("row", "col"),
        P(),
        P("row", "col"),
        P("row", "col"),
    )
    return jax.shard_map(
        body,
        mesh=mesh,
        in_specs=placed,
        out_specs=(P(None, None, "row", "col"), P(), P(None, None, "row", "col"), P()),
        check_vma=False,
    )
```

```python
import functools

import jax
import jax.numpy as jnp
from jax import lax
from jax.experimental import pallas as pl
from jax.experimental.pallas import tpu as pltpu
from jax.sharding import PartitionSpec as P

ITERS = 4
RHS = 4
MONTHS = 12
CROPS = 6
FIELDS = RHS * MONTHS
DHI = 16
DLO = 256
LANES = 128
TILE_ROWS = 16
CHUNKS = 32
LINES = 21
ID_FIELD = 14
PROXIMAL = 0.05
SHIFTS = (0.5, 8.0, 3.0, 1.0)
PAIRS = tuple((i, j) for i in range(ITERS) for j in range(i, ITERS))
MESH = pl.DeviceIdType.MESH
F32 = jnp.float32
CORE = pl.ds(8, 16)


def lanes_of(shape):
    return lax.broadcasted_iota(jnp.int32, shape, len(shape) - 1)


def rows_of(shape):
    return lax.broadcasted_iota(jnp.int32, shape, len(shape) - 2)


def beside(tiles):
    axis = tiles[0].ndim - 1
    lane = lanes_of(tiles[0].shape)
    ahead = [pltpu.roll(t, LANES - 1, axis) for t in tiles]
    behind = [pltpu.roll(t, 1, axis) for t in tiles]
    east = [jnp.where(lane == LANES - 1, ahead[(n + 1) % 3], ahead[n]) for n in range(3)]
    west = [jnp.where(lane == 0, behind[(n + 2) % 3], behind[n]) for n in range(3)]
    return east, west


def kernel(
    grid_cells,
    rhs_hbm,
    rdi_hbm,
    head_hbm,
    crop_hbm,
    cond_hbm,
    climate_hbm,
    id_hbm,
    active_hbm,
    wu_hbm,
    use_hbm,
    dual_ref,
    dual_di_ref,
    res_ref,
    res_di_ref,
    basis,
    image,
    stat,
    coef,
    headw,
    coefc,
    diag,
    dinv,
    cross,
    wcs,
    inner,
    grads,
    hot,
    lo_id,
    hi_id,
    cells,
    looks,
    wide_look,
    spread,
    rdi_ref,
    crop_ref,
    climate_ref,
    id_ref,
    active_ref,
    table,
    diag_di,
    wide,
    bdi,
    sum_in,
    sum_near,
    sum_z,
    sum_out,
    late_near,
    late_z,
    late_in,
    factors,
    row_out,
    row_in,
    col_out,
    col_in,
    xch_send,
    xch_recv,
    sum_send,
    sum_recv,
    load_sem,
    wu_ref,
    use_ref,
):
    rows, cols = lax.axis_size("row"), lax.axis_size("col")
    chips, group = rows // 2, 2 * cols
    per = CHUNKS // group
    row, col = lax.axis_index("row"), lax.axis_index("col")
    chip, core = row // 2, lax.rem(row, 2)
    mine = core * cols + col
    districts = rdi_ref.shape[1]

    def slot_at(slot):
        return slot * FIELDS + (MONTHS if slot else 0)


    def peer(k):
        other = lax.rem(mine + k, group)
        return other, (chip * 2 + other // cols, lax.rem(other, cols))

    def stack(k):
        return (lax.rem(row + 2 * k, rows), col)

    def around(dr, dc):
        return (lax.rem(row + dr + rows, rows), lax.rem(col + dc + cols, cols))

    loads = []
    for t in range(2):
        span = pl.ds(LANES * t, LANES)
        loads.append((cond_hbm.at[:, :, span], stat.at[pl.ds(0, 2), t, CORE]))
        loads.append((head_hbm.at[:, :, span], stat.at[pl.ds(2, MONTHS), t, CORE]))
    loads += [(id_hbm, id_ref), (climate_hbm, climate_ref), (active_hbm, active_ref)]
    loads += [(wu_hbm, wu_ref), (use_hbm, use_ref), (crop_hbm, crop_ref), (rdi_hbm, rdi_ref)]
    for t in range(2):
        loads.append((rhs_hbm.at[:, :, pl.ds(LANES * t, LANES)], basis.at[pl.ds(0, FIELDS), t, CORE]))
    loads = [pltpu.make_async_copy(src, dst, load_sem.at[k]) for k, (src, dst) in enumerate(loads)]
    for load in loads:
        load.start()

    barrier = pltpu.get_barrier_semaphore()

    def greet(k, carry):
        pl.semaphore_signal(barrier, inc=1, device_id=peer(k)[1], device_id_type=MESH)
        return carry

    def greet_stack(k, carry):
        pl.semaphore_signal(barrier, inc=1, device_id=stack(k), device_id_type=MESH)
        return carry

    lax.fori_loop(1, group, greet, 0)
    lax.fori_loop(1, chips, greet_stack, 0)
    offsets = [(dr, dc) for dr in (-1, 0, 1) for dc in (-1, 0, 1) if dr or dc]
    for dr, dc in offsets:
        pl.semaphore_signal(barrier, inc=1, device_id=around(dr, dc), device_id_type=MESH)

    north = jnp.where(row > 0, 1.0, 0.0).astype(F32)
    south = jnp.where(row < rows - 1, 1.0, 0.0).astype(F32)
    west = jnp.where(col > 0, 1.0, 0.0).astype(F32)
    east = jnp.where(col < cols - 1, 1.0, 0.0).astype(F32)

    def halo_copies(n, quads, groups):
        ahead, back = pl.ds(8, 8), pl.ds(0, 8)
        plan = [
            (row_out.at[n, 0, pl.ds(0, quads)], row_in.at[n, 0, pl.ds(0, quads)], (1, 0)),
            (row_out.at[n, 1, pl.ds(0, quads)], row_in.at[n, 1, pl.ds(0, quads)], (-1, 0)),
            (col_out.at[n, pl.ds(0, groups)], col_in.at[n, 0, pl.ds(0, groups), CORE], (0, 1)),
            (col_out.at[n, pl.ds(0, groups)], col_in.at[n, 1, pl.ds(0, groups), CORE], (0, -1)),
            (col_out.at[n, pl.ds(0, groups), ahead], col_in.at[n, 0, pl.ds(0, groups), pl.ds(0, 8)], (1, 1)),
            (col_out.at[n, pl.ds(0, groups), ahead], col_in.at[n, 1, pl.ds(0, groups), pl.ds(0, 8)], (1, -1)),
            (col_out.at[n, pl.ds(0, groups), back], col_in.at[n, 0, pl.ds(0, groups), pl.ds(24, 8)], (-1, 1)),
            (col_out.at[n, pl.ds(0, groups), back], col_in.at[n, 1, pl.ds(0, groups), pl.ds(24, 8)], (-1, -1)),
        ]
        return [
            pltpu.make_async_remote_copy(
                src_ref=src,
                dst_ref=dst,
                send_sem=xch_send.at[n, k],
                recv_sem=xch_recv.at[n, k],
                device_id=around(*to),
                device_id_type=MESH,
            )
            for k, (src, dst, to) in enumerate(plan)
        ]

    def halo_pack(n, ref, base, quads):
        lane = lanes_of((TILE_ROWS, LANES))

        def cols_of(f, packed, slot):
            both = jnp.where(lane < 64, ref[base + f, 0, CORE], ref[base + f, 1, CORE])
            moved = pltpu.roll(both, lax.rem(4 * slot + 2, LANES), 1)
            return jnp.where(lane // 4 == slot, moved, packed)

        for g in range((quads + 7) // 8):
            count = min(32, 4 * quads - 32 * g)

            def quad(k, packed):
                for u in range(4):
                    packed = cols_of(32 * g + 4 * k + u, packed, 4 * k + u)
                return packed

            col_out[n, g] = lax.fori_loop(0, count // 4, quad, jnp.zeros((TILE_ROWS, LANES), F32))

        def rows_quad(k, carry):
            for u in range(4):
                field = ref.at[base + 4 * k + u]
                for t in range(2):
                    row_out[n, 0, k, t, pl.ds(2 * u, 2)] = field[t, pl.ds(22, 2)]
                    row_out[n, 1, k, t, pl.ds(2 * u, 2)] = field[t, pl.ds(8, 2)]
            return carry

        lax.fori_loop(0, quads, rows_quad, 0)

    def halo_unpack(n, ref, base, quads):
        shape = (32, LANES)
        lane, place = lanes_of(shape), rows_of(shape)
        side = jnp.where(lax.rem(lane, 4) < 2, west, east)
        side = side * jnp.where(place < 8, north, jnp.where(place >= 24, south, 1.0))
        for g in range((quads + 7) // 8):
            count = min(32, 4 * quads - 32 * g)
            packed = jnp.where(lax.rem(lane, 4) < 2, col_in[n, 0, g], col_in[n, 1, g]) * side

            def quad(k, carry):
                for u in range(4):
                    slot = 4 * k + u
                    moved = pltpu.roll(packed, lax.rem(2 * LANES - 4 * slot - 2, LANES), 1)
                    ref[base + 32 * g + slot, 2] = moved
                return carry

            lax.fori_loop(0, count // 4, quad, 0)

        def rows_quad(k, carry):
            for u in range(4):
                for t in range(2):
                    ref[base + 4 * k + u, t, pl.ds(6, 2)] = row_in[n, 0, k, t, pl.ds(2 * u, 2)] * north
                    ref[base + 4 * k + u, t, pl.ds(24, 2)] = row_in[n, 1, k, t, pl.ds(2 * u, 2)] * south
            return carry

        lax.fori_loop(0, quads, rows_quad, 0)

    def bytes_of(ref, sem):
        pltpu.make_async_copy(ref, ref, sem).wait()

    def sum_scatter(n):
        def scatter(k, carry):
            other, device = peer(k)
            pltpu.make_async_remote_copy(
                src_ref=sum_in.at[n, other],
                dst_ref=sum_near.at[n, k],
                send_sem=sum_send.at[n, 0],
                recv_sem=sum_recv.at[n, 0],
                device_id=device,
                device_id_type=MESH,
            ).start()
            return carry

        lax.fori_loop(1, group, scatter, 0)
        sum_near[n, 0] = sum_in[n, mine]

    def sum_spread(n):
        bytes_of(sum_near.at[n, pl.ds(1, group - 1)], sum_recv.at[n, 0])
        sum_z[n, chip] = jnp.sum(sum_near[n], axis=0)

        def spread(k, carry):
            pltpu.make_async_remote_copy(
                src_ref=sum_z.at[n, chip],
                dst_ref=sum_z.at[n, chip],
                send_sem=sum_send.at[n, 1],
                recv_sem=sum_recv.at[n, 1],
                device_id=stack(k),
                device_id_type=MESH,
            ).start()
            return carry

        lax.fori_loop(1, chips, spread, 0)

    def sum_gather(n):
        bytes_of(sum_z.at[n, pl.ds(1, chips - 1)], sum_recv.at[n, 1])
        sum_out[n, mine] = jnp.sum(sum_z[n], axis=0)

        def gather(k, carry):
            pltpu.make_async_remote_copy(
                src_ref=sum_out.at[n, mine],
                dst_ref=sum_out.at[n, mine],
                send_sem=sum_send.at[n, 2],
                recv_sem=sum_recv.at[n, 2],
                device_id=peer(k)[1],
                device_id_type=MESH,
            ).start()
            return carry

        lax.fori_loop(1, group, gather, 0)

    def sum_done(n):
        bytes_of(sum_near.at[n, pl.ds(1, group - 1)], sum_recv.at[n, 2])

    def sum_drain(n):
        bytes_of(sum_near.at[n, pl.ds(1, group - 1)], sum_send.at[n, 0])
        bytes_of(sum_z.at[n, pl.ds(1, chips - 1)], sum_send.at[n, 1])
        bytes_of(sum_near.at[n, pl.ds(1, group - 1)], sum_send.at[n, 2])

    def chunk(k):
        return k // per, pl.ds(8 * (k % per), 8)

    def line_span(i):
        return pl.ds(pl.multiple_of(i * (2 * LANES), 2 * LANES), 2 * LANES)

    def to_district(n, count, first):
        size = count * DHI

        def line(i, carry):
            value = cells[pl.ds(0, count), pl.ds(i, 1), :]
            high = value.astype(jnp.bfloat16).astype(F32)
            here = (hi_id[pl.ds(i, 1), :] == rows_of((DHI, 2 * LANES)))[None]
            for k, part in enumerate((high, value - high)):
                part = jnp.where(here, jnp.broadcast_to(part, (count, DHI, 2 * LANES)), 0.0)
                spread[pl.ds(k * size, size), line_span(i)] = part.reshape(size, 2 * LANES).astype(jnp.bfloat16)
            return carry

        lax.fori_loop(0, TILE_ROWS, line, 0, unroll=2)
        total = lax.dot_general(
            hot[:, pl.ds(0, TILE_ROWS * 2 * LANES)], spread[pl.ds(0, 2 * size), :], (((1,), (1,)), ((), ())), preferred_element_type=F32
        ).T
        total = total[:size] + total[size:]
        for b in range(count):
            for t in range(2):
                for h in range(2):
                    at, part = chunk(4 * (first + b) + 2 * t + h)
                    sum_in[n, at, part] = total[DHI * b + 8 * h : DHI * b + 8 * h + 8, LANES * t : LANES * (t + 1)]

    def from_district(slot, count, first, lines=TILE_ROWS):
        size = count * RHS * DHI
        values = jnp.concatenate(
            [
                jnp.concatenate([table[slot + s, r, t] for t in range(2)], axis=1)
                for s in range(count)
                for r in range(RHS)
            ],
            axis=0,
        )
        high = values.astype(jnp.bfloat16).astype(F32)
        both = jnp.concatenate([high, values - high], axis=0).astype(jnp.bfloat16)

        def line(i, carry):
            picked = jnp.dot(both, hot[:, line_span(i)], preferred_element_type=F32)
            picked = (picked[:size] + picked[size:]).reshape(count * RHS, DHI, 2 * LANES)
            here = (hi_id[pl.ds(i, 1), :] == rows_of((DHI, 2 * LANES)))[None]
            picked = jnp.where(here, picked, 0.0)
            looks[pl.ds(first, count * RHS), pl.ds(i, 1), :] = jnp.sum(picked, axis=1, keepdims=True)
            return carry

        lax.fori_loop(0, lines, line, 0, unroll=3 if lines % 3 == 0 else 2)

    def cells_of(load, first):
        def one(r, carry):
            for t in range(2):
                total = jnp.zeros((TILE_ROWS, LANES), F32)
                for m in range(MONTHS):
                    total += cross[m, t] * load(r * MONTHS + m, t)
                cells[first + r, :, pl.ds(LANES * t, LANES)] = total
            return carry

        lax.fori_loop(0, RHS, one, 0)

    def core_of(slot):
        return lambda f, t: basis[slot_at(slot) + f, t, CORE]

    def smooth(slot, put):
        def one(r, carry):
            base = slot_at(slot) + r * MONTHS
            for mb in range(0, MONTHS, 4):
                months = pl.ds(base + mb, 4)
                here = [basis[months, t, pl.ds(4, 24)] for t in range(3)]
                e, w = beside(here)
                for t in range(3):
                    n_val = basis[months, t, pl.ds(3, 24)]
                    s_val = basis[months, t, pl.ds(5, 24)]
                    lap = coef[4, t] * here[t] - coef[0, t] * e[t] - coef[1, t] * w[t]
                    lap = lap - coef[2, t] * s_val - coef[3, t] * n_val
                    inner[pl.ds(mb, 4), t] = headw[pl.ds(mb, 4), t] * lap
            for t in range(2):
                totals = [jnp.zeros((TILE_ROWS, LANES), F32)] * CROPS
                for m in range(MONTHS):
                    value = basis[base + m, t, CORE]
                    totals = [totals[c] + wu_ref[c, m] * value for c in range(CROPS)]
                for c in range(CROPS):
                    grads[c, t] = totals[c] * wcs[c, t]
            for mb in range(0, MONTHS, 4):
                here = [inner[pl.ds(mb, 4), t, pl.ds(4, 16)] for t in range(3)]
                e, w = beside(here)
                for t in range(2):
                    n_val = inner[pl.ds(mb, 4), t, pl.ds(3, 16)]
                    s_val = inner[pl.ds(mb, 4), t, pl.ds(5, 16)]
                    lap = coefc[4, t] * here[t] - coefc[0, t] * e[t] - coefc[1, t] * w[t]
                    lap = lap - coefc[2, t] * s_val - coefc[3, t] * n_val
                    lap = lap + PROXIMAL * basis[pl.ds(base + mb, 4), t, CORE]
                    for u in range(4):
                        m = mb + u
                        total = lap[u]
                        for c in range(CROPS):
                            total = total + wu_ref[c, m] * grads[c, t]
                        put(r * MONTHS + m, t, dinv[m, t] * total)
            return carry

        lax.fori_loop(0, RHS, one, 0)

    def to_image(f, t, value):
        image[f, t] = value

    def to_second(f, t, value):
        basis[slot_at(1) + f, t, CORE] = value

    def advance_wide(shift):
        window = pl.ds(4, 24)

        def one(r, carry):
            for t in range(3):
                seen = wide_look[r, t, window]
                for m in range(MONTHS):
                    f = r * MONTHS + m
                    basis[slot_at(1) + f, t, window] = (
                        basis[slot_at(1) + f, t, window]
                        + basis[FIELDS + m, t, window] * seen
                        - shift * basis[f, t, window]
                    )
            return carry

        lax.fori_loop(0, RHS, one, 0)

    def repeat(packed):
        for width in (4, 8, 16, 32, 64):
            packed = packed + pltpu.roll(packed, width, 1)
        return packed

    def fill_wide_look():
        shape = (24, LANES)
        own = lanes_of(shape) // 4 == rows_of(shape)
        for r in range(RHS):
            for t in range(2):
                span = pl.ds(LANES * t, LANES)
                wide_look[r, t, CORE] = looks[r, pl.ds(0, TILE_ROWS), span]
                wide_look[r, t, pl.ds(6, 2)] = looks[r, pl.ds(16, 2), span]
                wide_look[r, t, pl.ds(24, 2)] = looks[r, pl.ds(18, 2), span]
            edge = repeat(jnp.where(own, looks[r, pl.ds(20, 1), pl.ds(0, LANES)], 0.0))
            wide_look[r, 2, pl.ds(4, 24)] = pltpu.roll(edge, LANES - 2, 1)

    def wide_ids():
        shape = (24, LANES)
        edge = pltpu.roll(stat[ID_FIELD, 2, pl.ds(4, 24)], 2, 1)
        edge = repeat(jnp.where(lanes_of(shape) < 4, edge, 0.0))
        edge = jnp.sum(jnp.where(lanes_of(shape) // 4 == rows_of(shape), edge, 0.0), axis=0, keepdims=True)
        lines = [jnp.concatenate([stat[ID_FIELD, t, pl.ds(i, 1)] for t in range(2)], axis=1) for i in (6, 7, 24, 25)]
        lines.append(jnp.concatenate([edge, edge], axis=1))
        for k, one in enumerate(lines):
            ids = one.astype(jnp.int32)
            hi_id[pl.ds(16 + k, 1), :] = ids // DLO
            lo_id[pl.ds(16 + k, 1), :] = lax.rem(ids, DLO)
        lax.fori_loop(TILE_ROWS, LINES, hot_line, 0)

    def advance(slot, look, shift):
        def one(r, carry):
            for t in range(2):
                seen = looks[look + r, pl.ds(0, TILE_ROWS), pl.ds(LANES * t, LANES)]
                for m in range(MONTHS):
                    f = r * MONTHS + m
                    basis[slot_at(slot + 1) + f, t, CORE] = (
                        image[f, t] + basis[FIELDS + m, t, CORE] * seen - shift * basis[slot_at(slot) + f, t, CORE]
                    )
            return carry

        lax.fori_loop(0, RHS, one, 0)

    for t in range(2):
        stat[15, t, CORE] = jnp.zeros((TILE_ROWS, LANES), F32)
    sum_in[...] = jnp.zeros_like(sum_in)
    for load in loads[:5]:
        load.wait()
    for t in range(2):
        stat[ID_FIELD, t, CORE] = id_ref[:, pl.ds(LANES * t, LANES)].astype(F32)
    halo_pack(0, stat, 0, 4)
    pl.semaphore_wait(barrier, group + chips - 2 + len(offsets))
    halo_stat = halo_copies(0, 4, 1)
    for copy in halo_stat:
        copy.start()

    for load in loads[5:]:
        load.wait()
    scale = (districts / grid_cells) ** 0.5
    ids = id_ref[...]
    hi_id[pl.ds(0, TILE_ROWS), :] = ids // DLO
    lo_id[pl.ds(0, TILE_ROWS), :] = lax.rem(ids, DLO)

    def hot_line(i, carry):
        same = lo_id[pl.ds(i, 1), :] == rows_of((DLO, 2 * LANES))
        hot[:, line_span(i)] = jnp.where(same, 1.0, 0.0).astype(jnp.bfloat16)
        return carry

    lax.fori_loop(0, TILE_ROWS, hot_line, 0)
    for t in range(2):
        span = pl.ds(LANES * t, LANES)
        live = active_ref[:, span].astype(F32)
        weight = live * climate_ref[:, span]
        crops = [crop_ref[c, :, span] for c in range(CROPS)]
        own = jnp.zeros((TILE_ROWS, LANES), F32)
        for c in range(CROPS):
            use = scale * use_ref[c] * live
            own = own + use * use * crops[c]
            wcs[c, t] = weight * weight * crops[c]
        cells[0, :, span] = own
        for m in range(MONTHS):
            square = jnp.zeros((TILE_ROWS, LANES), F32)
            mixed = jnp.zeros((TILE_ROWS, LANES), F32)
            for c in range(CROPS):
                drawn = wu_ref[c, m] * crops[c]
                square = square + wu_ref[c, m] * drawn
                mixed = mixed + use_ref[c] * drawn
            diag[m, t] = weight * weight * square + PROXIMAL
            cross[m, t] = weight * live * (scale * mixed)
    for r in range(RHS):
        for t in range(2):
            bdi[r, t] = jnp.zeros((DHI, LANES), F32)
            for hi in range(districts // DLO):
                at = LANES * (2 * hi + t)
                bdi[r, t, pl.ds(hi, 1)] = rdi_ref[pl.ds(r, 1), pl.ds(at, LANES)]

    for copy in halo_stat:
        copy.wait_recv()
    halo_unpack(0, stat, 0, 4)
    window = pl.ds(4, 24)
    faces = [[stat[k, t, window] for t in range(3)] for k in range(2)]
    east_side, west_side = beside(faces[0])
    for t in range(3):
        south_north = stat[1, t, pl.ds(3, 24)]
        coef[0, t] = faces[0][t]
        coef[1, t] = west_side[t]
        coef[2, t] = faces[1][t]
        coef[3, t] = south_north
        coef[4, t] = faces[0][t] + west_side[t] + faces[1][t] + south_north
    for k in range(5):
        for t in range(2):
            coefc[k, t] = coef[k, t, pl.ds(4, 16)]

    def month_diag(m, carry):
        for t in range(3):
            headw[m, t] = stat[2 + m, t, window]
        here = [stat[2 + m, t, CORE] for t in range(3)]
        e, w = beside(here)
        for t in range(2):
            fe, fw, fs, fn, total = [coefc[k, t] for k in range(5)]
            value = diag[m, t] + here[t] * total * total + fe * fe * e[t] + fw * fw * w[t]
            value = value + fs * fs * stat[2 + m, t, pl.ds(9, 16)] + fn * fn * stat[2 + m, t, pl.ds(7, 16)]
            diag[m, t] = value
            inverse = 1.0 / value
            dinv[m, t] = inverse
            basis[FIELDS + m, t, CORE] = cross[m, t] * inverse
        return carry

    lax.fori_loop(0, MONTHS, month_diag, 0)

    def start_basis(r, carry):
        for t in range(2):
            for m in range(MONTHS):
                f = r * MONTHS + m
                basis[f, t, CORE] = basis[f, t, CORE] * dinv[m, t]
        return carry

    lax.fori_loop(0, RHS, start_basis, 0)

    both = (FIELDS + MONTHS) // 4
    halo_pack(1, basis, 0, both)
    halo_first = halo_copies(1, both, 2)
    for copy in halo_first:
        copy.start()
    for t in range(2):
        total = jnp.zeros((TILE_ROWS, LANES), F32)
        for m in range(MONTHS):
            total += cross[m, t] * basis[FIELDS + m, t, CORE]
        cells[1, :, pl.ds(LANES * t, LANES)] = total
    cells_of(core_of(0), 2)
    to_district(0, 2 + RHS, 0)
    sum_scatter(0)

    wide_ids()
    for copy in halo_first:
        copy.wait_recv()
    halo_unpack(1, basis, 0, both)
    smooth(0, to_second)
    sum_spread(0)
    halo_pack(2, basis, slot_at(1), FIELDS // 4)
    halo_second = halo_copies(2, FIELDS // 4, 2)
    for copy in halo_second:
        copy.start()
    cells_of(core_of(1), 0)
    to_district(1, RHS, 0)
    sum_scatter(1)
    sum_gather(0)
    for copy in halo_second:
        copy.wait_recv()
    halo_unpack(2, basis, slot_at(1), FIELDS // 4)
    sum_done(0)

    def total_of(n, b):
        parts = [sum_out[(n,) + chunk(4 * b + k)] for k in range(4)]
        return jnp.stack([jnp.concatenate(parts[:2], axis=0), jnp.concatenate(parts[2:], axis=0)])

    diag_di[...] = total_of(0, 0) + PROXIMAL
    wide[...] = total_of(0, 1)
    for r in range(RHS):
        t0 = bdi[r] / diag_di[...]
        table[0, r] = t0
        table[1, r] = total_of(0, 2 + r) / diag_di[...] + (1 - SHIFTS[0]) * t0
    sum_spread(1)
    from_district(0, 2, 0, LINES)
    fill_wide_look()
    advance_wide(SHIFTS[0])
    sum_gather(1)
    smooth(1, to_image)
    advance(1, RHS, SHIFTS[1])
    halo_pack(3, basis, slot_at(2), FIELDS // 4)
    halo_third = halo_copies(3, FIELDS // 4, 2)
    for copy in halo_third:
        copy.start()
    cells_of(core_of(2), 0)
    to_district(2, RHS, 0)
    sum_done(1)
    for r in range(RHS):
        z1 = total_of(1, r) + wide[...] * table[0, r] - SHIFTS[0] * total_of(0, 2 + r)
        table[2, r] = z1 / diag_di[...] + (1 - SHIFTS[1]) * table[1, r]
    from_district(2, 1, 0)
    for copy in halo_third:
        copy.wait_recv()
    halo_unpack(3, basis, slot_at(2), FIELDS // 4)
    smooth(2, to_image)
    advance(2, 0, SHIFTS[2])
    halo_pack(4, basis, slot_at(3), FIELDS // 4)
    halo_fourth = halo_copies(4, FIELDS // 4, 2)
    for copy in halo_fourth:
        copy.start()
    cells_of(core_of(3), 0)
    to_district(2, RHS, RHS)
    sum_scatter(2)

    shape = (8, LANES)

    def inner_products(r, packed):
        totals = [jnp.zeros(shape, F32) for _ in PAIRS]
        for m in range(MONTHS):
            for t in range(2):
                values = [basis[slot_at(s) + r * MONTHS + m, t, CORE] for s in range(ITERS)]
                scaled = [diag[m, t] * v for v in values]
                for n, (i, j) in enumerate(PAIRS):
                    term = scaled[i] * values[j]
                    totals[n] = totals[n] + (term[:8] + term[8:])
        for n, total in enumerate(totals):
            here = (rows_of(shape) == r) & (lanes_of(shape) == n)
            packed = jnp.where(here, jnp.sum(total, keepdims=True), packed)
        return packed

    packed = lax.fori_loop(0, RHS, inner_products, jnp.zeros(shape, F32))
    for copy in halo_fourth:
        copy.wait_recv()
    halo_unpack(4, basis, slot_at(3), FIELDS // 4)

    def top_product(r, packed):
        total = jnp.zeros(shape, F32)
        base = slot_at(3) + r * MONTHS
        draws = [[jnp.zeros((TILE_ROWS, LANES), F32)] * CROPS for _ in range(2)]
        for m in range(MONTHS):
            here = [basis[base + m, t, CORE] for t in range(3)]
            e, w = beside(here)
            for t in range(2):
                lap = coefc[4, t] * here[t] - coefc[0, t] * e[t] - coefc[1, t] * w[t]
                lap = lap - coefc[2, t] * basis[base + m, t, pl.ds(9, 16)]
                lap = lap - coefc[3, t] * basis[base + m, t, pl.ds(7, 16)]
                term = stat[2 + m, t, CORE] * lap * lap + PROXIMAL * here[t] * here[t]
                total = total + (term[:8] + term[8:])
                draws[t] = [draws[t][c] + wu_ref[c, m] * here[t] for c in range(CROPS)]
        for t in range(2):
            for c in range(CROPS):
                term = wcs[c, t] * draws[t][c] * draws[t][c]
                total = total + (term[:8] + term[8:])
        here = (rows_of(shape) == r) & (lanes_of(shape) == len(PAIRS))
        return jnp.where(here, jnp.sum(total, keepdims=True), packed)

    late_in[...] = lax.fori_loop(0, RHS, top_product, packed)

    def late_first(k, carry):
        pltpu.make_async_remote_copy(
            src_ref=late_in,
            dst_ref=late_near.at[mine],
            send_sem=sum_send.at[3, 0],
            recv_sem=sum_recv.at[3, 0],
            device_id=peer(k)[1],
            device_id_type=MESH,
        ).start()
        return carry

    lax.fori_loop(1, group, late_first, 0)
    late_near[mine] = late_in[...]
    sum_spread(2)
    smooth(3, to_image)
    sum_gather(2)
    bytes_of(late_near.at[pl.ds(1, group - 1)], sum_recv.at[3, 0])
    late_z[chip] = jnp.sum(late_near[...], axis=0)

    def late_second(k, carry):
        pltpu.make_async_remote_copy(
            src_ref=late_z.at[chip],
            dst_ref=late_z.at[chip],
            send_sem=sum_send.at[3, 1],
            recv_sem=sum_recv.at[3, 1],
            device_id=stack(k),
            device_id_type=MESH,
        ).start()
        return carry

    lax.fori_loop(1, chips, late_second, 0)
    sum_done(2)
    for r in range(RHS):
        table[3, r] = total_of(2, r) / diag_di[...] + (1 - SHIFTS[2]) * table[2, r]
        table[4, r] = total_of(2, RHS + r) / diag_di[...] + (1 - SHIFTS[3]) * table[3, r]
    from_district(3, 1, 0)

    def district_part(i, j):
        out = jnp.zeros(shape, F32)
        for r in range(RHS):
            if j < ITERS:
                term = diag_di[...] * table[i, r] * table[j, r]
            else:
                term = table[3, r] * (2 * total_of(2, RHS + r) + diag_di[...] * table[3, r])
            line = jnp.sum(jnp.sum(term, axis=0), axis=0, keepdims=True)
            out = jnp.where(rows_of(shape) == r, line, out)
        return out

    parts = [district_part(i, j) for i, j in PAIRS + ((3, ITERS),)]
    bytes_of(late_z.at[pl.ds(1, chips - 1)], sum_recv.at[3, 1])
    totals = jnp.sum(late_z[...], axis=0)
    gram = [[None] * (ITERS + 1) for _ in range(ITERS + 1)]
    values = []
    for n, part in enumerate(parts):
        both = part + jnp.where(lanes_of(shape) == n, totals, 0.0)
        values.append(jnp.broadcast_to(jnp.sum(both, axis=1, keepdims=True), shape))
    for n, (i, j) in enumerate(PAIRS):
        gram[i][j] = gram[j][i] = values[n]
    for i in range(ITERS):
        ahead = values[-1] if i == ITERS - 1 else gram[i + 1][ITERS - 1] + SHIFTS[i] * gram[i][ITERS - 1]
        gram[i][ITERS] = ahead - SHIFTS[ITERS - 1] * gram[i][ITERS - 1]

    one, zero = jnp.ones(shape, F32), jnp.zeros(shape, F32)
    x, res, dirn = [zero] * ITERS, [one] + [zero] * ITERS, [one] + [zero] * (ITERS - 1)
    rho = gram[0][0]
    for it in range(ITERS):
        moved = [zero] * (ITERS + 1)
        for k in range(it + 1):
            moved[k + 1] = moved[k + 1] + dirn[k]
            moved[k] = moved[k] + SHIFTS[k] * dirn[k]
        curve = zero
        for i in range(it + 1):
            line = zero
            for j in range(it + 2):
                line = line + moved[j] * gram[i][j]
            curve = curve + dirn[i] * line
        alpha = rho / curve
        x = [x[i] + alpha * dirn[i] for i in range(ITERS)]
        res = [res[i] - alpha * moved[i] for i in range(ITERS + 1)]
        if it + 1 < ITERS:
            rho_new = zero
            for i in range(it + 2):
                line = zero
                for j in range(it + 2):
                    line = line + res[j] * gram[i][j]
                rho_new = rho_new + res[i] * line
            ratio = rho_new / rho
            rho = rho_new
            dirn = [res[i] + ratio * dirn[i] for i in range(ITERS)]
    for k, value in enumerate(x + res):
        factors[k] = value

    def finish(r, carry):
        xs = [factors[k, pl.ds(r, 1)] for k in range(ITERS)]
        rs = [factors[ITERS + k, pl.ds(r, 1)] for k in range(ITERS + 1)]
        for t in range(2):
            span = pl.ds(LANES * t, LANES)
            seen = looks[r, pl.ds(0, TILE_ROWS), span]
            for m in range(MONTHS):
                f = r * MONTHS + m
                vs = [basis[slot_at(s) + f, t, CORE] for s in range(ITERS)]
                vs.append(image[f, t] + basis[FIELDS + m, t, CORE] * seen - SHIFTS[3] * vs[3])
                dual_ref[f, :, span] = xs[0] * vs[0] + xs[1] * vs[1] + xs[2] * vs[2] + xs[3] * vs[3]
                total = rs[0] * vs[0]
                for k in range(1, ITERS + 1):
                    total = total + rs[k] * vs[k]
                res_ref[f, :, span] = diag[m, t] * total
        return carry

    lax.fori_loop(0, RHS, finish, 0)
    for r in range(RHS):
        xs = [factors[k, pl.ds(r, 1)] for k in range(ITERS)]
        rs = [factors[ITERS + k, pl.ds(r, 1)] for k in range(ITERS + 1)]
        for t in range(2):
            dual = xs[0] * table[0, r, t]
            total = rs[0] * table[0, r, t]
            for k in range(1, ITERS):
                dual = dual + xs[k] * table[k, r, t]
            for k in range(1, ITERS + 1):
                total = total + rs[k] * table[k, r, t]
            total = total * diag_di[t]
            for hi in range(districts // DLO):
                span = pl.ds(LANES * (2 * hi + t), LANES)
                dual_di_ref[pl.ds(r, 1), span] = dual[hi : hi + 1]
                res_di_ref[pl.ds(r, 1), span] = total[hi : hi + 1]

    for copies in (halo_stat, halo_first, halo_second, halo_third, halo_fourth):
        for copy in copies:
            copy.wait_send()
    for n in range(3):
        sum_drain(n)
    bytes_of(late_near.at[pl.ds(1, group - 1)], sum_send.at[3, 0])
    bytes_of(late_z.at[pl.ds(1, chips - 1)], sum_send.at[3, 1])


def body(
    right_aquifer,
    right_district,
    head_scale,
    crop_scale,
    conductance,
    water_use,
    climate,
    district_use,
    district_id,
    active,
):
    rows, cols = lax.axis_size("row"), lax.axis_size("col")
    group, chips = 2 * cols, rows // 2
    per = CHUNKS // group
    tile_rows, tile_cols = climate.shape
    grid_cells = tile_rows * rows * tile_cols * cols
    whole = pl.BlockSpec(memory_space=pltpu.VMEM)
    block = (FIELDS, tile_rows, tile_cols)
    vmem = lambda *shape: pltpu.VMEM(shape, F32)
    core = (2, TILE_ROWS, LANES)
    outs = pl.pallas_call(
        functools.partial(kernel, grid_cells),
        out_shape=(
            jax.ShapeDtypeStruct(block, F32),
            jax.ShapeDtypeStruct(right_district.shape, F32),
            jax.ShapeDtypeStruct(block, F32),
            jax.ShapeDtypeStruct(right_district.shape, F32),
        ),
        in_specs=[pl.BlockSpec(memory_space=pltpu.HBM)] * 10,
        out_specs=(whole,) * 4,
        scratch_shapes=[
            vmem(ITERS * FIELDS + MONTHS, 3, 32, LANES),
            vmem(FIELDS, *core),
            vmem(16, 3, 32, LANES),
            vmem(5, 3, 24, LANES),
            vmem(MONTHS, 3, 24, LANES),
            vmem(5, *core),
            vmem(MONTHS, *core),
            vmem(MONTHS, *core),
            vmem(MONTHS, *core),
            vmem(CROPS, *core),
            vmem(MONTHS, 3, 24, LANES),
            vmem(CROPS, *core),
            pltpu.VMEM((DLO, LINES * 2 * LANES), jnp.bfloat16),
            pltpu.VMEM((24, 2 * LANES), jnp.int32),
            pltpu.VMEM((24, 2 * LANES), jnp.int32),
            vmem(2 + RHS, TILE_ROWS, 2 * LANES),
            vmem(2 * RHS, 24, 2 * LANES),
            vmem(RHS, 3, 32, LANES),
            pltpu.VMEM((2 * (2 + RHS) * DHI, TILE_ROWS * 2 * LANES), jnp.bfloat16),
            vmem(*right_district.shape),
            vmem(*crop_scale.shape),
            vmem(*climate.shape),
            pltpu.VMEM(district_id.shape, jnp.int32),
            pltpu.VMEM(active.shape, jnp.int32),
            vmem(ITERS + 1, RHS, 2, DHI, LANES),
            vmem(2, DHI, LANES),
            vmem(2, DHI, LANES),
            vmem(RHS, 2, DHI, LANES),
            vmem(3, group, 8 * per, LANES),
            vmem(3, group, 8 * per, LANES),
            vmem(3, chips, 8 * per, LANES),
            vmem(3, group, 8 * per, LANES),
            vmem(group, 8, LANES),
            vmem(chips, 8, LANES),
            vmem(8, LANES),
            vmem(2 * ITERS + 1, 8, LANES),
            vmem(5, 2, 15, 2, 8, LANES),
            vmem(5, 2, 15, 2, 8, LANES),
            vmem(5, 2, TILE_ROWS, LANES),
            vmem(5, 2, 2, 32, LANES),
            pltpu.SemaphoreType.DMA((5, 8)),
            pltpu.SemaphoreType.DMA((5, 8)),
            pltpu.SemaphoreType.DMA((4, 3)),
            pltpu.SemaphoreType.DMA((4, 3)),
            pltpu.SemaphoreType.DMA((13,)),
            pltpu.SMEM(water_use.shape[::-1], F32),
            pltpu.SMEM(district_use.shape, F32),
        ],
        compiler_params=pltpu.CompilerParams(
            collective_id=0, has_side_effects=True, vmem_limit_bytes=48 * 1024 * 1024
        ),
    )(
        *(
            pltpu.with_memory_space_constraint(value, pltpu.HBM)
            for value in (
                right_aquifer.reshape(block),
                right_district,
                head_scale,
                crop_scale,
                conductance,
                climate,
                district_id,
                active,
                water_use.T,
                district_use,
            )
        )
    )
    dual, dual_di, res, res_di = outs
    return dual.reshape(right_aquifer.shape), dual_di, res.reshape(right_aquifer.shape), res_di


def solution(mesh):
    placed = (
        P(None, None, "row", "col"),
        P(),
        P(None, "row", "col"),
        P(None, "row", "col"),
        P(None, "row", "col"),
        P(),
        P("row", "col"),
        P(),
        P("row", "col"),
        P("row", "col"),
    )
    return jax.shard_map(
        body,
        mesh=mesh,
        in_specs=placed,
        out_specs=(P(None, None, "row", "col"), P(), P(None, None, "row", "col"), P()),
        check_vma=False,
    )
```

```python
import functools

import jax
import jax.numpy as jnp
from jax import lax
from jax.experimental import pallas as pl
from jax.experimental.pallas import tpu as pltpu
from jax.sharding import PartitionSpec as P

ITERS = 4
RHS = 4
MONTHS = 12
CROPS = 6
FIELDS = RHS * MONTHS
DHI = 16
DLO = 256
LANES = 128
TILE_ROWS = 16
CHUNKS = 32
LINES = 21
ID_FIELD = 14
PROXIMAL = 0.05
SHIFTS = (0.5, 8.0, 3.0, 1.0)
PAIRS = tuple((i, j) for i in range(ITERS) for j in range(i, ITERS))
MESH = pl.DeviceIdType.MESH
F32 = jnp.float32
CORE = pl.ds(8, 16)


def lanes_of(shape):
    return lax.broadcasted_iota(jnp.int32, shape, len(shape) - 1)


def rows_of(shape):
    return lax.broadcasted_iota(jnp.int32, shape, len(shape) - 2)


def beside(tiles):
    axis = tiles[0].ndim - 1
    lane = lanes_of(tiles[0].shape)
    ahead = [pltpu.roll(t, LANES - 1, axis) for t in tiles]
    behind = [pltpu.roll(t, 1, axis) for t in tiles]
    east = [jnp.where(lane == LANES - 1, ahead[(n + 1) % 3], ahead[n]) for n in range(3)]
    west = [jnp.where(lane == 0, behind[(n + 2) % 3], behind[n]) for n in range(3)]
    return east, west


def kernel(
    grid_cells,
    rhs_hbm,
    rdi_hbm,
    head_hbm,
    crop_hbm,
    cond_hbm,
    climate_hbm,
    id_hbm,
    active_hbm,
    wu_hbm,
    use_hbm,
    dual_ref,
    dual_di_ref,
    res_ref,
    res_di_ref,
    basis,
    image,
    stat,
    coef,
    headw,
    coefc,
    diag,
    dinv,
    cross,
    wcs,
    inner,
    hot,
    lo_id,
    hi_id,
    cells,
    looks,
    wide_look,
    spread,
    rdi_ref,
    crop_ref,
    climate_ref,
    id_ref,
    active_ref,
    table,
    diag_di,
    wide,
    bdi,
    sum_in,
    sum_near,
    sum_z,
    sum_out,
    late_near,
    late_z,
    late_in,
    factors,
    row_out,
    row_in,
    col_out,
    col_in,
    xch_send,
    xch_recv,
    sum_send,
    sum_recv,
    load_sem,
    wu_ref,
    use_ref,
):
    rows, cols = lax.axis_size("row"), lax.axis_size("col")
    chips, group = rows // 2, 2 * cols
    per = CHUNKS // group
    row, col = lax.axis_index("row"), lax.axis_index("col")
    chip, core = row // 2, lax.rem(row, 2)
    mine = core * cols + col
    districts = rdi_ref.shape[1]

    def slot_at(slot):
        return slot * FIELDS + (MONTHS if slot else 0)


    def peer(k):
        other = lax.rem(mine + k, group)
        return other, (chip * 2 + other // cols, lax.rem(other, cols))

    def stack(k):
        return (lax.rem(row + 2 * k, rows), col)

    def around(dr, dc):
        return (lax.rem(row + dr + rows, rows), lax.rem(col + dc + cols, cols))

    loads = []
    for t in range(2):
        span = pl.ds(LANES * t, LANES)
        loads.append((cond_hbm.at[:, :, span], stat.at[pl.ds(0, 2), t, CORE]))
        loads.append((head_hbm.at[:, :, span], stat.at[pl.ds(2, MONTHS), t, CORE]))
    loads += [(id_hbm, id_ref), (climate_hbm, climate_ref), (active_hbm, active_ref)]
    loads += [(wu_hbm, wu_ref), (use_hbm, use_ref), (crop_hbm, crop_ref), (rdi_hbm, rdi_ref)]
    for t in range(2):
        loads.append((rhs_hbm.at[:, :, pl.ds(LANES * t, LANES)], basis.at[pl.ds(0, FIELDS), t, CORE]))
    loads = [pltpu.make_async_copy(src, dst, load_sem.at[k]) for k, (src, dst) in enumerate(loads)]
    for load in loads:
        load.start()

    barrier = pltpu.get_barrier_semaphore()

    def greet(k, carry):
        pl.semaphore_signal(barrier, inc=1, device_id=peer(k)[1], device_id_type=MESH)
        return carry

    def greet_stack(k, carry):
        pl.semaphore_signal(barrier, inc=1, device_id=stack(k), device_id_type=MESH)
        return carry

    lax.fori_loop(1, group, greet, 0)
    lax.fori_loop(1, chips, greet_stack, 0)
    offsets = [(dr, dc) for dr in (-1, 0, 1) for dc in (-1, 0, 1) if dr or dc]
    for dr, dc in offsets:
        pl.semaphore_signal(barrier, inc=1, device_id=around(dr, dc), device_id_type=MESH)

    north = jnp.where(row > 0, 1.0, 0.0).astype(F32)
    south = jnp.where(row < rows - 1, 1.0, 0.0).astype(F32)
    west = jnp.where(col > 0, 1.0, 0.0).astype(F32)
    east = jnp.where(col < cols - 1, 1.0, 0.0).astype(F32)

    def halo_copies(n, quads, groups):
        ahead, back = pl.ds(8, 8), pl.ds(0, 8)
        plan = [
            (row_out.at[n, 0, pl.ds(0, quads)], row_in.at[n, 0, pl.ds(0, quads)], (1, 0)),
            (row_out.at[n, 1, pl.ds(0, quads)], row_in.at[n, 1, pl.ds(0, quads)], (-1, 0)),
            (col_out.at[n, pl.ds(0, groups)], col_in.at[n, 0, pl.ds(0, groups), CORE], (0, 1)),
            (col_out.at[n, pl.ds(0, groups)], col_in.at[n, 1, pl.ds(0, groups), CORE], (0, -1)),
            (col_out.at[n, pl.ds(0, groups), ahead], col_in.at[n, 0, pl.ds(0, groups), pl.ds(0, 8)], (1, 1)),
            (col_out.at[n, pl.ds(0, groups), ahead], col_in.at[n, 1, pl.ds(0, groups), pl.ds(0, 8)], (1, -1)),
            (col_out.at[n, pl.ds(0, groups), back], col_in.at[n, 0, pl.ds(0, groups), pl.ds(24, 8)], (-1, 1)),
            (col_out.at[n, pl.ds(0, groups), back], col_in.at[n, 1, pl.ds(0, groups), pl.ds(24, 8)], (-1, -1)),
        ]
        return [
            pltpu.make_async_remote_copy(
                src_ref=src,
                dst_ref=dst,
                send_sem=xch_send.at[n, k],
                recv_sem=xch_recv.at[n, k],
                device_id=around(*to),
                device_id_type=MESH,
            )
            for k, (src, dst, to) in enumerate(plan)
        ]

    def halo_pack(n, ref, base, quads):
        lane = lanes_of((TILE_ROWS, LANES))

        def cols_of(f, packed, slot):
            both = jnp.where(lane < 64, ref[base + f, 0, CORE], ref[base + f, 1, CORE])
            moved = pltpu.roll(both, lax.rem(4 * slot + 2, LANES), 1)
            return jnp.where(lane // 4 == slot, moved, packed)

        for g in range((quads + 7) // 8):
            count = min(32, 4 * quads - 32 * g)

            def quad(k, packed):
                for u in range(4):
                    packed = cols_of(32 * g + 4 * k + u, packed, 4 * k + u)
                return packed

            col_out[n, g] = lax.fori_loop(0, count // 4, quad, jnp.zeros((TILE_ROWS, LANES), F32), unroll=count // 4)

        def rows_quad(k, carry):
            for u in range(4):
                field = ref.at[base + 4 * k + u]
                for t in range(2):
                    row_out[n, 0, k, t, pl.ds(2 * u, 2)] = field[t, pl.ds(22, 2)]
                    row_out[n, 1, k, t, pl.ds(2 * u, 2)] = field[t, pl.ds(8, 2)]
            return carry

        lax.fori_loop(0, quads, rows_quad, 0, unroll=quads // 4 if quads % 4 == 0 else 5)

    def halo_unpack(n, ref, base, quads):
        shape = (32, LANES)
        lane, place = lanes_of(shape), rows_of(shape)
        side = jnp.where(lax.rem(lane, 4) < 2, west, east)
        side = side * jnp.where(place < 8, north, jnp.where(place >= 24, south, 1.0))
        for g in range((quads + 7) // 8):
            count = min(32, 4 * quads - 32 * g)
            packed = jnp.where(lax.rem(lane, 4) < 2, col_in[n, 0, g], col_in[n, 1, g]) * side

            def quad(k, carry):
                for u in range(4):
                    slot = 4 * k + u
                    moved = pltpu.roll(packed, lax.rem(2 * LANES - 4 * slot - 2, LANES), 1)
                    ref[base + 32 * g + slot, 2] = moved
                return carry

            lax.fori_loop(0, count // 4, quad, 0, unroll=count // 4)

        def rows_quad(k, carry):
            for u in range(4):
                for t in range(2):
                    ref[base + 4 * k + u, t, pl.ds(6, 2)] = row_in[n, 0, k, t, pl.ds(2 * u, 2)] * north
                    ref[base + 4 * k + u, t, pl.ds(24, 2)] = row_in[n, 1, k, t, pl.ds(2 * u, 2)] * south
            return carry

        lax.fori_loop(0, quads, rows_quad, 0, unroll=quads // 4 if quads % 4 == 0 else 5)

    def bytes_of(ref, sem):
        pltpu.make_async_copy(ref, ref, sem).wait()

    def sum_scatter(n):
        def scatter(k, carry):
            other, device = peer(k)
            pltpu.make_async_remote_copy(
                src_ref=sum_in.at[n, other],
                dst_ref=sum_near.at[n, k],
                send_sem=sum_send.at[n, 0],
                recv_sem=sum_recv.at[n, 0],
                device_id=device,
                device_id_type=MESH,
            ).start()
            return carry

        lax.fori_loop(1, group, scatter, 0)
        sum_near[n, 0] = sum_in[n, mine]

    def sum_spread(n):
        bytes_of(sum_near.at[n, pl.ds(1, group - 1)], sum_recv.at[n, 0])
        sum_z[n, chip] = jnp.sum(sum_near[n], axis=0)

        def spread(k, carry):
            pltpu.make_async_remote_copy(
                src_ref=sum_z.at[n, chip],
                dst_ref=sum_z.at[n, chip],
                send_sem=sum_send.at[n, 1],
                recv_sem=sum_recv.at[n, 1],
                device_id=stack(k),
                device_id_type=MESH,
            ).start()
            return carry

        lax.fori_loop(1, chips, spread, 0)

    def sum_gather(n):
        bytes_of(sum_z.at[n, pl.ds(1, chips - 1)], sum_recv.at[n, 1])
        sum_out[n, mine] = jnp.sum(sum_z[n], axis=0)

        def gather(k, carry):
            pltpu.make_async_remote_copy(
                src_ref=sum_out.at[n, mine],
                dst_ref=sum_out.at[n, mine],
                send_sem=sum_send.at[n, 2],
                recv_sem=sum_recv.at[n, 2],
                device_id=peer(k)[1],
                device_id_type=MESH,
            ).start()
            return carry

        lax.fori_loop(1, group, gather, 0)

    def sum_done(n):
        bytes_of(sum_near.at[n, pl.ds(1, group - 1)], sum_recv.at[n, 2])

    def sum_drain(n):
        bytes_of(sum_near.at[n, pl.ds(1, group - 1)], sum_send.at[n, 0])
        bytes_of(sum_z.at[n, pl.ds(1, chips - 1)], sum_send.at[n, 1])
        bytes_of(sum_near.at[n, pl.ds(1, group - 1)], sum_send.at[n, 2])

    def chunk(k):
        return k // per, pl.ds(8 * (k % per), 8)

    def line_span(i):
        return pl.ds(pl.multiple_of(i * (2 * LANES), 2 * LANES), 2 * LANES)

    def to_district(n, count, first):
        size = count * DHI

        def line(i, carry):
            value = cells[pl.ds(0, count), pl.ds(i, 1), :]
            high = value.astype(jnp.bfloat16).astype(F32)
            here = (hi_id[pl.ds(i, 1), :] == rows_of((DHI, 2 * LANES)))[None]
            for k, part in enumerate((high, value - high)):
                part = jnp.where(here, jnp.broadcast_to(part, (count, DHI, 2 * LANES)), 0.0)
                spread[pl.ds(k * size, size), line_span(i)] = part.reshape(size, 2 * LANES).astype(jnp.bfloat16)
            return carry

        lax.fori_loop(0, TILE_ROWS, line, 0, unroll=2)
        total = lax.dot_general(
            hot[:, pl.ds(0, TILE_ROWS * 2 * LANES)], spread[pl.ds(0, 2 * size), :], (((1,), (1,)), ((), ())), preferred_element_type=F32
        ).T
        total = total[:size] + total[size:]
        for b in range(count):
            for t in range(2):
                for h in range(2):
                    at, part = chunk(4 * (first + b) + 2 * t + h)
                    sum_in[n, at, part] = total[DHI * b + 8 * h : DHI * b + 8 * h + 8, LANES * t : LANES * (t + 1)]

    def from_district(slot, count, first, lines=TILE_ROWS):
        size = count * RHS * DHI
        values = jnp.concatenate(
            [
                jnp.concatenate([table[slot + s, r, t] for t in range(2)], axis=1)
                for s in range(count)
                for r in range(RHS)
            ],
            axis=0,
        )
        high = values.astype(jnp.bfloat16).astype(F32)
        both = jnp.concatenate([high, values - high], axis=0).astype(jnp.bfloat16)

        def line(i, carry):
            picked = jnp.dot(both, hot[:, line_span(i)], preferred_element_type=F32)
            picked = (picked[:size] + picked[size:]).reshape(count * RHS, DHI, 2 * LANES)
            here = (hi_id[pl.ds(i, 1), :] == rows_of((DHI, 2 * LANES)))[None]
            picked = jnp.where(here, picked, 0.0)
            looks[pl.ds(first, count * RHS), pl.ds(i, 1), :] = jnp.sum(picked, axis=1, keepdims=True)
            return carry

        lax.fori_loop(0, lines, line, 0, unroll=3 if lines % 3 == 0 else 2)

    def cells_of(load, first):
        def one(r, carry):
            for t in range(2):
                total = jnp.zeros((TILE_ROWS, LANES), F32)
                for m in range(MONTHS):
                    total += cross[m, t] * load(r * MONTHS + m, t)
                cells[first + r, :, pl.ds(LANES * t, LANES)] = total
            return carry

        lax.fori_loop(0, RHS, one, 0)

    def core_of(slot):
        return lambda f, t: basis[slot_at(slot) + f, t, CORE]

    def smooth(slot, put):
        def one(r, carry):
            base = slot_at(slot) + r * MONTHS
            for k in range(3):
                part, place = pl.ds(8 * k, 8), pl.ds(4 + 8 * k, 8)
                face = [[coef[j, t, part] for t in range(3)] for j in range(5)]
                for m in range(MONTHS):
                    here = [basis[base + m, t, place] for t in range(3)]
                    e, w = beside(here)
                    for t in range(3):
                        lap = face[4][t] * here[t] - face[0][t] * e[t] - face[1][t] * w[t]
                        lap = lap - face[2][t] * basis[base + m, t, pl.ds(5 + 8 * k, 8)]
                        lap = lap - face[3][t] * basis[base + m, t, pl.ds(3 + 8 * k, 8)]
                        inner[m, t, part] = headw[m, t, part] * lap
            for k in range(2):
                part, place = pl.ds(8 * k, 8), pl.ds(8 + 8 * k, 8)
                draws = [[jnp.zeros((8, LANES), F32)] * CROPS for _ in range(2)]
                for m in range(MONTHS):
                    value = [basis[base + m, t, place] for t in range(2)]
                    for c in range(CROPS):
                        for t in range(2):
                            draws[t][c] = draws[t][c] + wu_ref[c, m] * value[t]
                draws = [[wcs[c, t, part] * draws[t][c] for c in range(CROPS)] for t in range(2)]
                face = [[coefc[j, t, part] for t in range(2)] for j in range(5)]
                for m in range(MONTHS):
                    here = [inner[m, t, pl.ds(4 + 8 * k, 8)] for t in range(3)]
                    e, w = beside(here)
                    for t in range(2):
                        own = basis[base + m, t, place]
                        lap = face[4][t] * here[t] - face[0][t] * e[t] - face[1][t] * w[t]
                        lap = lap - face[2][t] * inner[m, t, pl.ds(5 + 8 * k, 8)]
                        lap = lap - face[3][t] * inner[m, t, pl.ds(3 + 8 * k, 8)]
                        total = lap + PROXIMAL * own
                        for c in range(CROPS):
                            total = total + wu_ref[c, m] * draws[t][c]
                        put(r, m, t, k, dinv[m, t, part] * total, own)
            return carry

        lax.fori_loop(0, RHS, one, 0)

    def to_image(r, m, t, k, value, own):
        image[r * MONTHS + m, t, pl.ds(8 * k, 8)] = value

    def to_second(r, m, t, k, value, own):
        basis[slot_at(1) + r * MONTHS + m, t, pl.ds(8 + 8 * k, 8)] = value

    def to_next(slot, look, shift):
        def put(r, m, t, k, value, own):
            place = pl.ds(8 + 8 * k, 8)
            seen = looks[look + r, pl.ds(8 * k, 8), pl.ds(LANES * t, LANES)]
            value = value + basis[FIELDS + m, t, place] * seen - shift * own
            basis[slot_at(slot + 1) + r * MONTHS + m, t, place] = value

        return put

    def advance_wide(shift):
        window = pl.ds(4, 24)

        def one(r, carry):
            for t in range(3):
                seen = wide_look[r, t, window]
                for m in range(MONTHS):
                    f = r * MONTHS + m
                    basis[slot_at(1) + f, t, window] = (
                        basis[slot_at(1) + f, t, window]
                        + basis[FIELDS + m, t, window] * seen
                        - shift * basis[f, t, window]
                    )
            return carry

        lax.fori_loop(0, RHS, one, 0)

    def repeat(packed):
        for width in (4, 8, 16, 32, 64):
            packed = packed + pltpu.roll(packed, width, 1)
        return packed

    def fill_wide_look():
        shape = (24, LANES)
        own = lanes_of(shape) // 4 == rows_of(shape)
        for r in range(RHS):
            for t in range(2):
                span = pl.ds(LANES * t, LANES)
                wide_look[r, t, CORE] = looks[r, pl.ds(0, TILE_ROWS), span]
                wide_look[r, t, pl.ds(6, 2)] = looks[r, pl.ds(16, 2), span]
                wide_look[r, t, pl.ds(24, 2)] = looks[r, pl.ds(18, 2), span]
            edge = repeat(jnp.where(own, looks[r, pl.ds(20, 1), pl.ds(0, LANES)], 0.0))
            wide_look[r, 2, pl.ds(4, 24)] = pltpu.roll(edge, LANES - 2, 1)

    def wide_ids():
        shape = (24, LANES)
        edge = pltpu.roll(stat[ID_FIELD, 2, pl.ds(4, 24)], 2, 1)
        edge = repeat(jnp.where(lanes_of(shape) < 4, edge, 0.0))
        edge = jnp.sum(jnp.where(lanes_of(shape) // 4 == rows_of(shape), edge, 0.0), axis=0, keepdims=True)
        lines = [jnp.concatenate([stat[ID_FIELD, t, pl.ds(i, 1)] for t in range(2)], axis=1) for i in (6, 7, 24, 25)]
        lines.append(jnp.concatenate([edge, edge], axis=1))
        for k, one in enumerate(lines):
            ids = one.astype(jnp.int32)
            hi_id[pl.ds(16 + k, 1), :] = ids // DLO
            lo_id[pl.ds(16 + k, 1), :] = lax.rem(ids, DLO)
        lax.fori_loop(TILE_ROWS, LINES, hot_line, 0)

    for t in range(2):
        stat[15, t, CORE] = jnp.zeros((TILE_ROWS, LANES), F32)
    sum_in[...] = jnp.zeros_like(sum_in)
    for load in loads[:5]:
        load.wait()
    for t in range(2):
        stat[ID_FIELD, t, CORE] = id_ref[:, pl.ds(LANES * t, LANES)].astype(F32)
    halo_pack(0, stat, 0, 4)
    for load in loads[5:]:
        load.wait()
    scale = (districts / grid_cells) ** 0.5
    ids = id_ref[...]
    hi_id[pl.ds(0, TILE_ROWS), :] = ids // DLO
    lo_id[pl.ds(0, TILE_ROWS), :] = lax.rem(ids, DLO)

    def hot_line(i, carry):
        same = lo_id[pl.ds(i, 1), :] == rows_of((DLO, 2 * LANES))
        hot[:, line_span(i)] = jnp.where(same, 1.0, 0.0).astype(jnp.bfloat16)
        return carry

    lax.fori_loop(0, TILE_ROWS, hot_line, 0)
    for t in range(2):
        span = pl.ds(LANES * t, LANES)
        live = active_ref[:, span].astype(F32)
        weight = live * climate_ref[:, span]
        crops = [crop_ref[c, :, span] for c in range(CROPS)]
        own = jnp.zeros((TILE_ROWS, LANES), F32)
        for c in range(CROPS):
            use = scale * use_ref[c] * live
            own = own + use * use * crops[c]
            wcs[c, t] = weight * weight * crops[c]
        cells[0, :, span] = own
        for m in range(MONTHS):
            square = jnp.zeros((TILE_ROWS, LANES), F32)
            mixed = jnp.zeros((TILE_ROWS, LANES), F32)
            for c in range(CROPS):
                drawn = wu_ref[c, m] * crops[c]
                square = square + wu_ref[c, m] * drawn
                mixed = mixed + use_ref[c] * drawn
            diag[m, t] = weight * weight * square + PROXIMAL
            cross[m, t] = weight * live * (scale * mixed)
    for r in range(RHS):
        for t in range(2):
            bdi[r, t] = jnp.zeros((DHI, LANES), F32)
            for hi in range(districts // DLO):
                at = LANES * (2 * hi + t)
                bdi[r, t, pl.ds(hi, 1)] = rdi_ref[pl.ds(r, 1), pl.ds(at, LANES)]

    pl.semaphore_wait(barrier, group + chips - 2 + len(offsets))
    halo_stat = halo_copies(0, 4, 1)
    for copy in halo_stat:
        copy.start()

    for copy in halo_stat:
        copy.wait_recv()
    halo_unpack(0, stat, 0, 4)
    window = pl.ds(4, 24)
    faces = [[stat[k, t, window] for t in range(3)] for k in range(2)]
    east_side, west_side = beside(faces[0])
    for t in range(3):
        south_north = stat[1, t, pl.ds(3, 24)]
        coef[0, t] = faces[0][t]
        coef[1, t] = west_side[t]
        coef[2, t] = faces[1][t]
        coef[3, t] = south_north
        coef[4, t] = faces[0][t] + west_side[t] + faces[1][t] + south_north
    for k in range(5):
        for t in range(2):
            coefc[k, t] = coef[k, t, pl.ds(4, 16)]

    def month_diag(m, carry):
        for t in range(3):
            headw[m, t] = stat[2 + m, t, window]
        here = [stat[2 + m, t, CORE] for t in range(3)]
        e, w = beside(here)
        for t in range(2):
            fe, fw, fs, fn, total = [coefc[k, t] for k in range(5)]
            value = diag[m, t] + here[t] * total * total + fe * fe * e[t] + fw * fw * w[t]
            value = value + fs * fs * stat[2 + m, t, pl.ds(9, 16)] + fn * fn * stat[2 + m, t, pl.ds(7, 16)]
            diag[m, t] = value
            inverse = 1.0 / value
            dinv[m, t] = inverse
            basis[FIELDS + m, t, CORE] = cross[m, t] * inverse
        return carry

    lax.fori_loop(0, MONTHS, month_diag, 0)

    def start_basis(r, carry):
        for t in range(2):
            for m in range(MONTHS):
                f = r * MONTHS + m
                basis[f, t, CORE] = basis[f, t, CORE] * dinv[m, t]
        return carry

    lax.fori_loop(0, RHS, start_basis, 0)

    both = (FIELDS + MONTHS) // 4
    halo_pack(1, basis, 0, both)
    halo_first = halo_copies(1, both, 2)
    for copy in halo_first:
        copy.start()
    for t in range(2):
        total = jnp.zeros((TILE_ROWS, LANES), F32)
        for m in range(MONTHS):
            total += cross[m, t] * basis[FIELDS + m, t, CORE]
        cells[1, :, pl.ds(LANES * t, LANES)] = total
    cells_of(core_of(0), 2)
    to_district(0, 2 + RHS, 0)
    sum_scatter(0)

    wide_ids()
    sum_spread(0)
    for copy in halo_first:
        copy.wait_recv()
    halo_unpack(1, basis, 0, both)
    smooth(0, to_second)
    halo_pack(2, basis, slot_at(1), FIELDS // 4)
    halo_second = halo_copies(2, FIELDS // 4, 2)
    for copy in halo_second:
        copy.start()
    sum_gather(0)
    cells_of(core_of(1), 0)
    to_district(1, RHS, 0)
    sum_scatter(1)
    sum_done(0)

    def total_of(n, b):
        parts = [sum_out[(n,) + chunk(4 * b + k)] for k in range(4)]
        return jnp.stack([jnp.concatenate(parts[:2], axis=0), jnp.concatenate(parts[2:], axis=0)])

    diag_di[...] = total_of(0, 0) + PROXIMAL
    wide[...] = total_of(0, 1)
    for r in range(RHS):
        t0 = bdi[r] / diag_di[...]
        table[0, r] = t0
        table[1, r] = total_of(0, 2 + r) / diag_di[...] + (1 - SHIFTS[0]) * t0
    from_district(0, 2, 0, LINES)
    fill_wide_look()
    for copy in halo_second:
        copy.wait_recv()
    halo_unpack(2, basis, slot_at(1), FIELDS // 4)
    sum_spread(1)
    advance_wide(SHIFTS[0])
    smooth(1, to_next(1, RHS, SHIFTS[1]))
    halo_pack(3, basis, slot_at(2), FIELDS // 4)
    halo_third = halo_copies(3, FIELDS // 4, 2)
    for copy in halo_third:
        copy.start()
    sum_gather(1)
    cells_of(core_of(2), 0)
    to_district(2, RHS, 0)
    sum_done(1)
    for r in range(RHS):
        z1 = total_of(1, r) + wide[...] * table[0, r] - SHIFTS[0] * total_of(0, 2 + r)
        table[2, r] = z1 / diag_di[...] + (1 - SHIFTS[1]) * table[1, r]
    from_district(2, 1, 0)
    for copy in halo_third:
        copy.wait_recv()
    halo_unpack(3, basis, slot_at(2), FIELDS // 4)
    smooth(2, to_next(2, 0, SHIFTS[2]))
    halo_pack(4, basis, slot_at(3), FIELDS // 4)
    halo_fourth = halo_copies(4, FIELDS // 4, 2)
    for copy in halo_fourth:
        copy.start()
    cells_of(core_of(3), 0)
    to_district(2, RHS, RHS)
    sum_scatter(2)

    shape = (8, LANES)

    def inner_products(r, packed):
        totals = [jnp.zeros(shape, F32) for _ in PAIRS]
        for m in range(MONTHS):
            for t in range(2):
                values = [basis[slot_at(s) + r * MONTHS + m, t, CORE] for s in range(ITERS)]
                scaled = [diag[m, t] * v for v in values]
                for n, (i, j) in enumerate(PAIRS):
                    term = scaled[i] * values[j]
                    totals[n] = totals[n] + (term[:8] + term[8:])
        for n, total in enumerate(totals):
            here = (rows_of(shape) == r) & (lanes_of(shape) == n)
            packed = jnp.where(here, jnp.sum(total, keepdims=True), packed)
        return packed

    packed = lax.fori_loop(0, RHS, inner_products, jnp.zeros(shape, F32))
    sum_spread(2)
    for copy in halo_fourth:
        copy.wait_recv()
    halo_unpack(4, basis, slot_at(3), FIELDS // 4)

    def top_product(r, packed):
        total = jnp.zeros(shape, F32)
        base = slot_at(3) + r * MONTHS
        draws = [[jnp.zeros((TILE_ROWS, LANES), F32)] * CROPS for _ in range(2)]
        for m in range(MONTHS):
            here = [basis[base + m, t, CORE] for t in range(3)]
            e, w = beside(here)
            for t in range(2):
                lap = coefc[4, t] * here[t] - coefc[0, t] * e[t] - coefc[1, t] * w[t]
                lap = lap - coefc[2, t] * basis[base + m, t, pl.ds(9, 16)]
                lap = lap - coefc[3, t] * basis[base + m, t, pl.ds(7, 16)]
                term = stat[2 + m, t, CORE] * lap * lap + PROXIMAL * here[t] * here[t]
                total = total + (term[:8] + term[8:])
                draws[t] = [draws[t][c] + wu_ref[c, m] * here[t] for c in range(CROPS)]
        for t in range(2):
            for c in range(CROPS):
                term = wcs[c, t] * draws[t][c] * draws[t][c]
                total = total + (term[:8] + term[8:])
        here = (rows_of(shape) == r) & (lanes_of(shape) == len(PAIRS))
        return jnp.where(here, jnp.sum(total, keepdims=True), packed)

    late_in[...] = lax.fori_loop(0, RHS, top_product, packed)

    def late_first(k, carry):
        pltpu.make_async_remote_copy(
            src_ref=late_in,
            dst_ref=late_near.at[mine],
            send_sem=sum_send.at[3, 0],
            recv_sem=sum_recv.at[3, 0],
            device_id=peer(k)[1],
            device_id_type=MESH,
        ).start()
        return carry

    lax.fori_loop(1, group, late_first, 0)
    late_near[mine] = late_in[...]
    smooth(3, to_image)
    sum_gather(2)
    bytes_of(late_near.at[pl.ds(1, group - 1)], sum_recv.at[3, 0])
    late_z[chip] = jnp.sum(late_near[...], axis=0)

    def late_second(k, carry):
        pltpu.make_async_remote_copy(
            src_ref=late_z.at[chip],
            dst_ref=late_z.at[chip],
            send_sem=sum_send.at[3, 1],
            recv_sem=sum_recv.at[3, 1],
            device_id=stack(k),
            device_id_type=MESH,
        ).start()
        return carry

    lax.fori_loop(1, chips, late_second, 0)
    sum_done(2)
    for r in range(RHS):
        table[3, r] = total_of(2, r) / diag_di[...] + (1 - SHIFTS[2]) * table[2, r]
        table[4, r] = total_of(2, RHS + r) / diag_di[...] + (1 - SHIFTS[3]) * table[3, r]
    from_district(3, 1, 0)

    def district_part(i, j):
        out = jnp.zeros(shape, F32)
        for r in range(RHS):
            if j < ITERS:
                term = diag_di[...] * table[i, r] * table[j, r]
            else:
                term = table[3, r] * (2 * total_of(2, RHS + r) + diag_di[...] * table[3, r])
            line = jnp.sum(jnp.sum(term, axis=0), axis=0, keepdims=True)
            out = jnp.where(rows_of(shape) == r, line, out)
        return out

    parts = [district_part(i, j) for i, j in PAIRS + ((3, ITERS),)]
    bytes_of(late_z.at[pl.ds(1, chips - 1)], sum_recv.at[3, 1])
    totals = jnp.sum(late_z[...], axis=0)
    gram = [[None] * (ITERS + 1) for _ in range(ITERS + 1)]
    values = []
    for n, part in enumerate(parts):
        both = part + jnp.where(lanes_of(shape) == n, totals, 0.0)
        values.append(jnp.broadcast_to(jnp.sum(both, axis=1, keepdims=True), shape))
    for n, (i, j) in enumerate(PAIRS):
        gram[i][j] = gram[j][i] = values[n]
    for i in range(ITERS):
        ahead = values[-1] if i == ITERS - 1 else gram[i + 1][ITERS - 1] + SHIFTS[i] * gram[i][ITERS - 1]
        gram[i][ITERS] = ahead - SHIFTS[ITERS - 1] * gram[i][ITERS - 1]

    one, zero = jnp.ones(shape, F32), jnp.zeros(shape, F32)
    x, res, dirn = [zero] * ITERS, [one] + [zero] * ITERS, [one] + [zero] * (ITERS - 1)
    rho = gram[0][0]
    for it in range(ITERS):
        moved = [zero] * (ITERS + 1)
        for k in range(it + 1):
            moved[k + 1] = moved[k + 1] + dirn[k]
            moved[k] = moved[k] + SHIFTS[k] * dirn[k]
        curve = zero
        for i in range(it + 1):
            line = zero
            for j in range(it + 2):
                line = line + moved[j] * gram[i][j]
            curve = curve + dirn[i] * line
        alpha = rho / curve
        x = [x[i] + alpha * dirn[i] for i in range(ITERS)]
        res = [res[i] - alpha * moved[i] for i in range(ITERS + 1)]
        if it + 1 < ITERS:
            rho_new = zero
            for i in range(it + 2):
                line = zero
                for j in range(it + 2):
                    line = line + res[j] * gram[i][j]
                rho_new = rho_new + res[i] * line
            ratio = rho_new / rho
            rho = rho_new
            dirn = [res[i] + ratio * dirn[i] for i in range(ITERS)]
    for k, value in enumerate(x + res):
        factors[k] = value

    def finish(r, carry):
        xs = [factors[k, pl.ds(r, 1)] for k in range(ITERS)]
        rs = [factors[ITERS + k, pl.ds(r, 1)] for k in range(ITERS + 1)]
        for t in range(2):
            span = pl.ds(LANES * t, LANES)
            seen = looks[r, pl.ds(0, TILE_ROWS), span]
            for m in range(MONTHS):
                f = r * MONTHS + m
                vs = [basis[slot_at(s) + f, t, CORE] for s in range(ITERS)]
                vs.append(image[f, t] + basis[FIELDS + m, t, CORE] * seen - SHIFTS[3] * vs[3])
                dual_ref[f, :, span] = xs[0] * vs[0] + xs[1] * vs[1] + xs[2] * vs[2] + xs[3] * vs[3]
                total = rs[0] * vs[0]
                for k in range(1, ITERS + 1):
                    total = total + rs[k] * vs[k]
                res_ref[f, :, span] = diag[m, t] * total
        return carry

    lax.fori_loop(0, RHS, finish, 0)
    for r in range(RHS):
        xs = [factors[k, pl.ds(r, 1)] for k in range(ITERS)]
        rs = [factors[ITERS + k, pl.ds(r, 1)] for k in range(ITERS + 1)]
        for t in range(2):
            dual = xs[0] * table[0, r, t]
            total = rs[0] * table[0, r, t]
            for k in range(1, ITERS):
                dual = dual + xs[k] * table[k, r, t]
            for k in range(1, ITERS + 1):
                total = total + rs[k] * table[k, r, t]
            total = total * diag_di[t]
            for hi in range(districts // DLO):
                span = pl.ds(LANES * (2 * hi + t), LANES)
                dual_di_ref[pl.ds(r, 1), span] = dual[hi : hi + 1]
                res_di_ref[pl.ds(r, 1), span] = total[hi : hi + 1]

    for copies in (halo_stat, halo_first, halo_second, halo_third, halo_fourth):
        for copy in copies:
            copy.wait_send()
    for n in range(3):
        sum_drain(n)
    bytes_of(late_near.at[pl.ds(1, group - 1)], sum_send.at[3, 0])
    bytes_of(late_z.at[pl.ds(1, chips - 1)], sum_send.at[3, 1])


def body(
    right_aquifer,
    right_district,
    head_scale,
    crop_scale,
    conductance,
    water_use,
    climate,
    district_use,
    district_id,
    active,
):
    rows, cols = lax.axis_size("row"), lax.axis_size("col")
    group, chips = 2 * cols, rows // 2
    per = CHUNKS // group
    tile_rows, tile_cols = climate.shape
    grid_cells = tile_rows * rows * tile_cols * cols
    whole = pl.BlockSpec(memory_space=pltpu.VMEM)
    block = (FIELDS, tile_rows, tile_cols)
    vmem = lambda *shape: pltpu.VMEM(shape, F32)
    core = (2, TILE_ROWS, LANES)
    outs = pl.pallas_call(
        functools.partial(kernel, grid_cells),
        out_shape=(
            jax.ShapeDtypeStruct(block, F32),
            jax.ShapeDtypeStruct(right_district.shape, F32),
            jax.ShapeDtypeStruct(block, F32),
            jax.ShapeDtypeStruct(right_district.shape, F32),
        ),
        in_specs=[pl.BlockSpec(memory_space=pltpu.HBM)] * 10,
        out_specs=(whole,) * 4,
        scratch_shapes=[
            vmem(ITERS * FIELDS + MONTHS, 3, 32, LANES),
            vmem(FIELDS, *core),
            vmem(16, 3, 32, LANES),
            vmem(5, 3, 24, LANES),
            vmem(MONTHS, 3, 24, LANES),
            vmem(5, *core),
            vmem(MONTHS, *core),
            vmem(MONTHS, *core),
            vmem(MONTHS, *core),
            vmem(CROPS, *core),
            vmem(MONTHS, 3, 24, LANES),
            pltpu.VMEM((DLO, LINES * 2 * LANES), jnp.bfloat16),
            pltpu.VMEM((24, 2 * LANES), jnp.int32),
            pltpu.VMEM((24, 2 * LANES), jnp.int32),
            vmem(2 + RHS, TILE_ROWS, 2 * LANES),
            vmem(2 * RHS, 24, 2 * LANES),
            vmem(RHS, 3, 32, LANES),
            pltpu.VMEM((2 * (2 + RHS) * DHI, TILE_ROWS * 2 * LANES), jnp.bfloat16),
            vmem(*right_district.shape),
            vmem(*crop_scale.shape),
            vmem(*climate.shape),
            pltpu.VMEM(district_id.shape, jnp.int32),
            pltpu.VMEM(active.shape, jnp.int32),
            vmem(ITERS + 1, RHS, 2, DHI, LANES),
            vmem(2, DHI, LANES),
            vmem(2, DHI, LANES),
            vmem(RHS, 2, DHI, LANES),
            vmem(3, group, 8 * per, LANES),
            vmem(3, group, 8 * per, LANES),
            vmem(3, chips, 8 * per, LANES),
            vmem(3, group, 8 * per, LANES),
            vmem(group, 8, LANES),
            vmem(chips, 8, LANES),
            vmem(8, LANES),
            vmem(2 * ITERS + 1, 8, LANES),
            vmem(5, 2, 15, 2, 8, LANES),
            vmem(5, 2, 15, 2, 8, LANES),
            vmem(5, 2, TILE_ROWS, LANES),
            vmem(5, 2, 2, 32, LANES),
            pltpu.SemaphoreType.DMA((5, 8)),
            pltpu.SemaphoreType.DMA((5, 8)),
            pltpu.SemaphoreType.DMA((4, 3)),
            pltpu.SemaphoreType.DMA((4, 3)),
            pltpu.SemaphoreType.DMA((13,)),
            pltpu.SMEM(water_use.shape[::-1], F32),
            pltpu.SMEM(district_use.shape, F32),
        ],
        compiler_params=pltpu.CompilerParams(
            collective_id=0, has_side_effects=True, vmem_limit_bytes=48 * 1024 * 1024
        ),
    )(
        *(
            pltpu.with_memory_space_constraint(value, pltpu.HBM)
            for value in (
                right_aquifer.reshape(block),
                right_district,
                head_scale,
                crop_scale,
                conductance,
                climate,
                district_id,
                active,
                water_use.T,
                district_use,
            )
        )
    )
    dual, dual_di, res, res_di = outs
    return dual.reshape(right_aquifer.shape), dual_di, res.reshape(right_aquifer.shape), res_di


def solution(mesh):
    placed = (
        P(None, None, "row", "col"),
        P(),
        P(None, "row", "col"),
        P(None, "row", "col"),
        P(None, "row", "col"),
        P(),
        P("row", "col"),
        P(),
        P("row", "col"),
        P("row", "col"),
    )
    return jax.shard_map(
        body,
        mesh=mesh,
        in_specs=placed,
        out_specs=(P(None, None, "row", "col"), P(), P(None, None, "row", "col"), P()),
        check_vma=False,
    )
```

```python
import functools

import jax
import jax.numpy as jnp
from jax import lax
from jax.experimental import pallas as pl
from jax.experimental.pallas import tpu as pltpu
from jax.sharding import PartitionSpec as P

ITERS = 4
RHS = 4
MONTHS = 12
CROPS = 6
FIELDS = RHS * MONTHS
DHI = 16
DLO = 256
LANES = 128
TILE_ROWS = 16
CHUNKS = 32
LINES = 22
ID_FIELD = 14
PROXIMAL = 0.05
SHIFTS = (0.5, 8.0, 3.0, 1.0)
PAIRS = tuple((i, j) for i in range(ITERS) for j in range(i, ITERS))
MESH = pl.DeviceIdType.MESH
F32 = jnp.float32
CORE = pl.ds(8, 16)


def lanes_of(shape):
    return lax.broadcasted_iota(jnp.int32, shape, len(shape) - 1)


def rows_of(shape):
    return lax.broadcasted_iota(jnp.int32, shape, len(shape) - 2)


def beside(tiles):
    axis = tiles[0].ndim - 1
    lane = lanes_of(tiles[0].shape)
    ahead = [pltpu.roll(t, LANES - 1, axis) for t in tiles]
    behind = [pltpu.roll(t, 1, axis) for t in tiles]
    east = [jnp.where(lane == LANES - 1, ahead[(n + 1) % 3], ahead[n]) for n in range(3)]
    west = [jnp.where(lane == 0, behind[(n + 2) % 3], behind[n]) for n in range(3)]
    return east, west


def kernel(
    grid_cells,
    rhs_hbm,
    rdi_hbm,
    head_hbm,
    crop_hbm,
    cond_hbm,
    climate_hbm,
    id_hbm,
    active_hbm,
    wu_hbm,
    use_hbm,
    dual_ref,
    dual_di_ref,
    res_ref,
    res_di_ref,
    basis,
    image,
    stat,
    coef,
    headw,
    coefc,
    diag,
    dinv,
    cross,
    wcs,
    inner,
    hot,
    lo_id,
    hi_id,
    cells,
    looks,
    wide_look,
    spread,
    rdi_ref,
    crop_ref,
    climate_ref,
    id_ref,
    active_ref,
    table,
    diag_di,
    wide,
    bdi,
    sum_in,
    sum_near,
    sum_z,
    sum_out,
    late_near,
    late_z,
    late_in,
    factors,
    row_out,
    row_in,
    col_out,
    col_in,
    xch_send,
    xch_recv,
    sum_send,
    sum_recv,
    load_sem,
    wu_ref,
    use_ref,
):
    rows, cols = lax.axis_size("row"), lax.axis_size("col")
    chips, group = rows // 2, 2 * cols
    per = CHUNKS // group
    row, col = lax.axis_index("row"), lax.axis_index("col")
    chip, core = row // 2, lax.rem(row, 2)
    mine = core * cols + col
    districts = rdi_ref.shape[1]

    def slot_at(slot):
        return slot * FIELDS + (MONTHS if slot else 0)


    def peer(k):
        other = lax.rem(mine + k, group)
        return other, (chip * 2 + other // cols, lax.rem(other, cols))

    def stack(k):
        return (lax.rem(row + 2 * k, rows), col)

    def around(dr, dc):
        return (lax.rem(row + dr + rows, rows), lax.rem(col + dc + cols, cols))

    loads = []
    for t in range(2):
        span = pl.ds(LANES * t, LANES)
        loads.append((cond_hbm.at[:, :, span], stat.at[pl.ds(0, 2), t, CORE]))
        loads.append((head_hbm.at[:, :, span], stat.at[pl.ds(2, MONTHS), t, CORE]))
    loads += [(id_hbm, id_ref), (climate_hbm, climate_ref), (active_hbm, active_ref)]
    loads += [(wu_hbm, wu_ref), (use_hbm, use_ref), (crop_hbm, crop_ref), (rdi_hbm, rdi_ref)]
    for t in range(2):
        loads.append((rhs_hbm.at[:, :, pl.ds(LANES * t, LANES)], basis.at[pl.ds(0, FIELDS), t, CORE]))
    loads = [pltpu.make_async_copy(src, dst, load_sem.at[k]) for k, (src, dst) in enumerate(loads)]
    for load in loads:
        load.start()

    barrier = pltpu.get_barrier_semaphore()

    def greet(k, carry):
        pl.semaphore_signal(barrier, inc=1, device_id=peer(k)[1], device_id_type=MESH)
        return carry

    def greet_stack(k, carry):
        pl.semaphore_signal(barrier, inc=1, device_id=stack(k), device_id_type=MESH)
        return carry

    lax.fori_loop(1, group, greet, 0)
    lax.fori_loop(1, chips, greet_stack, 0)
    offsets = [(dr, dc) for dr in (-1, 0, 1) for dc in (-1, 0, 1) if dr or dc]
    for dr, dc in offsets:
        pl.semaphore_signal(barrier, inc=1, device_id=around(dr, dc), device_id_type=MESH)

    north = jnp.where(row > 0, 1.0, 0.0).astype(F32)
    south = jnp.where(row < rows - 1, 1.0, 0.0).astype(F32)
    west = jnp.where(col > 0, 1.0, 0.0).astype(F32)
    east = jnp.where(col < cols - 1, 1.0, 0.0).astype(F32)

    def halo_copies(n, quads, groups):
        ahead, back = pl.ds(8, 8), pl.ds(0, 8)
        plan = [
            (row_out.at[n, 0, pl.ds(0, quads)], row_in.at[n, 0, pl.ds(0, quads)], (1, 0)),
            (row_out.at[n, 1, pl.ds(0, quads)], row_in.at[n, 1, pl.ds(0, quads)], (-1, 0)),
            (col_out.at[n, pl.ds(0, groups)], col_in.at[n, 0, pl.ds(0, groups), CORE], (0, 1)),
            (col_out.at[n, pl.ds(0, groups)], col_in.at[n, 1, pl.ds(0, groups), CORE], (0, -1)),
            (col_out.at[n, pl.ds(0, groups), ahead], col_in.at[n, 0, pl.ds(0, groups), pl.ds(0, 8)], (1, 1)),
            (col_out.at[n, pl.ds(0, groups), ahead], col_in.at[n, 1, pl.ds(0, groups), pl.ds(0, 8)], (1, -1)),
            (col_out.at[n, pl.ds(0, groups), back], col_in.at[n, 0, pl.ds(0, groups), pl.ds(24, 8)], (-1, 1)),
            (col_out.at[n, pl.ds(0, groups), back], col_in.at[n, 1, pl.ds(0, groups), pl.ds(24, 8)], (-1, -1)),
        ]
        return [
            pltpu.make_async_remote_copy(
                src_ref=src,
                dst_ref=dst,
                send_sem=xch_send.at[n, k],
                recv_sem=xch_recv.at[n, k],
                device_id=around(*to),
                device_id_type=MESH,
            )
            for k, (src, dst, to) in enumerate(plan)
        ]

    def halo_pack_cols(n, ref, base, quads):
        lane = lanes_of((TILE_ROWS, LANES))

        def cols_of(f, packed, slot):
            both = jnp.where(lane < 64, ref[base + f, 0, CORE], ref[base + f, 1, CORE])
            moved = pltpu.roll(both, lax.rem(4 * slot + 2, LANES), 1)
            return jnp.where(lane // 4 == slot, moved, packed)

        for g in range((quads + 7) // 8):
            count = min(32, 4 * quads - 32 * g)

            def quad(k, packed):
                for u in range(4):
                    packed = cols_of(32 * g + 4 * k + u, packed, 4 * k + u)
                return packed

            col_out[n, g] = lax.fori_loop(0, count // 4, quad, jnp.zeros((TILE_ROWS, LANES), F32), unroll=count // 4)

    def halo_pack_rows(n, ref, base, quads):
        def rows_quad(k, carry):
            for u in range(4):
                field = ref.at[base + 4 * k + u]
                for t in range(2):
                    row_out[n, 0, k, t, pl.ds(2 * u, 2)] = field[t, pl.ds(22, 2)]
                    row_out[n, 1, k, t, pl.ds(2 * u, 2)] = field[t, pl.ds(8, 2)]
            return carry

        lax.fori_loop(0, quads, rows_quad, 0, unroll=quads // 4 if quads % 4 == 0 else 5)

    def send_cols(n, ref, base, quads):
        copies = halo_copies(n, quads, (quads + 7) // 8)
        halo_pack_cols(n, ref, base, quads)
        for copy in copies[2:]:
            copy.start()
        return copies

    def send_rows(copies, n, ref, base, quads):
        halo_pack_rows(n, ref, base, quads)
        for copy in copies[:2]:
            copy.start()

    def halo_send(n, ref, base, quads):
        copies = send_cols(n, ref, base, quads)
        send_rows(copies, n, ref, base, quads)
        return copies

    def halo_cols(copies, n, ref, base, quads):
        for copy in copies[2:]:
            copy.wait_recv()
        shape = (32, LANES)
        lane, place = lanes_of(shape), rows_of(shape)
        side = jnp.where(lax.rem(lane, 4) < 2, west, east)
        side = side * jnp.where(place < 8, north, jnp.where(place >= 24, south, 1.0))
        for g in range((quads + 7) // 8):
            count = min(32, 4 * quads - 32 * g)
            packed = jnp.where(lax.rem(lane, 4) < 2, col_in[n, 0, g], col_in[n, 1, g]) * side

            def quad(k, carry):
                for u in range(4):
                    slot = 4 * k + u
                    moved = pltpu.roll(packed, lax.rem(2 * LANES - 4 * slot - 2, LANES), 1)
                    ref[base + 32 * g + slot, 2] = moved
                return carry

            lax.fori_loop(0, count // 4, quad, 0, unroll=count // 4)

    def halo_rows(copies, n, ref, base, quads):
        for copy in copies[:2]:
            copy.wait_recv()

        def rows_quad(k, carry):
            for u in range(4):
                for t in range(2):
                    ref[base + 4 * k + u, t, pl.ds(6, 2)] = row_in[n, 0, k, t, pl.ds(2 * u, 2)] * north
                    ref[base + 4 * k + u, t, pl.ds(24, 2)] = row_in[n, 1, k, t, pl.ds(2 * u, 2)] * south
            return carry

        lax.fori_loop(0, quads, rows_quad, 0, unroll=quads // 4 if quads % 4 == 0 else 5)

    def bytes_of(ref, sem):
        pltpu.make_async_copy(ref, ref, sem).wait()

    def sum_scatter(n):
        def scatter(k, carry):
            other, device = peer(k)
            pltpu.make_async_remote_copy(
                src_ref=sum_in.at[n, other],
                dst_ref=sum_near.at[n, k],
                send_sem=sum_send.at[n, 0],
                recv_sem=sum_recv.at[n, 0],
                device_id=device,
                device_id_type=MESH,
            ).start()
            return carry

        lax.fori_loop(1, group, scatter, 0)
        sum_near[n, 0] = sum_in[n, mine]

    def sum_spread(n):
        bytes_of(sum_near.at[n, pl.ds(1, group - 1)], sum_recv.at[n, 0])
        sum_z[n, chip] = jnp.sum(sum_near[n], axis=0)

        def spread(k, carry):
            pltpu.make_async_remote_copy(
                src_ref=sum_z.at[n, chip],
                dst_ref=sum_z.at[n, chip],
                send_sem=sum_send.at[n, 1],
                recv_sem=sum_recv.at[n, 1],
                device_id=stack(k),
                device_id_type=MESH,
            ).start()
            return carry

        lax.fori_loop(1, chips, spread, 0)

    def sum_gather(n):
        bytes_of(sum_z.at[n, pl.ds(1, chips - 1)], sum_recv.at[n, 1])
        sum_out[n, mine] = jnp.sum(sum_z[n], axis=0)

        def gather(k, carry):
            pltpu.make_async_remote_copy(
                src_ref=sum_out.at[n, mine],
                dst_ref=sum_out.at[n, mine],
                send_sem=sum_send.at[n, 2],
                recv_sem=sum_recv.at[n, 2],
                device_id=peer(k)[1],
                device_id_type=MESH,
            ).start()
            return carry

        lax.fori_loop(1, group, gather, 0)

    def sum_done(n):
        bytes_of(sum_near.at[n, pl.ds(1, group - 1)], sum_recv.at[n, 2])

    def sum_drain(n):
        bytes_of(sum_near.at[n, pl.ds(1, group - 1)], sum_send.at[n, 0])
        bytes_of(sum_z.at[n, pl.ds(1, chips - 1)], sum_send.at[n, 1])
        bytes_of(sum_near.at[n, pl.ds(1, group - 1)], sum_send.at[n, 2])

    def chunk(k):
        return k // per, pl.ds(8 * (k % per), 8)

    def line_span(i):
        return pl.ds(pl.multiple_of(i * (2 * LANES), 2 * LANES), 2 * LANES)

    def to_district(n, count, first):
        size = count * DHI

        def line(i, carry):
            value = cells[pl.ds(0, count), pl.ds(i, 1), :]
            high = value.astype(jnp.bfloat16).astype(F32)
            here = (hi_id[pl.ds(i, 1), :] == rows_of((DHI, 2 * LANES)))[None]
            for k, part in enumerate((high, value - high)):
                part = jnp.where(here, jnp.broadcast_to(part, (count, DHI, 2 * LANES)), 0.0)
                spread[pl.ds(k * size, size), line_span(i)] = part.reshape(size, 2 * LANES).astype(jnp.bfloat16)
            return carry

        lax.fori_loop(0, TILE_ROWS, line, 0, unroll=2)
        total = lax.dot_general(
            hot[:, pl.ds(0, TILE_ROWS * 2 * LANES)], spread[pl.ds(0, 2 * size), :], (((1,), (1,)), ((), ())), preferred_element_type=F32
        ).T
        total = total[:size] + total[size:]
        for b in range(count):
            for t in range(2):
                for h in range(2):
                    at, part = chunk(4 * (first + b) + 2 * t + h)
                    sum_in[n, at, part] = total[DHI * b + 8 * h : DHI * b + 8 * h + 8, LANES * t : LANES * (t + 1)]

    def from_district(slot, count, first, lines=TILE_ROWS):
        size = count * RHS * DHI
        values = jnp.concatenate(
            [
                jnp.concatenate([table[slot + s, r, t] for t in range(2)], axis=1)
                for s in range(count)
                for r in range(RHS)
            ],
            axis=0,
        )
        high = values.astype(jnp.bfloat16).astype(F32)
        both = jnp.concatenate([high, values - high], axis=0).astype(jnp.bfloat16)

        def two(k, carry):
            span = pl.ds(pl.multiple_of(k * (4 * LANES), 4 * LANES), 4 * LANES)
            picked = jnp.dot(both, hot[:, span], preferred_element_type=F32)
            picked = (picked[:size] + picked[size:]).reshape(count * RHS, DHI, 4 * LANES)
            for u in range(2):
                here = (hi_id[pl.ds(2 * k + u, 1), :] == rows_of((DHI, 2 * LANES)))[None]
                part = jnp.where(here, picked[:, :, 2 * LANES * u : 2 * LANES * (u + 1)], 0.0)
                looks[pl.ds(first, count * RHS), pl.ds(2 * k + u, 1), :] = jnp.sum(part, axis=1, keepdims=True)
            return carry

        lax.fori_loop(0, lines // 2, two, 0, unroll=lines // 2 if count == 1 else 1)

    def cells_of(load, first):
        def one(r, carry):
            for t in range(2):
                total = jnp.zeros((TILE_ROWS, LANES), F32)
                for m in range(MONTHS):
                    total += cross[m, t] * load(r * MONTHS + m, t)
                cells[first + r, :, pl.ds(LANES * t, LANES)] = total
            return carry

        lax.fori_loop(0, RHS, one, 0)

    def core_of(slot):
        return lambda f, t: basis[slot_at(slot) + f, t, CORE]

    def smooth(slot, put):
        def one(r, carry):
            base = slot_at(slot) + r * MONTHS
            for k in range(3):
                part, place = pl.ds(8 * k, 8), pl.ds(4 + 8 * k, 8)
                face = [[coef[j, t, part] for t in range(3)] for j in range(5)]
                for m in range(MONTHS):
                    here = [basis[base + m, t, place] for t in range(3)]
                    e, w = beside(here)
                    for t in range(3):
                        lap = face[4][t] * here[t] - face[0][t] * e[t] - face[1][t] * w[t]
                        lap = lap - face[2][t] * basis[base + m, t, pl.ds(5 + 8 * k, 8)]
                        lap = lap - face[3][t] * basis[base + m, t, pl.ds(3 + 8 * k, 8)]
                        inner[m, t, part] = headw[m, t, part] * lap
            for k in range(2):
                part, place = pl.ds(8 * k, 8), pl.ds(8 + 8 * k, 8)
                draws = [[jnp.zeros((8, LANES), F32)] * CROPS for _ in range(2)]
                for m in range(MONTHS):
                    value = [basis[base + m, t, place] for t in range(2)]
                    for c in range(CROPS):
                        for t in range(2):
                            draws[t][c] = draws[t][c] + wu_ref[c, m] * value[t]
                draws = [[wcs[c, t, part] * draws[t][c] for c in range(CROPS)] for t in range(2)]
                face = [[coefc[j, t, part] for t in range(2)] for j in range(5)]
                for m in range(MONTHS):
                    here = [inner[m, t, pl.ds(4 + 8 * k, 8)] for t in range(3)]
                    e, w = beside(here)
                    for t in range(2):
                        own = basis[base + m, t, place]
                        lap = face[4][t] * here[t] - face[0][t] * e[t] - face[1][t] * w[t]
                        lap = lap - face[2][t] * inner[m, t, pl.ds(5 + 8 * k, 8)]
                        lap = lap - face[3][t] * inner[m, t, pl.ds(3 + 8 * k, 8)]
                        total = lap + PROXIMAL * own
                        for c in range(CROPS):
                            total = total + wu_ref[c, m] * draws[t][c]
                        put(r, m, t, k, dinv[m, t, part] * total, own)
            return carry

        lax.fori_loop(0, RHS, one, 0)

    def to_image(r, m, t, k, value, own):
        image[r * MONTHS + m, t, pl.ds(8 * k, 8)] = value

    def to_second(r, m, t, k, value, own):
        basis[slot_at(1) + r * MONTHS + m, t, pl.ds(8 + 8 * k, 8)] = value

    def to_next(slot, look, shift):
        def put(r, m, t, k, value, own):
            place = pl.ds(8 + 8 * k, 8)
            seen = looks[look + r, pl.ds(8 * k, 8), pl.ds(LANES * t, LANES)]
            value = value + basis[FIELDS + m, t, place] * seen - shift * own
            basis[slot_at(slot + 1) + r * MONTHS + m, t, place] = value

        return put

    def advance_wide(shift):
        window = pl.ds(4, 24)

        def one(r, carry):
            for t in range(3):
                seen = wide_look[r, t, window]
                for m in range(MONTHS):
                    f = r * MONTHS + m
                    basis[slot_at(1) + f, t, window] = (
                        basis[slot_at(1) + f, t, window]
                        + basis[FIELDS + m, t, window] * seen
                        - shift * basis[f, t, window]
                    )
            return carry

        lax.fori_loop(0, RHS, one, 0)

    def repeat(packed):
        for width in (4, 8, 16, 32, 64):
            packed = packed + pltpu.roll(packed, width, 1)
        return packed

    def fill_wide_look():
        shape = (24, LANES)
        own = lanes_of(shape) // 4 == rows_of(shape)
        for r in range(RHS):
            for t in range(2):
                span = pl.ds(LANES * t, LANES)
                wide_look[r, t, CORE] = looks[r, pl.ds(0, TILE_ROWS), span]
                wide_look[r, t, pl.ds(6, 2)] = looks[r, pl.ds(16, 2), span]
                wide_look[r, t, pl.ds(24, 2)] = looks[r, pl.ds(18, 2), span]
            edge = repeat(jnp.where(own, looks[r, pl.ds(20, 1), pl.ds(0, LANES)], 0.0))
            wide_look[r, 2, pl.ds(4, 24)] = pltpu.roll(edge, LANES - 2, 1)

    def wide_ids():
        shape = (24, LANES)
        edge = pltpu.roll(stat[ID_FIELD, 2, pl.ds(4, 24)], 2, 1)
        edge = repeat(jnp.where(lanes_of(shape) < 4, edge, 0.0))
        edge = jnp.sum(jnp.where(lanes_of(shape) // 4 == rows_of(shape), edge, 0.0), axis=0, keepdims=True)
        lines = [jnp.concatenate([stat[ID_FIELD, t, pl.ds(i, 1)] for t in range(2)], axis=1) for i in (6, 7, 24, 25)]
        lines.append(jnp.concatenate([edge, edge], axis=1))
        for k, one in enumerate(lines):
            ids = one.astype(jnp.int32)
            hi_id[pl.ds(16 + k, 1), :] = ids // DLO
            lo_id[pl.ds(16 + k, 1), :] = lax.rem(ids, DLO)
        lax.fori_loop(TILE_ROWS, LINES - 1, hot_line, 0)

    for t in range(2):
        stat[15, t, CORE] = jnp.zeros((TILE_ROWS, LANES), F32)
    sum_in[...] = jnp.zeros_like(sum_in)
    for load in loads[:5]:
        load.wait()
    for t in range(2):
        stat[ID_FIELD, t, CORE] = id_ref[:, pl.ds(LANES * t, LANES)].astype(F32)
    halo_pack_cols(0, stat, 0, 4)
    halo_pack_rows(0, stat, 0, 4)
    for load in loads[5:]:
        load.wait()
    scale = (districts / grid_cells) ** 0.5
    ids = id_ref[...]
    hi_id[pl.ds(0, TILE_ROWS), :] = ids // DLO
    lo_id[pl.ds(0, TILE_ROWS), :] = lax.rem(ids, DLO)

    def hot_line(i, carry):
        same = lo_id[pl.ds(i, 1), :] == rows_of((DLO, 2 * LANES))
        hot[:, line_span(i)] = jnp.where(same, 1.0, 0.0).astype(jnp.bfloat16)
        return carry

    lax.fori_loop(0, TILE_ROWS, hot_line, 0)
    for t in range(2):
        span = pl.ds(LANES * t, LANES)
        live = active_ref[:, span].astype(F32)
        weight = live * climate_ref[:, span]
        crops = [crop_ref[c, :, span] for c in range(CROPS)]
        own = jnp.zeros((TILE_ROWS, LANES), F32)
        for c in range(CROPS):
            use = scale * use_ref[c] * live
            own = own + use * use * crops[c]
            wcs[c, t] = weight * weight * crops[c]
        cells[0, :, span] = own
        for m in range(MONTHS):
            square = jnp.zeros((TILE_ROWS, LANES), F32)
            mixed = jnp.zeros((TILE_ROWS, LANES), F32)
            for c in range(CROPS):
                drawn = wu_ref[c, m] * crops[c]
                square = square + wu_ref[c, m] * drawn
                mixed = mixed + use_ref[c] * drawn
            diag[m, t] = weight * weight * square + PROXIMAL
            cross[m, t] = weight * live * (scale * mixed)
    for r in range(RHS):
        for t in range(2):
            bdi[r, t] = jnp.zeros((DHI, LANES), F32)
            for hi in range(districts // DLO):
                at = LANES * (2 * hi + t)
                bdi[r, t, pl.ds(hi, 1)] = rdi_ref[pl.ds(r, 1), pl.ds(at, LANES)]

    pl.semaphore_wait(barrier, group + chips - 2 + len(offsets))
    halo_stat = halo_copies(0, 4, 1)
    for copy in halo_stat:
        copy.start()

    halo_rows(halo_stat, 0, stat, 0, 4)
    halo_cols(halo_stat, 0, stat, 0, 4)
    window = pl.ds(4, 24)
    faces = [[stat[k, t, window] for t in range(3)] for k in range(2)]
    east_side, west_side = beside(faces[0])
    for t in range(3):
        south_north = stat[1, t, pl.ds(3, 24)]
        coef[0, t] = faces[0][t]
        coef[1, t] = west_side[t]
        coef[2, t] = faces[1][t]
        coef[3, t] = south_north
        coef[4, t] = faces[0][t] + west_side[t] + faces[1][t] + south_north
    for k in range(5):
        for t in range(2):
            coefc[k, t] = coef[k, t, pl.ds(4, 16)]

    def month_diag(m, carry):
        for t in range(3):
            headw[m, t] = stat[2 + m, t, window]
        here = [stat[2 + m, t, CORE] for t in range(3)]
        e, w = beside(here)
        for t in range(2):
            fe, fw, fs, fn, total = [coefc[k, t] for k in range(5)]
            value = diag[m, t] + here[t] * total * total + fe * fe * e[t] + fw * fw * w[t]
            value = value + fs * fs * stat[2 + m, t, pl.ds(9, 16)] + fn * fn * stat[2 + m, t, pl.ds(7, 16)]
            diag[m, t] = value
            inverse = 1.0 / value
            dinv[m, t] = inverse
            basis[FIELDS + m, t, CORE] = cross[m, t] * inverse
        return carry

    lax.fori_loop(0, MONTHS, month_diag, 0, unroll=4)

    def start_basis(r, carry):
        for t in range(2):
            for m in range(MONTHS):
                f = r * MONTHS + m
                basis[f, t, CORE] = basis[f, t, CORE] * dinv[m, t]
        return carry

    lax.fori_loop(0, RHS, start_basis, 0)

    both = (FIELDS + MONTHS) // 4
    halo_first = halo_send(1, basis, 0, both)
    for t in range(2):
        total = jnp.zeros((TILE_ROWS, LANES), F32)
        for m in range(MONTHS):
            total += cross[m, t] * basis[FIELDS + m, t, CORE]
        cells[1, :, pl.ds(LANES * t, LANES)] = total
    cells_of(core_of(0), 2)
    to_district(0, 2 + RHS, 0)
    sum_scatter(0)

    wide_ids()
    sum_spread(0)
    halo_rows(halo_first, 1, basis, 0, both)
    halo_cols(halo_first, 1, basis, 0, both)
    smooth(0, to_second)
    halo_second = halo_send(2, basis, slot_at(1), FIELDS // 4)
    sum_gather(0)
    cells_of(core_of(1), 0)
    to_district(1, RHS, 0)
    sum_scatter(1)
    halo_rows(halo_second, 2, basis, slot_at(1), FIELDS // 4)
    sum_done(0)

    def total_of(n, b):
        parts = [sum_out[(n,) + chunk(4 * b + k)] for k in range(4)]
        return jnp.stack([jnp.concatenate(parts[:2], axis=0), jnp.concatenate(parts[2:], axis=0)])

    diag_di[...] = total_of(0, 0) + PROXIMAL
    wide[...] = total_of(0, 1)
    for r in range(RHS):
        t0 = bdi[r] / diag_di[...]
        table[0, r] = t0
        table[1, r] = total_of(0, 2 + r) / diag_di[...] + (1 - SHIFTS[0]) * t0
    from_district(0, 2, 0, LINES)
    fill_wide_look()
    halo_cols(halo_second, 2, basis, slot_at(1), FIELDS // 4)
    sum_spread(1)
    advance_wide(SHIFTS[0])
    smooth(1, to_next(1, RHS, SHIFTS[1]))
    halo_third = halo_send(3, basis, slot_at(2), FIELDS // 4)
    sum_gather(1)
    cells_of(core_of(2), 0)
    to_district(2, RHS, 0)
    sum_done(1)
    for r in range(RHS):
        z1 = total_of(1, r) + wide[...] * table[0, r] - SHIFTS[0] * total_of(0, 2 + r)
        table[2, r] = z1 / diag_di[...] + (1 - SHIFTS[1]) * table[1, r]
    from_district(2, 1, 0)
    halo_rows(halo_third, 3, basis, slot_at(2), FIELDS // 4)
    halo_cols(halo_third, 3, basis, slot_at(2), FIELDS // 4)
    smooth(2, to_next(2, 0, SHIFTS[2]))
    halo_fourth = send_cols(4, basis, slot_at(3), FIELDS // 4)
    cells_of(core_of(3), 0)
    to_district(2, RHS, RHS)
    sum_scatter(2)
    send_rows(halo_fourth, 4, basis, slot_at(3), FIELDS // 4)

    shape = (8, LANES)

    def inner_products(r, packed):
        totals = [jnp.zeros(shape, F32) for _ in PAIRS]
        for m in range(MONTHS):
            for t in range(2):
                values = [basis[slot_at(s) + r * MONTHS + m, t, CORE] for s in range(ITERS)]
                scaled = [diag[m, t] * v for v in values]
                for n, (i, j) in enumerate(PAIRS):
                    term = scaled[i] * values[j]
                    totals[n] = totals[n] + (term[:8] + term[8:])
        for n, total in enumerate(totals):
            here = (rows_of(shape) == r) & (lanes_of(shape) == n)
            packed = jnp.where(here, jnp.sum(total, keepdims=True), packed)
        return packed

    packed = lax.fori_loop(0, RHS, inner_products, jnp.zeros(shape, F32))
    sum_spread(2)
    halo_rows(halo_fourth, 4, basis, slot_at(3), FIELDS // 4)
    halo_cols(halo_fourth, 4, basis, slot_at(3), FIELDS // 4)

    def top_product(r, packed):
        total = jnp.zeros(shape, F32)
        base = slot_at(3) + r * MONTHS
        draws = [[jnp.zeros((TILE_ROWS, LANES), F32)] * CROPS for _ in range(2)]
        for m in range(MONTHS):
            here = [basis[base + m, t, CORE] for t in range(3)]
            e, w = beside(here)
            for t in range(2):
                lap = coefc[4, t] * here[t] - coefc[0, t] * e[t] - coefc[1, t] * w[t]
                lap = lap - coefc[2, t] * basis[base + m, t, pl.ds(9, 16)]
                lap = lap - coefc[3, t] * basis[base + m, t, pl.ds(7, 16)]
                term = stat[2 + m, t, CORE] * lap * lap + PROXIMAL * here[t] * here[t]
                total = total + (term[:8] + term[8:])
                draws[t] = [draws[t][c] + wu_ref[c, m] * here[t] for c in range(CROPS)]
        for t in range(2):
            for c in range(CROPS):
                term = wcs[c, t] * draws[t][c] * draws[t][c]
                total = total + (term[:8] + term[8:])
        here = (rows_of(shape) == r) & (lanes_of(shape) == len(PAIRS))
        return jnp.where(here, jnp.sum(total, keepdims=True), packed)

    late_in[...] = lax.fori_loop(0, RHS, top_product, packed, unroll=2)

    def late_first(k, carry):
        pltpu.make_async_remote_copy(
            src_ref=late_in,
            dst_ref=late_near.at[mine],
            send_sem=sum_send.at[3, 0],
            recv_sem=sum_recv.at[3, 0],
            device_id=peer(k)[1],
            device_id_type=MESH,
        ).start()
        return carry

    lax.fori_loop(1, group, late_first, 0)
    late_near[mine] = late_in[...]
    smooth(3, to_image)
    sum_gather(2)
    bytes_of(late_near.at[pl.ds(1, group - 1)], sum_recv.at[3, 0])
    late_z[chip] = jnp.sum(late_near[...], axis=0)

    def late_second(k, carry):
        pltpu.make_async_remote_copy(
            src_ref=late_z.at[chip],
            dst_ref=late_z.at[chip],
            send_sem=sum_send.at[3, 1],
            recv_sem=sum_recv.at[3, 1],
            device_id=stack(k),
            device_id_type=MESH,
        ).start()
        return carry

    lax.fori_loop(1, chips, late_second, 0)
    def district_part(i, j):
        out = jnp.zeros(shape, F32)
        for r in range(RHS):
            if j < ITERS:
                term = diag_di[...] * table[i, r] * table[j, r]
            else:
                term = table[3, r] * (2 * total_of(2, RHS + r) + diag_di[...] * table[3, r])
            line = jnp.sum(jnp.sum(term, axis=0), axis=0, keepdims=True)
            out = jnp.where(rows_of(shape) == r, line, out)
        return out

    early = {pair: district_part(*pair) for pair in PAIRS if pair[1] < 3}
    sum_done(2)
    for r in range(RHS):
        table[3, r] = total_of(2, r) / diag_di[...] + (1 - SHIFTS[2]) * table[2, r]
        table[4, r] = total_of(2, RHS + r) / diag_di[...] + (1 - SHIFTS[3]) * table[3, r]
    from_district(3, 1, 0)

    parts = [early[pair] if pair in early else district_part(*pair) for pair in PAIRS + ((3, ITERS),)]
    bytes_of(late_z.at[pl.ds(1, chips - 1)], sum_recv.at[3, 1])
    totals = jnp.sum(late_z[...], axis=0)
    gram = [[None] * (ITERS + 1) for _ in range(ITERS + 1)]
    values = []
    for n, part in enumerate(parts):
        both = part + jnp.where(lanes_of(shape) == n, totals, 0.0)
        values.append(jnp.broadcast_to(jnp.sum(both, axis=1, keepdims=True), shape))
    for n, (i, j) in enumerate(PAIRS):
        gram[i][j] = gram[j][i] = values[n]
    for i in range(ITERS):
        ahead = values[-1] if i == ITERS - 1 else gram[i + 1][ITERS - 1] + SHIFTS[i] * gram[i][ITERS - 1]
        gram[i][ITERS] = ahead - SHIFTS[ITERS - 1] * gram[i][ITERS - 1]

    one, zero = jnp.ones(shape, F32), jnp.zeros(shape, F32)
    x, res, dirn = [zero] * ITERS, [one] + [zero] * ITERS, [one] + [zero] * (ITERS - 1)
    rho = gram[0][0]
    for it in range(ITERS):
        moved = [zero] * (ITERS + 1)
        for k in range(it + 1):
            moved[k + 1] = moved[k + 1] + dirn[k]
            moved[k] = moved[k] + SHIFTS[k] * dirn[k]
        curve = zero
        for i in range(it + 1):
            line = zero
            for j in range(it + 2):
                line = line + moved[j] * gram[i][j]
            curve = curve + dirn[i] * line
        alpha = rho / curve
        x = [x[i] + alpha * dirn[i] for i in range(ITERS)]
        res = [res[i] - alpha * moved[i] for i in range(ITERS + 1)]
        if it + 1 < ITERS:
            rho_new = zero
            for i in range(it + 2):
                line = zero
                for j in range(it + 2):
                    line = line + res[j] * gram[i][j]
                rho_new = rho_new + res[i] * line
            ratio = rho_new / rho
            rho = rho_new
            dirn = [res[i] + ratio * dirn[i] for i in range(ITERS)]
    for k, value in enumerate(x + res):
        factors[k] = value

    def finish(r, carry):
        xs = [factors[k, pl.ds(r, 1)] for k in range(ITERS)]
        rs = [factors[ITERS + k, pl.ds(r, 1)] for k in range(ITERS + 1)]
        for t in range(2):
            span = pl.ds(LANES * t, LANES)
            seen = looks[r, pl.ds(0, TILE_ROWS), span]
            for m in range(MONTHS):
                f = r * MONTHS + m
                vs = [basis[slot_at(s) + f, t, CORE] for s in range(ITERS)]
                vs.append(image[f, t] + basis[FIELDS + m, t, CORE] * seen - SHIFTS[3] * vs[3])
                dual_ref[f, :, span] = xs[0] * vs[0] + xs[1] * vs[1] + xs[2] * vs[2] + xs[3] * vs[3]
                total = rs[0] * vs[0]
                for k in range(1, ITERS + 1):
                    total = total + rs[k] * vs[k]
                res_ref[f, :, span] = diag[m, t] * total
        return carry

    lax.fori_loop(0, RHS, finish, 0)
    for r in range(RHS):
        xs = [factors[k, pl.ds(r, 1)] for k in range(ITERS)]
        rs = [factors[ITERS + k, pl.ds(r, 1)] for k in range(ITERS + 1)]
        for t in range(2):
            dual = xs[0] * table[0, r, t]
            total = rs[0] * table[0, r, t]
            for k in range(1, ITERS):
                dual = dual + xs[k] * table[k, r, t]
            for k in range(1, ITERS + 1):
                total = total + rs[k] * table[k, r, t]
            total = total * diag_di[t]
            for hi in range(districts // DLO):
                span = pl.ds(LANES * (2 * hi + t), LANES)
                dual_di_ref[pl.ds(r, 1), span] = dual[hi : hi + 1]
                res_di_ref[pl.ds(r, 1), span] = total[hi : hi + 1]

    for copies in (halo_stat, halo_first, halo_second, halo_third, halo_fourth):
        for copy in copies:
            copy.wait_send()
    for n in range(3):
        sum_drain(n)
    bytes_of(late_near.at[pl.ds(1, group - 1)], sum_send.at[3, 0])
    bytes_of(late_z.at[pl.ds(1, chips - 1)], sum_send.at[3, 1])


def body(
    right_aquifer,
    right_district,
    head_scale,
    crop_scale,
    conductance,
    water_use,
    climate,
    district_use,
    district_id,
    active,
):
    rows, cols = lax.axis_size("row"), lax.axis_size("col")
    group, chips = 2 * cols, rows // 2
    per = CHUNKS // group
    tile_rows, tile_cols = climate.shape
    grid_cells = tile_rows * rows * tile_cols * cols
    whole = pl.BlockSpec(memory_space=pltpu.VMEM)
    block = (FIELDS, tile_rows, tile_cols)
    vmem = lambda *shape: pltpu.VMEM(shape, F32)
    core = (2, TILE_ROWS, LANES)
    outs = pl.pallas_call(
        functools.partial(kernel, grid_cells),
        out_shape=(
            jax.ShapeDtypeStruct(block, F32),
            jax.ShapeDtypeStruct(right_district.shape, F32),
            jax.ShapeDtypeStruct(block, F32),
            jax.ShapeDtypeStruct(right_district.shape, F32),
        ),
        in_specs=[pl.BlockSpec(memory_space=pltpu.HBM)] * 10,
        out_specs=(whole,) * 4,
        scratch_shapes=[
            vmem(ITERS * FIELDS + MONTHS, 3, 32, LANES),
            vmem(FIELDS, *core),
            vmem(16, 3, 32, LANES),
            vmem(5, 3, 24, LANES),
            vmem(MONTHS, 3, 24, LANES),
            vmem(5, *core),
            vmem(MONTHS, *core),
            vmem(MONTHS, *core),
            vmem(MONTHS, *core),
            vmem(CROPS, *core),
            vmem(MONTHS, 3, 24, LANES),
            pltpu.VMEM((DLO, LINES * 2 * LANES), jnp.bfloat16),
            pltpu.VMEM((24, 2 * LANES), jnp.int32),
            pltpu.VMEM((24, 2 * LANES), jnp.int32),
            vmem(2 + RHS, TILE_ROWS, 2 * LANES),
            vmem(2 * RHS, 24, 2 * LANES),
            vmem(RHS, 3, 32, LANES),
            pltpu.VMEM((2 * (2 + RHS) * DHI, TILE_ROWS * 2 * LANES), jnp.bfloat16),
            vmem(*right_district.shape),
            vmem(*crop_scale.shape),
            vmem(*climate.shape),
            pltpu.VMEM(district_id.shape, jnp.int32),
            pltpu.VMEM(active.shape, jnp.int32),
            vmem(ITERS + 1, RHS, 2, DHI, LANES),
            vmem(2, DHI, LANES),
            vmem(2, DHI, LANES),
            vmem(RHS, 2, DHI, LANES),
            vmem(3, group, 8 * per, LANES),
            vmem(3, group, 8 * per, LANES),
            vmem(3, chips, 8 * per, LANES),
            vmem(3, group, 8 * per, LANES),
            vmem(group, 8, LANES),
            vmem(chips, 8, LANES),
            vmem(8, LANES),
            vmem(2 * ITERS + 1, 8, LANES),
            vmem(5, 2, 15, 2, 8, LANES),
            vmem(5, 2, 15, 2, 8, LANES),
            vmem(5, 2, TILE_ROWS, LANES),
            vmem(5, 2, 2, 32, LANES),
            pltpu.SemaphoreType.DMA((5, 8)),
            pltpu.SemaphoreType.DMA((5, 8)),
            pltpu.SemaphoreType.DMA((4, 3)),
            pltpu.SemaphoreType.DMA((4, 3)),
            pltpu.SemaphoreType.DMA((13,)),
            pltpu.SMEM(water_use.shape[::-1], F32),
            pltpu.SMEM(district_use.shape, F32),
        ],
        compiler_params=pltpu.CompilerParams(
            collective_id=0, has_side_effects=True, vmem_limit_bytes=48 * 1024 * 1024
        ),
    )(
        *(
            pltpu.with_memory_space_constraint(value, pltpu.HBM)
            for value in (
                right_aquifer.reshape(block),
                right_district,
                head_scale,
                crop_scale,
                conductance,
                climate,
                district_id,
                active,
                water_use.T,
                district_use,
            )
        )
    )
    dual, dual_di, res, res_di = outs
    return dual.reshape(right_aquifer.shape), dual_di, res.reshape(right_aquifer.shape), res_di


def solution(mesh):
    placed = (
        P(None, None, "row", "col"),
        P(),
        P(None, "row", "col"),
        P(None, "row", "col"),
        P(None, "row", "col"),
        P(),
        P("row", "col"),
        P(),
        P("row", "col"),
        P("row", "col"),
    )
    return jax.shard_map(
        body,
        mesh=mesh,
        in_specs=placed,
        out_specs=(P(None, None, "row", "col"), P(), P(None, None, "row", "col"), P()),
        check_vma=False,
    )
```

```python
import functools

import jax
import jax.numpy as jnp
from jax import lax
from jax.experimental import pallas as pl
from jax.experimental.pallas import tpu as pltpu
from jax.sharding import PartitionSpec as P

ITERS = 4
RHS = 4
MONTHS = 12
CROPS = 6
FIELDS = RHS * MONTHS
DHI = 16
DLO = 256
LANES = 128
TILE_ROWS = 16
CHUNKS = 32
LINES = 22
ID_FIELD = 14
PROXIMAL = 0.05
SHIFTS = (0.5, 8.0, 3.0, 1.0)
PAIRS = tuple((i, j) for i in range(ITERS) for j in range(i, ITERS))
MESH = pl.DeviceIdType.MESH
F32 = jnp.float32
CORE = pl.ds(8, 16)


def lanes_of(shape):
    return lax.broadcasted_iota(jnp.int32, shape, len(shape) - 1)


def rows_of(shape):
    return lax.broadcasted_iota(jnp.int32, shape, len(shape) - 2)


def beside(tiles):
    axis = tiles[0].ndim - 1
    lane = lanes_of(tiles[0].shape)
    ahead = [pltpu.roll(t, LANES - 1, axis) for t in tiles]
    behind = [pltpu.roll(t, 1, axis) for t in tiles]
    east = [jnp.where(lane == LANES - 1, ahead[(n + 1) % 3], ahead[n]) for n in range(3)]
    west = [jnp.where(lane == 0, behind[(n + 2) % 3], behind[n]) for n in range(3)]
    return east, west


def kernel(
    grid_cells,
    rhs_hbm,
    rdi_hbm,
    head_hbm,
    crop_hbm,
    cond_hbm,
    climate_hbm,
    id_hbm,
    active_hbm,
    wu_hbm,
    use_hbm,
    dual_ref,
    dual_di_ref,
    res_ref,
    res_di_ref,
    basis,
    image,
    stat,
    coef,
    headw,
    coefc,
    diag,
    dinv,
    cross,
    wcs,
    inner,
    hot,
    lo_id,
    hi_id,
    cells,
    looks,
    wide_look,
    spread,
    rdi_ref,
    crop_ref,
    climate_ref,
    id_ref,
    active_ref,
    table,
    diag_di,
    wide,
    bdi,
    sum_in,
    sum_near,
    sum_z,
    sum_out,
    late_near,
    late_z,
    late_in,
    factors,
    row_out,
    row_in,
    col_out,
    col_in,
    xch_send,
    xch_recv,
    sum_send,
    sum_recv,
    load_sem,
    wu_ref,
    use_ref,
):
    rows, cols = lax.axis_size("row"), lax.axis_size("col")
    chips, group = rows // 2, 2 * cols
    per = CHUNKS // group
    row, col = lax.axis_index("row"), lax.axis_index("col")
    chip, core = row // 2, lax.rem(row, 2)
    mine = core * cols + col
    districts = rdi_ref.shape[1]

    def slot_at(slot):
        return slot * FIELDS + (MONTHS if slot else 0)


    def peer(k):
        other = lax.rem(mine + k, group)
        return other, (chip * 2 + other // cols, lax.rem(other, cols))

    def stack(k):
        return (lax.rem(row + 2 * k, rows), col)

    def around(dr, dc):
        return (lax.rem(row + dr + rows, rows), lax.rem(col + dc + cols, cols))

    loads = []
    for t in range(2):
        span = pl.ds(LANES * t, LANES)
        loads.append((cond_hbm.at[:, :, span], stat.at[pl.ds(0, 2), t, CORE]))
        loads.append((head_hbm.at[:, :, span], stat.at[pl.ds(2, MONTHS), t, CORE]))
    loads += [(id_hbm, id_ref), (climate_hbm, climate_ref), (active_hbm, active_ref)]
    loads += [(wu_hbm, wu_ref), (use_hbm, use_ref), (crop_hbm, crop_ref), (rdi_hbm, rdi_ref)]
    for t in range(2):
        loads.append((rhs_hbm.at[:, :, pl.ds(LANES * t, LANES)], basis.at[pl.ds(0, FIELDS), t, CORE]))
    loads = [pltpu.make_async_copy(src, dst, load_sem.at[k]) for k, (src, dst) in enumerate(loads)]
    for load in loads:
        load.start()

    barrier = pltpu.get_barrier_semaphore()

    def greet(k, carry):
        pl.semaphore_signal(barrier, inc=1, device_id=peer(k)[1], device_id_type=MESH)
        return carry

    def greet_stack(k, carry):
        pl.semaphore_signal(barrier, inc=1, device_id=stack(k), device_id_type=MESH)
        return carry

    lax.fori_loop(1, group, greet, 0)
    lax.fori_loop(1, chips, greet_stack, 0)
    offsets = [(dr, dc) for dr in (-1, 0, 1) for dc in (-1, 0, 1) if dr or dc]
    for dr, dc in offsets:
        pl.semaphore_signal(barrier, inc=1, device_id=around(dr, dc), device_id_type=MESH)

    north = jnp.where(row > 0, 1.0, 0.0).astype(F32)
    south = jnp.where(row < rows - 1, 1.0, 0.0).astype(F32)
    west = jnp.where(col > 0, 1.0, 0.0).astype(F32)
    east = jnp.where(col < cols - 1, 1.0, 0.0).astype(F32)

    def halo_copies(n, quads, groups):
        ahead, back = pl.ds(8, 8), pl.ds(0, 8)
        plan = [
            (row_out.at[n, 0, pl.ds(0, quads)], row_in.at[n, 0, pl.ds(0, quads)], (1, 0)),
            (row_out.at[n, 1, pl.ds(0, quads)], row_in.at[n, 1, pl.ds(0, quads)], (-1, 0)),
            (col_out.at[n, pl.ds(0, groups)], col_in.at[n, 0, pl.ds(0, groups), CORE], (0, 1)),
            (col_out.at[n, pl.ds(0, groups)], col_in.at[n, 1, pl.ds(0, groups), CORE], (0, -1)),
            (col_out.at[n, pl.ds(0, groups), ahead], col_in.at[n, 0, pl.ds(0, groups), pl.ds(0, 8)], (1, 1)),
            (col_out.at[n, pl.ds(0, groups), ahead], col_in.at[n, 1, pl.ds(0, groups), pl.ds(0, 8)], (1, -1)),
            (col_out.at[n, pl.ds(0, groups), back], col_in.at[n, 0, pl.ds(0, groups), pl.ds(24, 8)], (-1, 1)),
            (col_out.at[n, pl.ds(0, groups), back], col_in.at[n, 1, pl.ds(0, groups), pl.ds(24, 8)], (-1, -1)),
        ]
        return [
            pltpu.make_async_remote_copy(
                src_ref=src,
                dst_ref=dst,
                send_sem=xch_send.at[n, k],
                recv_sem=xch_recv.at[n, k],
                device_id=around(*to),
                device_id_type=MESH,
            )
            for k, (src, dst, to) in enumerate(plan)
        ]

    def halo_pack_cols(n, ref, base, quads):
        lane = lanes_of((TILE_ROWS, LANES))

        def cols_of(f, packed, slot):
            both = jnp.where(lane < 64, ref[base + f, 0, CORE], ref[base + f, 1, CORE])
            moved = pltpu.roll(both, lax.rem(4 * slot + 2, LANES), 1)
            return jnp.where(lane // 4 == slot, moved, packed)

        for g in range((quads + 7) // 8):
            count = min(32, 4 * quads - 32 * g)

            def quad(k, packed):
                for u in range(4):
                    packed = cols_of(32 * g + 4 * k + u, packed, 4 * k + u)
                return packed

            col_out[n, g] = lax.fori_loop(0, count // 4, quad, jnp.zeros((TILE_ROWS, LANES), F32), unroll=count // 4)

    def halo_pack_rows(n, ref, base, quads):
        def rows_quad(k, carry):
            for u in range(4):
                field = ref.at[base + 4 * k + u]
                for t in range(2):
                    row_out[n, 0, k, t, pl.ds(2 * u, 2)] = field[t, pl.ds(22, 2)]
                    row_out[n, 1, k, t, pl.ds(2 * u, 2)] = field[t, pl.ds(8, 2)]
            return carry

        lax.fori_loop(0, quads, rows_quad, 0, unroll=quads // 4 if quads % 4 == 0 else 5)

    def send_cols(n, ref, base, quads):
        copies = halo_copies(n, quads, (quads + 7) // 8)
        halo_pack_cols(n, ref, base, quads)
        for copy in copies[2:]:
            copy.start()
        return copies

    def send_rows(copies, n, ref, base, quads):
        halo_pack_rows(n, ref, base, quads)
        for copy in copies[:2]:
            copy.start()

    def halo_send(n, ref, base, quads):
        copies = send_cols(n, ref, base, quads)
        send_rows(copies, n, ref, base, quads)
        return copies

    def halo_cols(copies, n, ref, base, quads):
        for copy in copies[2:]:
            copy.wait_recv()
        shape = (32, LANES)
        lane, place = lanes_of(shape), rows_of(shape)
        side = jnp.where(lax.rem(lane, 4) < 2, west, east)
        side = side * jnp.where(place < 8, north, jnp.where(place >= 24, south, 1.0))
        for g in range((quads + 7) // 8):
            count = min(32, 4 * quads - 32 * g)
            packed = jnp.where(lax.rem(lane, 4) < 2, col_in[n, 0, g], col_in[n, 1, g]) * side

            def quad(k, carry):
                for u in range(4):
                    slot = 4 * k + u
                    moved = pltpu.roll(packed, lax.rem(2 * LANES - 4 * slot - 2, LANES), 1)
                    ref[base + 32 * g + slot, 2] = moved
                return carry

            lax.fori_loop(0, count // 4, quad, 0, unroll=count // 4)

    def halo_rows(copies, n, ref, base, quads):
        for copy in copies[:2]:
            copy.wait_recv()

        def rows_quad(k, carry):
            for u in range(4):
                for t in range(2):
                    ref[base + 4 * k + u, t, pl.ds(6, 2)] = row_in[n, 0, k, t, pl.ds(2 * u, 2)] * north
                    ref[base + 4 * k + u, t, pl.ds(24, 2)] = row_in[n, 1, k, t, pl.ds(2 * u, 2)] * south
            return carry

        lax.fori_loop(0, quads, rows_quad, 0, unroll=quads // 4 if quads % 4 == 0 else 5)

    def bytes_of(ref, sem):
        pltpu.make_async_copy(ref, ref, sem).wait()

    def sum_scatter(n):
        def scatter(k, carry):
            other, device = peer(k)
            pltpu.make_async_remote_copy(
                src_ref=sum_in.at[n, other],
                dst_ref=sum_near.at[n, k],
                send_sem=sum_send.at[n, 0],
                recv_sem=sum_recv.at[n, 0],
                device_id=device,
                device_id_type=MESH,
            ).start()
            return carry

        lax.fori_loop(1, group, scatter, 0)
        sum_near[n, 0] = sum_in[n, mine]

    def sum_spread(n):
        bytes_of(sum_near.at[n, pl.ds(1, group - 1)], sum_recv.at[n, 0])
        sum_z[n, chip] = jnp.sum(sum_near[n], axis=0)

        def spread(k, carry):
            pltpu.make_async_remote_copy(
                src_ref=sum_z.at[n, chip],
                dst_ref=sum_z.at[n, chip],
                send_sem=sum_send.at[n, 1],
                recv_sem=sum_recv.at[n, 1],
                device_id=stack(k),
                device_id_type=MESH,
            ).start()
            return carry

        lax.fori_loop(1, chips, spread, 0)

    def sum_gather(n):
        bytes_of(sum_z.at[n, pl.ds(1, chips - 1)], sum_recv.at[n, 1])
        sum_out[n, mine] = jnp.sum(sum_z[n], axis=0)

        def gather(k, carry):
            pltpu.make_async_remote_copy(
                src_ref=sum_out.at[n, mine],
                dst_ref=sum_out.at[n, mine],
                send_sem=sum_send.at[n, 2],
                recv_sem=sum_recv.at[n, 2],
                device_id=peer(k)[1],
                device_id_type=MESH,
            ).start()
            return carry

        lax.fori_loop(1, group, gather, 0)

    def sum_done(n):
        bytes_of(sum_near.at[n, pl.ds(1, group - 1)], sum_recv.at[n, 2])

    def sum_drain(n):
        bytes_of(sum_near.at[n, pl.ds(1, group - 1)], sum_send.at[n, 0])
        bytes_of(sum_z.at[n, pl.ds(1, chips - 1)], sum_send.at[n, 1])
        bytes_of(sum_near.at[n, pl.ds(1, group - 1)], sum_send.at[n, 2])

    def chunk(k):
        return k // per, pl.ds(8 * (k % per), 8)

    def line_span(i):
        return pl.ds(pl.multiple_of(i * (2 * LANES), 2 * LANES), 2 * LANES)

    def to_district(n, count, first):
        size = count * DHI

        def line(i, carry):
            value = cells[pl.ds(0, count), pl.ds(i, 1), :]
            high = value.astype(jnp.bfloat16).astype(F32)
            here = (hi_id[pl.ds(i, 1), :] == rows_of((DHI, 2 * LANES)))[None]
            for k, part in enumerate((high, value - high)):
                part = jnp.where(here, jnp.broadcast_to(part, (count, DHI, 2 * LANES)), 0.0)
                spread[pl.ds(k * size, size), line_span(i)] = part.reshape(size, 2 * LANES).astype(jnp.bfloat16)
            return carry

        lax.fori_loop(0, TILE_ROWS, line, 0, unroll=2)
        total = lax.dot_general(
            hot[:, pl.ds(0, TILE_ROWS * 2 * LANES)], spread[pl.ds(0, 2 * size), :], (((1,), (1,)), ((), ())), preferred_element_type=F32
        ).T
        total = total[:size] + total[size:]
        for b in range(count):
            for t in range(2):
                for h in range(2):
                    at, part = chunk(4 * (first + b) + 2 * t + h)
                    sum_in[n, at, part] = total[DHI * b + 8 * h : DHI * b + 8 * h + 8, LANES * t : LANES * (t + 1)]

    def from_district(slot, count, first, lines=TILE_ROWS):
        size = count * RHS * DHI
        values = jnp.concatenate(
            [
                jnp.concatenate([table[slot + s, r, t] for t in range(2)], axis=1)
                for s in range(count)
                for r in range(RHS)
            ],
            axis=0,
        )
        high = values.astype(jnp.bfloat16).astype(F32)
        both = jnp.concatenate([high, values - high], axis=0).astype(jnp.bfloat16)

        def two(k, carry):
            span = pl.ds(pl.multiple_of(k * (4 * LANES), 4 * LANES), 4 * LANES)
            picked = jnp.dot(both, hot[:, span], preferred_element_type=F32)
            picked = (picked[:size] + picked[size:]).reshape(count * RHS, DHI, 4 * LANES)
            for u in range(2):
                here = (hi_id[pl.ds(2 * k + u, 1), :] == rows_of((DHI, 2 * LANES)))[None]
                part = jnp.where(here, picked[:, :, 2 * LANES * u : 2 * LANES * (u + 1)], 0.0)
                looks[pl.ds(first, count * RHS), pl.ds(2 * k + u, 1), :] = jnp.sum(part, axis=1, keepdims=True)
            return carry

        lax.fori_loop(0, lines // 2, two, 0, unroll=lines // 2 if count == 1 else 1)

    def cells_of(load, first):
        def one(r, carry):
            for t in range(2):
                total = jnp.zeros((TILE_ROWS, LANES), F32)
                for m in range(MONTHS):
                    total += cross[m, t] * load(r * MONTHS + m, t)
                cells[first + r, :, pl.ds(LANES * t, LANES)] = total
            return carry

        lax.fori_loop(0, RHS, one, 0)

    def core_of(slot):
        return lambda f, t: basis[slot_at(slot) + f, t, CORE]

    def smooth(slot, put):
        def one(r, carry):
            base = slot_at(slot) + r * MONTHS
            for k in range(3):
                part, place = pl.ds(8 * k, 8), pl.ds(4 + 8 * k, 8)
                face = [[coef[j, t, part] for t in range(3)] for j in range(5)]
                for m in range(MONTHS):
                    here = [basis[base + m, t, place] for t in range(3)]
                    e, w = beside(here)
                    for t in range(3):
                        lap = face[4][t] * here[t] - face[0][t] * e[t] - face[1][t] * w[t]
                        lap = lap - face[2][t] * basis[base + m, t, pl.ds(5 + 8 * k, 8)]
                        lap = lap - face[3][t] * basis[base + m, t, pl.ds(3 + 8 * k, 8)]
                        inner[m, t, part] = headw[m, t, part] * lap
            for k in range(2):
                part, place = pl.ds(8 * k, 8), pl.ds(8 + 8 * k, 8)
                draws = [[jnp.zeros((8, LANES), F32)] * CROPS for _ in range(2)]
                for m in range(MONTHS):
                    value = [basis[base + m, t, place] for t in range(2)]
                    for c in range(CROPS):
                        for t in range(2):
                            draws[t][c] = draws[t][c] + wu_ref[c, m] * value[t]
                draws = [[wcs[c, t, part] * draws[t][c] for c in range(CROPS)] for t in range(2)]
                face = [[coefc[j, t, part] for t in range(2)] for j in range(5)]
                for m in range(MONTHS):
                    here = [inner[m, t, pl.ds(4 + 8 * k, 8)] for t in range(3)]
                    e, w = beside(here)
                    for t in range(2):
                        own = basis[base + m, t, place]
                        lap = face[4][t] * here[t] - face[0][t] * e[t] - face[1][t] * w[t]
                        lap = lap - face[2][t] * inner[m, t, pl.ds(5 + 8 * k, 8)]
                        lap = lap - face[3][t] * inner[m, t, pl.ds(3 + 8 * k, 8)]
                        total = lap + PROXIMAL * own
                        for c in range(CROPS):
                            total = total + wu_ref[c, m] * draws[t][c]
                        put(r, m, t, k, dinv[m, t, part] * total, own)
            return carry

        lax.fori_loop(0, RHS, one, 0)

    def to_image(r, m, t, k, value, own):
        image[r * MONTHS + m, t, pl.ds(8 * k, 8)] = value

    def to_second(r, m, t, k, value, own):
        basis[slot_at(1) + r * MONTHS + m, t, pl.ds(8 + 8 * k, 8)] = value

    def to_next(slot, look, shift):
        def put(r, m, t, k, value, own):
            place = pl.ds(8 + 8 * k, 8)
            seen = looks[look + r, pl.ds(8 * k, 8), pl.ds(LANES * t, LANES)]
            value = value + basis[FIELDS + m, t, place] * seen - shift * own
            basis[slot_at(slot + 1) + r * MONTHS + m, t, place] = value

        return put

    def advance_wide(shift):
        window = pl.ds(4, 24)

        def one(r, carry):
            for t in range(3):
                seen = wide_look[r, t, window]
                for m in range(MONTHS):
                    f = r * MONTHS + m
                    basis[slot_at(1) + f, t, window] = (
                        basis[slot_at(1) + f, t, window]
                        + basis[FIELDS + m, t, window] * seen
                        - shift * basis[f, t, window]
                    )
            return carry

        lax.fori_loop(0, RHS, one, 0)

    def repeat(packed):
        for width in (4, 8, 16, 32, 64):
            packed = packed + pltpu.roll(packed, width, 1)
        return packed

    def fill_wide_look():
        shape = (24, LANES)
        own = lanes_of(shape) // 4 == rows_of(shape)
        for r in range(RHS):
            for t in range(2):
                span = pl.ds(LANES * t, LANES)
                wide_look[r, t, CORE] = looks[r, pl.ds(0, TILE_ROWS), span]
                wide_look[r, t, pl.ds(6, 2)] = looks[r, pl.ds(16, 2), span]
                wide_look[r, t, pl.ds(24, 2)] = looks[r, pl.ds(18, 2), span]
            edge = repeat(jnp.where(own, looks[r, pl.ds(20, 1), pl.ds(0, LANES)], 0.0))
            wide_look[r, 2, pl.ds(4, 24)] = pltpu.roll(edge, LANES - 2, 1)

    def wide_ids():
        shape = (24, LANES)
        edge = pltpu.roll(stat[ID_FIELD, 2, pl.ds(4, 24)], 2, 1)
        edge = repeat(jnp.where(lanes_of(shape) < 4, edge, 0.0))
        edge = jnp.sum(jnp.where(lanes_of(shape) // 4 == rows_of(shape), edge, 0.0), axis=0, keepdims=True)
        lines = [jnp.concatenate([stat[ID_FIELD, t, pl.ds(i, 1)] for t in range(2)], axis=1) for i in (6, 7, 24, 25)]
        lines.append(jnp.concatenate([edge, edge], axis=1))
        for k, one in enumerate(lines):
            ids = one.astype(jnp.int32)
            hi_id[pl.ds(16 + k, 1), :] = ids // DLO
            lo_id[pl.ds(16 + k, 1), :] = lax.rem(ids, DLO)
        lax.fori_loop(TILE_ROWS, LINES - 1, hot_line, 0)

    for t in range(2):
        stat[15, t, CORE] = jnp.zeros((TILE_ROWS, LANES), F32)
    sum_in[...] = jnp.zeros_like(sum_in)
    for load in loads[:5]:
        load.wait()
    for t in range(2):
        stat[ID_FIELD, t, CORE] = id_ref[:, pl.ds(LANES * t, LANES)].astype(F32)
    halo_pack_cols(0, stat, 0, 4)
    halo_pack_rows(0, stat, 0, 4)
    for load in loads[5:]:
        load.wait()
    scale = (districts / grid_cells) ** 0.5
    ids = id_ref[...]
    hi_id[pl.ds(0, TILE_ROWS), :] = ids // DLO
    lo_id[pl.ds(0, TILE_ROWS), :] = lax.rem(ids, DLO)

    def hot_line(i, carry):
        same = lo_id[pl.ds(i, 1), :] == rows_of((DLO, 2 * LANES))
        hot[:, line_span(i)] = jnp.where(same, 1.0, 0.0).astype(jnp.bfloat16)
        return carry

    lax.fori_loop(0, TILE_ROWS, hot_line, 0)
    for t in range(2):
        span = pl.ds(LANES * t, LANES)
        live = active_ref[:, span].astype(F32)
        weight = live * climate_ref[:, span]
        crops = [crop_ref[c, :, span] for c in range(CROPS)]
        own = jnp.zeros((TILE_ROWS, LANES), F32)
        for c in range(CROPS):
            use = scale * use_ref[c] * live
            own = own + use * use * crops[c]
            wcs[c, t] = weight * weight * crops[c]
        cells[0, :, span] = own
        for m in range(MONTHS):
            square = jnp.zeros((TILE_ROWS, LANES), F32)
            mixed = jnp.zeros((TILE_ROWS, LANES), F32)
            for c in range(CROPS):
                drawn = wu_ref[c, m] * crops[c]
                square = square + wu_ref[c, m] * drawn
                mixed = mixed + use_ref[c] * drawn
            diag[m, t] = weight * weight * square + PROXIMAL
            cross[m, t] = weight * live * (scale * mixed)
    for r in range(RHS):
        for t in range(2):
            bdi[r, t] = jnp.zeros((DHI, LANES), F32)
            for hi in range(districts // DLO):
                at = LANES * (2 * hi + t)
                bdi[r, t, pl.ds(hi, 1)] = rdi_ref[pl.ds(r, 1), pl.ds(at, LANES)]

    pl.semaphore_wait(barrier, group + chips - 2 + len(offsets))
    halo_stat = halo_copies(0, 4, 1)
    for copy in halo_stat:
        copy.start()

    halo_rows(halo_stat, 0, stat, 0, 4)
    halo_cols(halo_stat, 0, stat, 0, 4)
    window = pl.ds(4, 24)
    faces = [[stat[k, t, window] for t in range(3)] for k in range(2)]
    east_side, west_side = beside(faces[0])
    for t in range(3):
        south_north = stat[1, t, pl.ds(3, 24)]
        coef[0, t] = faces[0][t]
        coef[1, t] = west_side[t]
        coef[2, t] = faces[1][t]
        coef[3, t] = south_north
        coef[4, t] = faces[0][t] + west_side[t] + faces[1][t] + south_north
    for k in range(5):
        for t in range(2):
            coefc[k, t] = coef[k, t, pl.ds(4, 16)]

    def month_diag(m, carry):
        for t in range(3):
            headw[m, t] = stat[2 + m, t, window]
        here = [stat[2 + m, t, CORE] for t in range(3)]
        e, w = beside(here)
        for t in range(2):
            fe, fw, fs, fn, total = [coefc[k, t] for k in range(5)]
            value = diag[m, t] + here[t] * total * total + fe * fe * e[t] + fw * fw * w[t]
            value = value + fs * fs * stat[2 + m, t, pl.ds(9, 16)] + fn * fn * stat[2 + m, t, pl.ds(7, 16)]
            diag[m, t] = value
            inverse = 1.0 / value
            dinv[m, t] = inverse
            basis[FIELDS + m, t, CORE] = cross[m, t] * inverse
        return carry

    lax.fori_loop(0, MONTHS, month_diag, 0, unroll=4)

    def start_basis(r, carry):
        for t in range(2):
            for m in range(MONTHS):
                f = r * MONTHS + m
                basis[f, t, CORE] = basis[f, t, CORE] * dinv[m, t]
        return carry

    lax.fori_loop(0, RHS, start_basis, 0)

    both = (FIELDS + MONTHS) // 4
    halo_first = halo_send(1, basis, 0, both)
    for t in range(2):
        total = jnp.zeros((TILE_ROWS, LANES), F32)
        for m in range(MONTHS):
            total += cross[m, t] * basis[FIELDS + m, t, CORE]
        cells[1, :, pl.ds(LANES * t, LANES)] = total
    cells_of(core_of(0), 2)
    to_district(0, 2 + RHS, 0)
    sum_scatter(0)

    wide_ids()
    sum_spread(0)
    halo_rows(halo_first, 1, basis, 0, both)
    halo_cols(halo_first, 1, basis, 0, both)
    smooth(0, to_second)
    halo_second = halo_send(2, basis, slot_at(1), FIELDS // 4)
    sum_gather(0)
    cells_of(core_of(1), 0)
    to_district(1, RHS, 0)
    sum_scatter(1)
    halo_rows(halo_second, 2, basis, slot_at(1), FIELDS // 4)
    sum_done(0)

    def total_of(n, b):
        parts = [sum_out[(n,) + chunk(4 * b + k)] for k in range(4)]
        return jnp.stack([jnp.concatenate(parts[:2], axis=0), jnp.concatenate(parts[2:], axis=0)])

    diag_di[...] = total_of(0, 0) + PROXIMAL
    wide[...] = total_of(0, 1)
    for r in range(RHS):
        t0 = bdi[r] / diag_di[...]
        table[0, r] = t0
        table[1, r] = total_of(0, 2 + r) / diag_di[...] + (1 - SHIFTS[0]) * t0
    from_district(0, 2, 0, LINES)
    fill_wide_look()
    halo_cols(halo_second, 2, basis, slot_at(1), FIELDS // 4)
    sum_spread(1)
    advance_wide(SHIFTS[0])
    smooth(1, to_next(1, RHS, SHIFTS[1]))
    halo_third = halo_send(3, basis, slot_at(2), FIELDS // 4)
    sum_gather(1)
    cells_of(core_of(2), 0)
    to_district(2, RHS, 0)
    halo_rows(halo_third, 3, basis, slot_at(2), FIELDS // 4)
    sum_done(1)
    for r in range(RHS):
        z1 = total_of(1, r) + wide[...] * table[0, r] - SHIFTS[0] * total_of(0, 2 + r)
        table[2, r] = z1 / diag_di[...] + (1 - SHIFTS[1]) * table[1, r]
    from_district(2, 1, 0)
    halo_cols(halo_third, 3, basis, slot_at(2), FIELDS // 4)
    smooth(2, to_next(2, 0, SHIFTS[2]))
    halo_fourth = send_cols(4, basis, slot_at(3), FIELDS // 4)
    cells_of(core_of(3), 0)
    to_district(2, RHS, RHS)
    sum_scatter(2)
    send_rows(halo_fourth, 4, basis, slot_at(3), FIELDS // 4)

    shape = (8, LANES)

    def inner_products(r, packed):
        totals = [jnp.zeros(shape, F32) for _ in PAIRS]
        for m in range(MONTHS):
            for t in range(2):
                values = [basis[slot_at(s) + r * MONTHS + m, t, CORE] for s in range(ITERS)]
                scaled = [diag[m, t] * v for v in values]
                for n, (i, j) in enumerate(PAIRS):
                    term = scaled[i] * values[j]
                    totals[n] = totals[n] + (term[:8] + term[8:])
        for n, total in enumerate(totals):
            here = (rows_of(shape) == r) & (lanes_of(shape) == n)
            packed = jnp.where(here, jnp.sum(total, keepdims=True), packed)
        return packed

    packed = lax.fori_loop(0, RHS, inner_products, jnp.zeros(shape, F32))
    sum_spread(2)
    halo_rows(halo_fourth, 4, basis, slot_at(3), FIELDS // 4)
    halo_cols(halo_fourth, 4, basis, slot_at(3), FIELDS // 4)

    def top_product(r, packed):
        total = jnp.zeros(shape, F32)
        base = slot_at(3) + r * MONTHS
        draws = [[jnp.zeros((TILE_ROWS, LANES), F32)] * CROPS for _ in range(2)]
        for m in range(MONTHS):
            here = [basis[base + m, t, CORE] for t in range(3)]
            e, w = beside(here)
            for t in range(2):
                lap = coefc[4, t] * here[t] - coefc[0, t] * e[t] - coefc[1, t] * w[t]
                lap = lap - coefc[2, t] * basis[base + m, t, pl.ds(9, 16)]
                lap = lap - coefc[3, t] * basis[base + m, t, pl.ds(7, 16)]
                term = stat[2 + m, t, CORE] * lap * lap + PROXIMAL * here[t] * here[t]
                total = total + (term[:8] + term[8:])
                draws[t] = [draws[t][c] + wu_ref[c, m] * here[t] for c in range(CROPS)]
        for t in range(2):
            for c in range(CROPS):
                term = wcs[c, t] * draws[t][c] * draws[t][c]
                total = total + (term[:8] + term[8:])
        here = (rows_of(shape) == r) & (lanes_of(shape) == len(PAIRS))
        return jnp.where(here, jnp.sum(total, keepdims=True), packed)

    late_in[...] = lax.fori_loop(0, RHS, top_product, packed, unroll=2)

    def late_first(k, carry):
        pltpu.make_async_remote_copy(
            src_ref=late_in,
            dst_ref=late_near.at[mine],
            send_sem=sum_send.at[3, 0],
            recv_sem=sum_recv.at[3, 0],
            device_id=peer(k)[1],
            device_id_type=MESH,
        ).start()
        return carry

    lax.fori_loop(1, group, late_first, 0)
    late_near[mine] = late_in[...]
    smooth(3, to_image)
    sum_gather(2)
    bytes_of(late_near.at[pl.ds(1, group - 1)], sum_recv.at[3, 0])
    late_z[chip] = jnp.sum(late_near[...], axis=0)

    def late_second(k, carry):
        pltpu.make_async_remote_copy(
            src_ref=late_z.at[chip],
            dst_ref=late_z.at[chip],
            send_sem=sum_send.at[3, 1],
            recv_sem=sum_recv.at[3, 1],
            device_id=stack(k),
            device_id_type=MESH,
        ).start()
        return carry

    lax.fori_loop(1, chips, late_second, 0)
    def district_part(i, j):
        out = jnp.zeros(shape, F32)
        for r in range(RHS):
            if j < ITERS:
                term = diag_di[...] * table[i, r] * table[j, r]
            else:
                term = table[3, r] * (2 * total_of(2, RHS + r) + diag_di[...] * table[3, r])
            line = jnp.sum(jnp.sum(term, axis=0), axis=0, keepdims=True)
            out = jnp.where(rows_of(shape) == r, line, out)
        return out

    early = {pair: district_part(*pair) for pair in PAIRS if pair[1] < 3}
    sum_done(2)
    for r in range(RHS):
        table[3, r] = total_of(2, r) / diag_di[...] + (1 - SHIFTS[2]) * table[2, r]
        table[4, r] = total_of(2, RHS + r) / diag_di[...] + (1 - SHIFTS[3]) * table[3, r]
    from_district(3, 1, 0)

    parts = [early[pair] if pair in early else district_part(*pair) for pair in PAIRS + ((3, ITERS),)]
    bytes_of(late_z.at[pl.ds(1, chips - 1)], sum_recv.at[3, 1])
    totals = jnp.sum(late_z[...], axis=0)
    gram = [[None] * (ITERS + 1) for _ in range(ITERS + 1)]
    values = []
    for n, part in enumerate(parts):
        both = part + jnp.where(lanes_of(shape) == n, totals, 0.0)
        values.append(jnp.broadcast_to(jnp.sum(both, axis=1, keepdims=True), shape))
    for n, (i, j) in enumerate(PAIRS):
        gram[i][j] = gram[j][i] = values[n]
    for i in range(ITERS):
        ahead = values[-1] if i == ITERS - 1 else gram[i + 1][ITERS - 1] + SHIFTS[i] * gram[i][ITERS - 1]
        gram[i][ITERS] = ahead - SHIFTS[ITERS - 1] * gram[i][ITERS - 1]

    one, zero = jnp.ones(shape, F32), jnp.zeros(shape, F32)
    x, res, dirn = [zero] * ITERS, [one] + [zero] * ITERS, [one] + [zero] * (ITERS - 1)
    rho = gram[0][0]
    for it in range(ITERS):
        moved = [zero] * (ITERS + 1)
        for k in range(it + 1):
            moved[k + 1] = moved[k + 1] + dirn[k]
            moved[k] = moved[k] + SHIFTS[k] * dirn[k]
        curve = zero
        for i in range(it + 1):
            line = zero
            for j in range(it + 2):
                line = line + moved[j] * gram[i][j]
            curve = curve + dirn[i] * line
        alpha = rho / curve
        x = [x[i] + alpha * dirn[i] for i in range(ITERS)]
        res = [res[i] - alpha * moved[i] for i in range(ITERS + 1)]
        if it + 1 < ITERS:
            rho_new = zero
            for i in range(it + 2):
                line = zero
                for j in range(it + 2):
                    line = line + res[j] * gram[i][j]
                rho_new = rho_new + res[i] * line
            ratio = rho_new / rho
            rho = rho_new
            dirn = [res[i] + ratio * dirn[i] for i in range(ITERS)]
    for k, value in enumerate(x + res):
        factors[k] = value

    def finish(r, carry):
        xs = [factors[k, pl.ds(r, 1)] for k in range(ITERS)]
        rs = [factors[ITERS + k, pl.ds(r, 1)] for k in range(ITERS + 1)]
        for t in range(2):
            span = pl.ds(LANES * t, LANES)
            seen = looks[r, pl.ds(0, TILE_ROWS), span]
            for m in range(MONTHS):
                f = r * MONTHS + m
                vs = [basis[slot_at(s) + f, t, CORE] for s in range(ITERS)]
                vs.append(image[f, t] + basis[FIELDS + m, t, CORE] * seen - SHIFTS[3] * vs[3])
                dual_ref[f, :, span] = xs[0] * vs[0] + xs[1] * vs[1] + xs[2] * vs[2] + xs[3] * vs[3]
                total = rs[0] * vs[0]
                for k in range(1, ITERS + 1):
                    total = total + rs[k] * vs[k]
                res_ref[f, :, span] = diag[m, t] * total
        return carry

    lax.fori_loop(0, RHS, finish, 0)
    for r in range(RHS):
        xs = [factors[k, pl.ds(r, 1)] for k in range(ITERS)]
        rs = [factors[ITERS + k, pl.ds(r, 1)] for k in range(ITERS + 1)]
        for t in range(2):
            dual = xs[0] * table[0, r, t]
            total = rs[0] * table[0, r, t]
            for k in range(1, ITERS):
                dual = dual + xs[k] * table[k, r, t]
            for k in range(1, ITERS + 1):
                total = total + rs[k] * table[k, r, t]
            total = total * diag_di[t]
            for hi in range(districts // DLO):
                span = pl.ds(LANES * (2 * hi + t), LANES)
                dual_di_ref[pl.ds(r, 1), span] = dual[hi : hi + 1]
                res_di_ref[pl.ds(r, 1), span] = total[hi : hi + 1]

    for copies in (halo_stat, halo_first, halo_second, halo_third, halo_fourth):
        for copy in copies:
            copy.wait_send()
    for n in range(3):
        sum_drain(n)
    bytes_of(late_near.at[pl.ds(1, group - 1)], sum_send.at[3, 0])
    bytes_of(late_z.at[pl.ds(1, chips - 1)], sum_send.at[3, 1])


def body(
    right_aquifer,
    right_district,
    head_scale,
    crop_scale,
    conductance,
    water_use,
    climate,
    district_use,
    district_id,
    active,
):
    rows, cols = lax.axis_size("row"), lax.axis_size("col")
    group, chips = 2 * cols, rows // 2
    per = CHUNKS // group
    tile_rows, tile_cols = climate.shape
    grid_cells = tile_rows * rows * tile_cols * cols
    whole = pl.BlockSpec(memory_space=pltpu.VMEM)
    block = (FIELDS, tile_rows, tile_cols)
    vmem = lambda *shape: pltpu.VMEM(shape, F32)
    core = (2, TILE_ROWS, LANES)
    outs = pl.pallas_call(
        functools.partial(kernel, grid_cells),
        out_shape=(
            jax.ShapeDtypeStruct(block, F32),
            jax.ShapeDtypeStruct(right_district.shape, F32),
            jax.ShapeDtypeStruct(block, F32),
            jax.ShapeDtypeStruct(right_district.shape, F32),
        ),
        in_specs=[pl.BlockSpec(memory_space=pltpu.HBM)] * 10,
        out_specs=(whole,) * 4,
        scratch_shapes=[
            vmem(ITERS * FIELDS + MONTHS, 3, 32, LANES),
            vmem(FIELDS, *core),
            vmem(16, 3, 32, LANES),
            vmem(5, 3, 24, LANES),
            vmem(MONTHS, 3, 24, LANES),
            vmem(5, *core),
            vmem(MONTHS, *core),
            vmem(MONTHS, *core),
            vmem(MONTHS, *core),
            vmem(CROPS, *core),
            vmem(MONTHS, 3, 24, LANES),
            pltpu.VMEM((DLO, LINES * 2 * LANES), jnp.bfloat16),
            pltpu.VMEM((24, 2 * LANES), jnp.int32),
            pltpu.VMEM((24, 2 * LANES), jnp.int32),
            vmem(2 + RHS, TILE_ROWS, 2 * LANES),
            vmem(2 * RHS, 24, 2 * LANES),
            vmem(RHS, 3, 32, LANES),
            pltpu.VMEM((2 * (2 + RHS) * DHI, TILE_ROWS * 2 * LANES), jnp.bfloat16),
            vmem(*right_district.shape),
            vmem(*crop_scale.shape),
            vmem(*climate.shape),
            pltpu.VMEM(district_id.shape, jnp.int32),
            pltpu.VMEM(active.shape, jnp.int32),
            vmem(ITERS + 1, RHS, 2, DHI, LANES),
            vmem(2, DHI, LANES),
            vmem(2, DHI, LANES),
            vmem(RHS, 2, DHI, LANES),
            vmem(3, group, 8 * per, LANES),
            vmem(3, group, 8 * per, LANES),
            vmem(3, chips, 8 * per, LANES),
            vmem(3, group, 8 * per, LANES),
            vmem(group, 8, LANES),
            vmem(chips, 8, LANES),
            vmem(8, LANES),
            vmem(2 * ITERS + 1, 8, LANES),
            vmem(5, 2, 15, 2, 8, LANES),
            vmem(5, 2, 15, 2, 8, LANES),
            vmem(5, 2, TILE_ROWS, LANES),
            vmem(5, 2, 2, 32, LANES),
            pltpu.SemaphoreType.DMA((5, 8)),
            pltpu.SemaphoreType.DMA((5, 8)),
            pltpu.SemaphoreType.DMA((4, 3)),
            pltpu.SemaphoreType.DMA((4, 3)),
            pltpu.SemaphoreType.DMA((13,)),
            pltpu.SMEM(water_use.shape[::-1], F32),
            pltpu.SMEM(district_use.shape, F32),
        ],
        compiler_params=pltpu.CompilerParams(
            collective_id=0, has_side_effects=True, vmem_limit_bytes=48 * 1024 * 1024
        ),
    )(
        *(
            pltpu.with_memory_space_constraint(value, pltpu.HBM)
            for value in (
                right_aquifer.reshape(block),
                right_district,
                head_scale,
                crop_scale,
                conductance,
                climate,
                district_id,
                active,
                water_use.T,
                district_use,
            )
        )
    )
    dual, dual_di, res, res_di = outs
    return dual.reshape(right_aquifer.shape), dual_di, res.reshape(right_aquifer.shape), res_di


def solution(mesh):
    placed = (
        P(None, None, "row", "col"),
        P(),
        P(None, "row", "col"),
        P(None, "row", "col"),
        P(None, "row", "col"),
        P(),
        P("row", "col"),
        P(),
        P("row", "col"),
        P("row", "col"),
    )
    return jax.shard_map(
        body,
        mesh=mesh,
        in_specs=placed,
        out_specs=(P(None, None, "row", "col"), P(), P(None, None, "row", "col"), P()),
        check_vma=False,
    )
```
